32 devices in a mesh: batch: 4 (over y, core), seq: 8 (over z, x).
Axes of the slice: x: 2, y: 2, z: 4, core: 2. Of those that a mesh axis runs over, the one named last changes fastest.
Arguments:
- tokens: bfloat16 [20, 2048, 960], P('batch', 'seq'), may hold values from -6 to 6
- doc_starts: int32 [20, 2048], P('batch'), may hold values from 0 to 1, as said below
- pregain: bfloat16 [960], replicated, may hold values from 0.5 to 1.5
- query_base: bfloat16 [960, 960], replicated, may hold values from -0.1875 to 0.1875
- key_base: bfloat16 [960, 320], replicated, may hold values from -0.1875 to 0.1875
- value_base: bfloat16 [960, 320], replicated, may hold values from -0.1875 to 0.1875
- output_base: bfloat16 [960, 960], replicated, may hold values from -1.5 to 1.5
- query_down: bfloat16 [960, 8], replicated, may hold values from -0.1875 to 0.1875
- query_up: bfloat16 [8, 960], replicated, may hold values from -0.59765625 to 0.59765625
- key_down: bfloat16 [960, 8], replicated, may hold values from -0.1875 to 0.1875
- key_up: bfloat16 [8, 320], replicated, may hold values from -0.59765625 to 0.59765625
- value_down: bfloat16 [960, 8], replicated, may hold values from -0.1875 to 0.1875
- value_up: bfloat16 [8, 320], replicated, may hold values from -0.59765625 to 0.59765625
- out_down: bfloat16 [960, 8], replicated, may hold values from -1.5 to 1.5
- out_up: bfloat16 [8, 960], replicated, may hold values from -0.59765625 to 0.59765625
- query_map: bfloat16 [15, 64, 64], replicated, may hold values from -0.75 to 0.75
- key_map: bfloat16 [5, 64, 64], replicated, may hold values from -0.75 to 0.75
- postgain: bfloat16 [960], replicated, may hold values from 0.5 to 1.5
- gate_proj: bfloat16 [960, 2560], replicated, may hold values from -0.1875 to 0.1875
- up_proj: bfloat16 [960, 2560], replicated, may hold values from -0.1875 to 0.1875
- down_proj: bfloat16 [2560, 960], replicated, may hold values from -0.125 to 0.125
- cotangent: bfloat16 [20, 2048, 960], P('batch', 'seq'), may hold values from -6 to 6
Outputs:
- layer_out: bfloat16 [20, 2048, 960], P('batch', 'seq')
- grad_tokens: float32 [20, 2048, 960], P('batch', 'seq')
- grad_pregain: float32 [960], replicated
- grad_querydown: float32 [960, 8], replicated
- grad_queryup: float32 [8, 960], replicated
- grad_keydown: float32 [960, 8], replicated
- grad_keyup: float32 [8, 320], replicated
- grad_valuedown: float32 [960, 8], replicated
- grad_valueup: float32 [8, 320], replicated
- grad_outdown: float32 [960, 8], replicated
- grad_outup: float32 [8, 960], replicated
- grad_querymap: float32 [15, 64, 64], replicated
- grad_keymap: float32 [5, 64, 64], replicated
- grad_postgain: float32 [960], replicated
- grad_gateproj: float32 [960, 2560], replicated
- grad_upproj: float32 [960, 2560], replicated
- grad_downproj: float32 [2560, 960], replicated
The draws below stay inside these ranges and needn't reach their ends.
Inputs may be any that keep to these rules, and one draw needn't show every extreme that they name: doc_starts is 1 at the first token of every row; in each aligned block of 5 rows one row, drawn from the seed, has no other start.
All inputs are finite; a program needn't handle non-finite values.
Results may differ from the reference program's by a relative error of at most 0.02.
Values may be sent and summed in bfloat16 or wider, within the bound.
A program may use at most 384 MiB of HBM per device.

```python
from functools import partial
import jax
import jax.numpy as jnp
from jax import lax

D = 960
HEADS = 15
KV_HEADS = 5
HEAD = 64
FF = 2560
RANK = 8
WINDOW = 64
STRETCH = 256
ROW_DEV = 5
FEAT = 128
ROWS = 20
LENGTH = 2048


def draw_doc_starts(key, part):
    key = jax.random.fold_in(key, 7)
    first, second = jax.random.split(key)
    marks = (jax.random.randint(first, (ROWS, LENGTH), 0, 4 * STRETCH) == 0).astype(jnp.int32)
    chosen = jax.random.randint(second, (ROWS // ROW_DEV, 1), 0, ROW_DEV)
    whole = (jnp.arange(ROW_DEV, dtype=jnp.int32)[None, :] == chosen).reshape(ROWS, 1)
    marks = jnp.where(whole, 0, marks)
    return marks.at[:, 0].set(1)


def level_of(key, shape, cuts, smallest, high):
    level = 1.0
    for axis_at, shards_of in cuts:
        draws = jax.random.uniform(jax.random.fold_in(jax.random.fold_in(key, 6), axis_at), (shards_of,), jnp.float32, smallest / len(cuts), high / len(cuts))
        level = level * jnp.repeat(jnp.exp(draws), shape[axis_at] // shards_of).reshape((-1,) + (1,) * (len(shape) - 1 - axis_at))
    return level


def scatter_about(stream_key, extent, spread, bound, cuts=(), held_as=jnp.bfloat16):
    values = jax.random.normal(stream_key, extent, jnp.float32) * spread
    if len(cuts) > 0:
        values = level_of(stream_key, extent, cuts, -0.22, 0.18) * values
    return jnp.clip(values, min=-bound, max=bound).astype(held_as)


def setup_inputs(seed: int = 0) -> dict:
    key_list = jax.random.split(jax.random.key(seed), 23)
    tokens = scatter_about(key_list[0], (ROWS, LENGTH, D), 1.0, 6.0, ((0, 4), (1, 8)))
    doc_starts = draw_doc_starts(jax.random.fold_in(key_list[22], 71), 0)
    pregain = jnp.clip(1.0 + 0.1 * jax.random.normal(key_list[2], (D,), jnp.float32), 0.5, 1.5).astype(jnp.bfloat16)
    query_base = scatter_about(key_list[3], (D, D), D ** -0.5, 0.1875)
    key_base = scatter_about(key_list[4], (D, KV_HEADS * HEAD), D ** -0.5, 0.1875)
    value_base = scatter_about(key_list[5], (D, KV_HEADS * HEAD), D ** -0.5, 0.1875)
    output_base = scatter_about(key_list[6], (D, D), HEADS ** -0.5, 1.5)
    query_down = scatter_about(key_list[7], (D, RANK), D ** -0.5, 0.1875)
    query_up = scatter_about(key_list[8], (RANK, D), 0.1, 0.59765625)
    key_down = scatter_about(key_list[9], (D, RANK), D ** -0.5, 0.1875)
    key_up = scatter_about(key_list[10], (RANK, KV_HEADS * HEAD), 0.1, 0.59765625)
    value_down = scatter_about(key_list[11], (D, RANK), D ** -0.5, 0.1875)
    value_up = scatter_about(key_list[12], (RANK, KV_HEADS * HEAD), 0.1, 0.59765625)
    out_down = scatter_about(key_list[13], (D, RANK), HEADS ** -0.5, 1.5)
    out_up = scatter_about(key_list[14], (RANK, D), 0.1, 0.59765625)
    query_map = scatter_about(key_list[15], (HEADS, HEAD, HEAD), HEAD ** -0.5, 0.75)
    key_map = scatter_about(key_list[16], (KV_HEADS, HEAD, HEAD), HEAD ** -0.5, 0.75)
    postgain = jnp.clip(1.0 + 0.1 * jax.random.normal(key_list[17], (D,), jnp.float32), 0.5, 1.5).astype(jnp.bfloat16)
    gate_proj = scatter_about(key_list[18], (D, FF), D ** -0.5, 0.1875)
    up_proj = scatter_about(key_list[19], (D, FF), D ** -0.5, 0.1875)
    down_proj = scatter_about(key_list[20], (FF, D), FF ** -0.5, 0.125)
    cotangent = scatter_about(key_list[21], (ROWS, LENGTH, D), 1.0, 6.0, ((0, 4), (1, 8)))
    return dict(tokens=tokens, doc_starts=doc_starts, pregain=pregain, query_base=query_base, key_base=key_base, value_base=value_base, output_base=output_base, query_down=query_down, query_up=query_up, key_down=key_down, key_up=key_up, value_down=value_down, value_up=value_up, out_down=out_down, out_up=out_up, query_map=query_map, key_map=key_map, postgain=postgain, gate_proj=gate_proj, up_proj=up_proj, down_proj=down_proj, cotangent=cotangent)


@jax.custom_vjp
def low(v):
    return lax.optimization_barrier(v.astype(jnp.bfloat16)).astype(jnp.float32)

@jax.custom_vjp
def low_back(v):
    return v

def low_keep(v):
    return (low(v), None)

def low_pass(kept, grad):
    return (grad,)

def back_keep(v):
    return (v, None)

def back_low(kept, grad):
    return (low(grad),)
low.defvjp(low_keep, low_pass)
low_back.defvjp(back_keep, back_low)
EPSILON = 1e-05
EXACT = lax.Precision.HIGHEST

def product(left, right):
    return jnp.dot(left, right, precision=EXACT, preferred_element_type=jnp.float32)

def normalize(value, gain):
    return value * lax.rsqrt(lax.optimization_barrier(jnp.mean(value * value, axis=-1, keepdims=True)) + EPSILON) * gain

def feature(logit):
    return jnp.concatenate([jax.nn.softmax(logit, axis=-1), jax.nn.softmax(-logit, axis=-1)], axis=-1)

def project(normed, base, down, up):
    inner = low_back(low(product(normed, down)))
    return low_back(low(product(normed, base) + 2.0 * product(inner, up)))

def attend_block(tables, carry, block):
    query_table, key_map = tables
    state, norm, tail_key, tail_value, tail_marks = carry
    query_blk, key_blk, value_blk, mark_blk = block
    span = mark_blk.shape[0]
    width = tail_marks.shape[0]
    keys = jnp.concatenate([tail_key, key_blk], axis=0)
    values = jnp.concatenate([tail_value, value_blk], axis=0)
    marks = jnp.concatenate([tail_marks, mark_blk], axis=0)
    segment = jnp.cumsum(marks).astype(jnp.int32)
    query_seg = segment[width:]
    key_pos = jnp.arange(span + width, dtype=jnp.int32)
    query_pos = jnp.arange(span, dtype=jnp.int32)
    same = query_seg[:, None] == segment[None, :]
    lin_mask = same & (key_pos[None, :] <= query_pos[:, None])
    win_mask = same & (key_pos[None, :] > query_pos[:, None]) & (key_pos[None, :] <= query_pos[:, None] + width)
    shown = (query_seg == 0).astype(jnp.float32)[:, None, None]
    query_logit = low_back(jnp.einsum('lkgd,kgde->lkge', query_blk, query_table, precision=EXACT))
    query_phi = low_back(low(feature(query_logit)))
    key_logit = low_back(jnp.einsum('ekd,kdf->ekf', keys, key_map, precision=EXACT))
    key_phi = low_back(low(feature(key_logit)))
    linear = low_back(jnp.einsum('lkgf,ekf->kgle', query_phi, key_phi, precision=EXACT))
    score = low_back(jnp.einsum('lkgd,ekd->kgle', query_blk, keys, precision=EXACT) * HEAD ** (-0.5))
    weights = jnp.where(lin_mask, linear, 0.0) + jnp.where(win_mask, jnp.exp(score), 0.0)
    local = jnp.einsum('kgle,ekd->lkgd', low(weights), values, precision=EXACT)
    carried = jnp.einsum('lkgf,kdf->lkgd', query_phi, state, precision=EXACT)
    numer = low_back(local + shown[..., None] * carried)
    denom = jnp.transpose(lax.optimization_barrier(jnp.sum(weights, axis=-1)), (2, 0, 1)) + shown * jnp.einsum('lkgf,kf->lkg', query_phi, norm, precision=EXACT)
    mixed = low_back(low(numer / denom[..., None]))
    keep_mask = ((key_pos < span) & (segment == segment[span - 1])).astype(jnp.float32)
    kept = (segment[span - 1] == 0).astype(jnp.float32)
    masked = key_phi * keep_mask[:, None, None]
    new_state = kept * state + jnp.einsum('ekd,ekf->kdf', values, masked, precision=EXACT)
    new_norm = kept * norm + lax.optimization_barrier(jnp.sum(masked, axis=0))
    return ((new_state, new_norm, key_blk[span - width:], value_blk[span - width:], mark_blk[span - width:]), mixed)

def layer_row(trained, frozen, row, marks):
    pregain, query_down, query_up, key_down, key_up, value_down, value_up, out_down, out_up, query_map, key_map, postgain, gate_proj, up_proj, down_proj = trained
    query_base, key_base, value_base, output_base = frozen
    group = HEADS // KV_HEADS
    blocks = LENGTH // STRETCH
    normed = low(normalize(row, pregain))
    query = project(normed, query_base, query_down, query_up)
    key = project(normed, key_base, key_down, key_up)
    value = project(normed, value_base, value_down, value_up)
    query_all = query.reshape(blocks, STRETCH, KV_HEADS, group, HEAD)
    key_all = key.reshape(blocks, STRETCH, KV_HEADS, HEAD)
    value_all = value.reshape(blocks, STRETCH, KV_HEADS, HEAD)
    mark_all = marks.reshape(blocks, STRETCH)
    tables = (query_map.reshape(KV_HEADS, group, HEAD, HEAD), key_map)
    start = (jnp.zeros((KV_HEADS, HEAD, FEAT), jnp.float32), jnp.zeros((KV_HEADS, FEAT), jnp.float32), jnp.zeros((WINDOW, KV_HEADS, HEAD), jnp.float32), jnp.zeros((WINDOW, KV_HEADS, HEAD), jnp.float32), jnp.zeros((WINDOW,), jnp.int32))
    stepper = jax.checkpoint(partial(attend_block, tables))
    final, mixed = lax.scan(stepper, start, (query_all, key_all, value_all, mark_all))
    attended = mixed.reshape(LENGTH, D)
    inner_out = low_back(low(product(attended, out_down)))
    branch = low_back(product(attended, output_base) + 2.0 * product(inner_out, out_up))
    middle = row + branch
    normed_two = low(normalize(middle, postgain))
    gate = low_back(product(normed_two, gate_proj))
    lifted = low_back(product(normed_two, up_proj))
    hidden = low_back(low(jax.nn.silu(gate) * lifted))
    return low(middle + product(hidden, down_proj))

def reference(tokens, doc_starts, pregain, query_base, key_base, value_base, output_base, query_down, query_up, key_down, key_up, value_down, value_up, out_down, out_up, query_map, key_map, postgain, gate_proj, up_proj, down_proj, cotangent):
    trained = tuple((item.astype(jnp.float32) for item in (pregain, query_down, query_up, key_down, key_up, value_down, value_up, out_down, out_up, query_map, key_map, postgain, gate_proj, up_proj, down_proj)))
    frozen = tuple((item.astype(jnp.float32) for item in (query_base, key_base, value_base, output_base)))
    inputs = tokens.astype(jnp.float32)

    def forward(params, rows):

        def one(pair):
            return layer_row(params, frozen, pair[0], pair[1])
        return lax.map(jax.checkpoint(one), (rows, doc_starts))
    result, pullback = jax.vjp(forward, trained, inputs)
    grads, grad_rows = pullback(cotangent.astype(jnp.float32))
    return (result.astype(jnp.bfloat16), grad_rows, grads[0], grads[1], grads[2], grads[3], grads[4], grads[5], grads[6], grads[7], grads[8], grads[9], grads[10], grads[11], grads[12], grads[13], grads[14])
```

```python
import functools

import jax
import jax.numpy as jnp
from jax import lax
from jax.experimental import pallas as pl
from jax.experimental.pallas import tpu as pltpu
from jax.sharding import PartitionSpec as P

WINDOW = 64
EPSILON = 1e-05
BF = jnp.bfloat16
F32 = jnp.float32
NN = (((1,), (0,)), ((), ()))
NT = (((1,), (1,)), ((), ()))
TN = (((0,), (0,)), ((), ()))
HI = 4
TILE = 256
AUG = 80
VMEM = 62 << 20


def dot(left, right, dims=NN):
    return lax.dot_general(left, right, dims, preferred_element_type=F32)


def split_seq(index, count):
    low = max(count // HI, 1)
    return index // low, index % low, count // low, low


def rms(value):
    return lax.rsqrt(jnp.mean(value * value, axis=0, keepdims=True) + EPSILON)


def soft_pair(logit):
    top = jnp.max(logit, axis=0, keepdims=True)
    low = jnp.min(logit, axis=0, keepdims=True)
    up = jnp.exp(logit - top)
    down = jnp.exp(low - logit)
    up = up / jnp.sum(up, axis=0, keepdims=True)
    down = down / jnp.sum(down, axis=0, keepdims=True)
    return jnp.concatenate([up, down], axis=0).astype(BF)


def soft_pair_back(phi, grad):
    half = phi.shape[0] // 2
    up, down = phi[:half].astype(F32), phi[half:].astype(F32)
    gu, gd = grad[:half], grad[half:]
    gu = up * (gu - jnp.sum(up * gu, axis=0, keepdims=True))
    gd = down * (gd - jnp.sum(down * gd, axis=0, keepdims=True))
    return (gu - gd).astype(BF)


def qkv_kernel(tok, gain, wq, wkv, down, qkv, normed, inner, tails, ext):
    width = tok.shape[1]
    kv = wkv.shape[0]
    value = tok[0].astype(F32)
    norm = (value * rms(value) * gain[...]).astype(BF)
    normed[0] = norm
    low = dot(down[...], norm).astype(BF)
    inner[0] = low
    ext[0:width] = norm
    ext[width:] = jnp.zeros((ext.shape[0] - width, ext.shape[1]), BF)
    ext[width : width + low.shape[0]] = low
    qkv[0, 0:width] = dot(wq[...], ext[...], TN).astype(BF)
    both = dot(wkv[...], ext[...]).astype(BF)
    qkv[0, width:] = both
    span = tok.shape[2]
    tails[0] = jnp.concatenate(
        [both[: kv // 2, span - WINDOW :], both[kv // 2 :, span - WINDOW :]], axis=1
    )


def aug_value(value):
    extra = lax.broadcasted_iota(jnp.int32, (AUG - value.shape[0], value.shape[1]), 0) == 0
    return jnp.concatenate([value, jnp.where(extra, 1.0, 0.0).astype(BF)], axis=0)


def key_kernel(kv_heads, qkv, tails, kmap, keep, phi, con):
    head = kmap.shape[1]
    first = qkv.shape[1] - 2 * kv_heads * head
    keeping = keep[0].astype(BF)
    for k in range(kv_heads):
        at = first + k * head
        key = jnp.concatenate([qkv[0, at : at + head], tails[0, k * head : (k + 1) * head, :WINDOW]], axis=1)
        at += kv_heads * head
        val = jnp.concatenate([qkv[0, at : at + head], tails[0, k * head : (k + 1) * head, WINDOW:]], axis=1)
        feat = soft_pair(dot(kmap[k], key, TN))
        phi[0, k] = feat
        con[0, k * AUG : (k + 1) * AUG] = dot(aug_value(val), feat * keeping, NT).astype(BF)


def masks(segq, segk, span):
    extent = segk.shape[0]
    row = lax.broadcasted_iota(jnp.int32, (extent, span), 0)
    pos = jnp.where(row < span, row, row - extent)
    query = lax.broadcasted_iota(jnp.int32, (extent, span), 1)
    same = segk == segq
    far = pos + WINDOW <= query
    return same & far, same & (pos <= query) & jnp.logical_not(far)


def attend_kernel(
    kv_heads, group, qkv, tails, phik, state, segq, segk, qmap, tok, wo, down, gain,
    mixed, den, phiq, middle, normed, inner, ext, lin_bias, win_bias,
):
    head = qmap.shape[1]
    width = tok.shape[1]
    span = tok.shape[2]
    far, near = masks(segq[0], segk[0], span)
    lin_bias[...] = jnp.where(far, 1.0, 0.0)
    win_bias[...] = jnp.where(near, 0.0, -1e30)
    shown = jnp.where(segq[0] == 0, 1.0, 0.0)
    shown3 = jnp.concatenate([shown] * group, axis=1)
    den[0] = jnp.zeros_like(den[0])
    for k in range(kv_heads):
        at = width + k * head
        key = jnp.concatenate([qkv[0, at : at + head], tails[0, k * head : (k + 1) * head, :WINDOW]], axis=1)
        at += kv_heads * head
        val = jnp.concatenate([qkv[0, at : at + head], tails[0, k * head : (k + 1) * head, WINDOW:]], axis=1)
        queries, feats = [], []
        for h in range(k * group, (k + 1) * group):
            q = qkv[0, h * head : (h + 1) * head]
            f = soft_pair(dot(qmap[h], q, TN))
            phiq[0, h] = f
            queries.append(q)
            feats.append(f)
        query = jnp.concatenate(queries, axis=1) * (head**-0.5)
        feat = jnp.concatenate(feats, axis=1)
        lin = dot(phik[0, k], feat, TN)
        score = dot(key, query, TN)
        lb = jnp.concatenate([lin_bias[...]] * group, axis=1)
        wb = jnp.concatenate([win_bias[...]] * group, axis=1)
        weights = lin * lb + jnp.exp(score + wb)
        carried = dot(state[0, k * AUG : (k + 1) * AUG], feat) * shown3
        total = jnp.sum(weights, axis=0, keepdims=True) + carried[head : head + 1]
        numer = dot(val, weights.astype(BF)) + carried[:head]
        out = (numer / total).astype(BF)
        for g in range(group):
            h = k * group + g
            ext[h * head : (h + 1) * head] = out[:, g * span : (g + 1) * span]
            den[0, h : h + 1] = total[:, g * span : (g + 1) * span]
    got = ext[0:width]
    mixed[0] = got
    low = dot(down[...], got).astype(BF)
    inner[0] = low
    ext[width:] = jnp.zeros((ext.shape[0] - width, span), BF)
    ext[width : width + low.shape[0]] = low
    mid = tok[0].astype(F32) + dot(wo[...], ext[...], TN)
    middle[0] = mid
    normed[0] = (mid * rms(mid) * gain[...]).astype(BF)


def ff_kernel(
    width, normed_h, cot_h, middle, gain, gate_h, up_h, down_h,
    out, grad_mid, grad_gain, grads,
    normed, cot, gate_v, up_v, down_v, hid, dgate, dup, sem, act_sem,
):
    step = pl.program_id(0)
    rows = normed_h.shape[0]
    span = normed_h.shape[2]
    high = normed.shape[0]
    hidden = gate_h.shape[1]
    tiles = hidden // TILE

    def act_copies():
        made = []
        for r in range(rows):
            at = pl.ds(r * span, span)
            made.append(pltpu.make_async_copy(normed_h.at[r], normed.at[0:width, at], act_sem.at[r, 0]))
            made.append(pltpu.make_async_copy(cot_h.at[r], cot.at[0:width, at], act_sem.at[r, 1]))
        return made

    def tile_copies(j):
        at = pl.ds(pl.multiple_of(j * TILE, TILE), TILE)
        return [
            pltpu.make_async_copy(gate_h.at[:, at], gate_v.at[0:width, at], sem.at[j, 0]),
            pltpu.make_async_copy(up_h.at[:, at], up_v.at[0:width, at], sem.at[j, 1]),
            pltpu.make_async_copy(down_h.at[:, at], down_v.at[0:width, at], sem.at[j, 2]),
        ]

    @pl.when(step == 0)
    def _():
        for copy in act_copies():
            copy.start()
        for j in range(tiles):
            for copy in tile_copies(j):
                copy.start()
        for ref in (gate_v, up_v, down_v):
            ref[width:] = jnp.zeros((high - width, hidden), BF)
        for ref in (normed, cot):
            ref[width:] = jnp.zeros((high - width, rows * span), BF)
        for copy in act_copies():
            copy.wait()

    @pl.when(step < tiles)
    def _():
        for copy in tile_copies(step):
            copy.wait()
        at = pl.ds(pl.multiple_of(step * TILE, TILE), TILE)
        gate, up, down = gate_v[:, at], up_v[:, at], down_v[:, at]
        for r in range(rows):
            lane = pl.ds(r * span, span)
            n2 = normed[:, lane]
            g = dot(gate, n2, TN)
            u = dot(up, n2, TN)
            dh = dot(down, cot[:, lane], TN).astype(BF).astype(F32)
            sig = 1.0 / (1.0 + jnp.exp(-g))
            act = g * sig
            hid[at, lane] = (act * u).astype(BF)
            dup[at, lane] = (dh * act).astype(BF)
            dgate[at, lane] = (dh * u * (sig + act * (1.0 - sig))).astype(BF)
        grads[0, 0] = dot(normed[...], dgate[at, :], NT)[:width].astype(BF)
        grads[0, 1] = dot(normed[...], dup[at, :], NT)[:width].astype(BF)
        grads[0, 2] = dot(cot[...], hid[at, :], NT)[:width].astype(BF)

    @pl.when(step >= tiles)
    def _():
        r = step - tiles
        lane = pl.ds(pl.multiple_of(r * span, span), span)
        back = dot(gate_v[0:width], dgate[:, lane]) + dot(up_v[0:width], dup[:, lane])
        mid = middle[0]
        scale = rms(mid)
        unit = mid * scale
        grad_unit = back * gain[...]
        grad_mid[0] = cot[0:width, lane].astype(F32) + scale * (
            grad_unit - unit * jnp.mean(grad_unit * unit, axis=0, keepdims=True)
        )

        @pl.when(r == 0)
        def _():
            grad_gain[...] = jnp.zeros_like(grad_gain)

        grad_gain[...] += jnp.sum(back * unit, axis=1, keepdims=True)
        out[0] = (mid + dot(down_v[0:width], hid[:, lane])).astype(BF)


def pull_kernel(
    kv_heads, group, grad_mid, mixed, den, phiq, segq, inner, wo, down,
    dnum, dden, dstate, gup, gdown,
):
    width = mixed.shape[1]
    span = mixed.shape[2]
    head = width // (kv_heads * group)
    low = inner.shape[1]

    @pl.when(pl.program_id(0) == 0)
    def _():
        gup[...] = jnp.zeros_like(gup)
        gdown[...] = jnp.zeros_like(gdown)

    branch = grad_mid[0].astype(BF)
    wide = dot(wo[...], branch)
    grad_inner = wide[width : width + low].astype(BF)
    grad = (wide[:width] + dot(down[...], grad_inner, TN)).astype(BF).astype(F32)
    gup[...] += 2.0 * dot(inner[0], branch, NT)
    gdown[...] += dot(grad_inner, mixed[0], NT)
    shown = jnp.where(segq[0] == 0, 1.0, 0.0)
    dden[0] = jnp.zeros_like(dden[0])
    pad = jnp.zeros((AUG - head - 1, span), F32)
    for k in range(kv_heads):
        total = None
        for g in range(group):
            h = k * group + g
            at = pl.ds(h * head, head)
            dm = grad[h * head : (h + 1) * head]
            inv = 1.0 / den[0, h : h + 1]
            dd = -jnp.sum(dm * mixed[0, at].astype(F32), axis=0, keepdims=True) * inv
            dn = (dm * inv).astype(BF)
            dnum[0, at] = dn
            dden[0, h : h + 1] = dd
            aug = (jnp.concatenate([dn.astype(F32), dd, pad], axis=0) * shown).astype(BF)
            part = dot(aug, phiq[0, h], NT)
            total = part if total is None else total + part
        dstate[0, k * AUG : (k + 1) * AUG] = total.astype(BF)


def back_kernel(
    kv_heads, group, qkv, tails, phik, phiq, state, dcon, dnum, dden, segq, segk, keep, qmap, kmap,
    dq_out, dkv_out, dtails, gqmap, gkmap, lin_bias, win_bias,
):
    head = qmap.shape[1]
    width = dq_out.shape[1]
    span = dq_out.shape[2]
    scale = head**-0.5

    @pl.when(pl.program_id(0) == 0)
    def _():
        gqmap[...] = jnp.zeros_like(gqmap)
        gkmap[...] = jnp.zeros_like(gkmap)

    far, near = masks(segq[0], segk[0], span)
    lin_bias[...] = jnp.where(far, 1.0, 0.0)
    win_bias[...] = jnp.where(near, 0.0, -1e30)
    shown = jnp.where(segq[0] == 0, 1.0, 0.0)
    shown3 = jnp.concatenate([shown] * group, axis=1)
    keeping = keep[0]
    pad = jnp.zeros((AUG - head - 1, group * span), F32)
    for k in range(kv_heads):
        at = width + k * head
        key = jnp.concatenate([qkv[0, at : at + head], tails[0, k * head : (k + 1) * head, :WINDOW]], axis=1)
        at += kv_heads * head
        val = jnp.concatenate([qkv[0, at : at + head], tails[0, k * head : (k + 1) * head, WINDOW:]], axis=1)
        hs = range(k * group, (k + 1) * group)
        queries = [qkv[0, h * head : (h + 1) * head] for h in hs]
        query = jnp.concatenate(queries, axis=1) * scale
        feat = jnp.concatenate([phiq[0, h] for h in hs], axis=1)
        dn = jnp.concatenate([dnum[0, h * head : (h + 1) * head] for h in hs], axis=1)
        dd = jnp.concatenate([dden[0, h : h + 1] for h in hs], axis=1)
        kfeat = phik[0, k]
        lb = jnp.concatenate([lin_bias[...]] * group, axis=1)
        wb = jnp.concatenate([win_bias[...]] * group, axis=1)
        growth = jnp.exp(dot(key, query, TN) + wb)
        weights = (dot(kfeat, feat, TN) * lb + growth).astype(BF)
        dw = dot(val, dn, TN) + dd
        dlin = (dw * lb).astype(BF)
        dscore = (dw * growth).astype(BF)
        dv = dot(dn, weights, NT)
        aug = (jnp.concatenate([dn.astype(F32), dd, pad], axis=0) * shown3).astype(BF)
        held = state[0, k * AUG : (k + 1) * AUG]
        dfeat = dot(kfeat, dlin) + dot(held, aug, TN)
        con = dcon[0, k * AUG : (k + 1) * AUG]
        dkfeat = dot(feat, dlin, NT) + dot(con, aug_value(val), TN) * keeping
        dv = dv + dot(con[:head], kfeat * keeping.astype(BF))
        dq = dot(key, dscore) * scale
        dk = dot(query, dscore, NT)
        dt = soft_pair_back(feat, dfeat.astype(BF).astype(F32))
        for g in range(group):
            h = k * group + g
            part = dt[:, g * span : (g + 1) * span]
            gqmap[h] += dot(queries[g], part, NT)
            full = dq[:, g * span : (g + 1) * span] + dot(qmap[h], part)
            dq_out[0, h * head : (h + 1) * head] = full.astype(BF)
        dtk = soft_pair_back(kfeat, dkfeat.astype(BF).astype(F32))
        gkmap[k] += dot(key, dtk, NT)
        dk = dk + dot(kmap[k], dtk)
        ks, vs = k * head, (kv_heads + k) * head
        dkv_out[0, ks : ks + head] = dk[:, :span]
        dkv_out[0, vs : vs + head] = dv[:, :span]
        dtails[0, ks : ks + head] = jnp.concatenate([dk[:, span:], dv[:, span:]], axis=1).astype(BF)


def final_kernel(
    tok, grad_mid, gain, dq, dkv, returned, normed, inner, wq, wkv, down,
    grad_tok, ggain, gdown, gup,
):
    width = tok.shape[1]
    span = tok.shape[2]
    low = down.shape[0]

    @pl.when(pl.program_id(0) == 0)
    def _():
        ggain[...] = jnp.zeros_like(ggain)
        gdown[...] = jnp.zeros_like(gdown)
        gup[...] = jnp.zeros_like(gup)

    got = returned[0].astype(F32)
    got = jnp.concatenate([got[:, :WINDOW], got[:, WINDOW:]], axis=0)
    own = dkv[0]
    both = jnp.concatenate([own[:, : span - WINDOW], own[:, span - WINDOW :] + got], axis=1).astype(BF)
    grad_q = dq[0]
    wide = dot(wq[...], grad_q) + dot(wkv[...], both, TN)
    grad_inner = wide[width : width + low].astype(BF)
    back = wide[:width] + dot(down[...], grad_inner, TN)
    gdown[...] += dot(grad_inner, normed[0], NT)
    gup[:, :width] += 2.0 * dot(inner[0], grad_q, NT)
    gup[:, width:] += 2.0 * dot(inner[0], both, NT)
    value = tok[0].astype(F32)
    scale = rms(value)
    unit = value * scale
    grad_unit = back * gain[...]
    ggain[...] += jnp.sum(back * unit, axis=1, keepdims=True)
    grad_tok[0] = grad_mid[0] + scale * (
        grad_unit - unit * jnp.mean(grad_unit * unit, axis=0, keepdims=True)
    )


def row_spec(*shape):
    zeros = (0,) * len(shape)
    return pl.BlockSpec((1,) + shape, lambda r: (r,) + zeros)


def whole_spec(*shape):
    zeros = (0,) * len(shape)
    return pl.BlockSpec(shape, lambda r: zeros, pipeline_mode=pl.Buffered(1))


def shape_of(shape, kind):
    return jax.ShapeDtypeStruct(shape, kind)


def row_call(kernel, rows, args, outs, scratch=()):
    in_specs = [row_spec(*a.shape[1:]) if by_row else whole_spec(*a.shape) for a, by_row in args]
    out_specs = tuple(row_spec(*s[1:]) if by_row else pl.BlockSpec(s, functools.partial(lambda n, r: (0,) * n, len(s))) for s, _, by_row in outs)
    return pl.pallas_call(
        kernel,
        grid=(rows,),
        in_specs=in_specs,
        out_specs=out_specs,
        out_shape=tuple(shape_of(s, kind) for s, kind, _ in outs),
        scratch_shapes=list(scratch),
        compiler_params=pltpu.CompilerParams(vmem_limit_bytes=VMEM),
    )(*[a for a, _ in args])


def shifted(array, route):
    return lax.ppermute(array, "seq", route)


def fold(parts, keeps):
    total = None
    for part, keep in zip(parts, keeps):
        total = part if total is None else part + keep[:, None, None] * total
    return total


def carried_states(own, kept, index, count, reverse):
    hi, lo, n_hi, n_lo = split_seq(index, count)
    step = -1 if reverse else 1
    ranks = range(count)

    def keep_of(at):
        return lax.dynamic_slice_in_dim(kept, at, 1, 1)[:, 0]

    around = [own]
    for d in range(1, n_lo):
        route = [(i, i // n_lo * n_lo + (i % n_lo + d) % n_lo) for i in ranks]
        around.append(shifted(own, route))
    around = jnp.stack(around).astype(F32)
    order = list(range(n_lo))[::step]
    total = jnp.zeros_like(around[0])
    before = jnp.zeros_like(around[0])
    keep_all = jnp.ones_like(kept[:, 0])
    keep_before = keep_all
    for pos in order:
        here = lo == pos
        before = jnp.where(here, total, before)
        keep_before = jnp.where(here, keep_all, keep_before)
        part = lax.dynamic_index_in_dim(around, (lo - pos) % n_lo, 0, False)
        keep = keep_of(hi * n_lo + pos)
        total = part + keep[:, None, None] * total
        keep_all = keep * keep_all
    entering = jnp.zeros_like(total)
    for hop in range(n_hi - 1):
        leaving = (total + keep_all[:, None, None] * entering).astype(BF)
        route = [(i, i + step * n_lo) for i in ranks if 0 <= i + step * n_lo < count]
        got = shifted(leaving, route).astype(F32)
        at = n_hi - 2 - hop if reverse else hop + 1
        entering = jnp.where(hi == at, got, entering)
    return (before + keep_before[:, None, None] * entering).astype(BF)


def frames(doc_starts, index, count, span):
    rows = doc_starts.shape[0]
    padded = jnp.concatenate([jnp.zeros((rows, WINDOW), jnp.int32), doc_starts], axis=1)
    kept = jnp.sum(padded[:, : count * span].reshape(rows, count, span), axis=2) == 0
    marks = lax.dynamic_slice_in_dim(padded, index * span, span + WINDOW, 1)
    segment = jnp.cumsum(marks, axis=1)
    own, tail = segment[:, WINDOW:], segment[:, :WINDOW]
    last = own[:, span - WINDOW - 1 : span - WINDOW]
    keys = jnp.concatenate([own, tail], axis=1)
    valid = jnp.concatenate([jnp.arange(span) < span - WINDOW, jnp.full((WINDOW,), True)])
    keep = ((keys == last) & valid[None]).astype(F32)
    return kept.astype(F32), own[:, None, :], keys[:, :, None], keep[:, None, :]


def body(
    tokens, doc_starts, pregain, query_base, key_base, value_base, output_base, query_down, query_up,
    key_down, key_up, value_down, value_up, out_down, out_up, query_map, key_map, postgain, gate_proj,
    up_proj, down_proj, cotangent,
):
    rows, span, width = tokens.shape
    heads, head, _ = query_map.shape
    kv_heads = key_map.shape[0]
    group = heads // kv_heads
    kv_width = kv_heads * head
    rank = query_up.shape[0]
    extent = span + WINDOW
    hidden = gate_proj.shape[1]
    tiles = hidden // TILE
    high = -(-width // 256) * 256
    feats = 2 * head
    slots = -(-heads // 8) * 8
    count = lax.axis_size("seq")
    index = lax.axis_index("seq")

    tok = jnp.swapaxes(tokens, 1, 2)
    cot = jnp.swapaxes(cotangent, 1, 2)
    gain_one = pregain.astype(F32)[:, None]
    gain_two = postgain.astype(F32)[:, None]
    kept, segq, segk, keep = frames(doc_starts, index, count, span)

    zeros = functools.partial(jnp.zeros, dtype=BF)
    wq = jnp.concatenate([query_base, 2 * query_up, zeros((high - width - rank, width))], axis=0)
    kup = jnp.concatenate([zeros((kv_width, rank)), 2 * key_up.T, zeros((kv_width, high - width - 2 * rank))], axis=1)
    vup = jnp.concatenate([zeros((kv_width, 2 * rank)), 2 * value_up.T, zeros((kv_width, high - width - 3 * rank))], axis=1)
    wkv = jnp.concatenate(
        [jnp.concatenate([key_base.T, value_base.T], axis=0), jnp.concatenate([kup, vup], axis=0)], axis=1
    )
    wo = jnp.concatenate([output_base, 2 * out_up, zeros((high - width - rank, width))], axis=0)
    down = jnp.concatenate([query_down.T, key_down.T, value_down.T], axis=0)
    odown = out_down.T

    ext = pltpu.VMEM((high, span), BF)
    biases = [pltpu.VMEM((extent, span), F32)] * 2
    qkv, normed, inner, tails = row_call(
        qkv_kernel,
        rows,
        [(tok, 1), (gain_one, 0), (wq, 0), (wkv, 0), (down, 0)],
        [
            ((rows, width + 2 * kv_width, span), BF, 1),
            ((rows, width, span), BF, 1),
            ((rows, 3 * rank, span), BF, 1),
            ((rows, kv_width, 2 * WINDOW), BF, 1),
        ],
        [ext],
    )
    tails = shifted(tails, [(i, i + 1) for i in range(count - 1)])
    phik, con = row_call(
        functools.partial(key_kernel, kv_heads),
        rows,
        [(qkv, 1), (tails, 1), (key_map, 0), (keep, 1)],
        [((rows, kv_heads, feats, extent), BF, 1), ((rows, kv_heads * AUG, feats), BF, 1)],
    )
    state = carried_states(con, kept, index, count, False)
    mixed, den, phiq, middle, normed2, inner_o = row_call(
        functools.partial(attend_kernel, kv_heads, group),
        rows,
        [
            (qkv, 1), (tails, 1), (phik, 1), (state, 1), (segq, 1), (segk, 1), (query_map, 0), (tok, 1),
            (wo, 0), (odown, 0), (gain_two, 0),
        ],
        [
            ((rows, width, span), BF, 1),
            ((rows, slots, span), F32, 1),
            ((rows, heads, feats, span), BF, 1),
            ((rows, width, span), F32, 1),
            ((rows, width, span), BF, 1),
            ((rows, rank, span), BF, 1),
        ],
        [ext] + biases,
    )

    last = lambda s: (jnp.maximum(s - tiles, 0), 0, 0)
    fixed = lambda s: (0, 0)
    anywhere = pl.BlockSpec(memory_space=pl.ANY)
    layer_out, grad_mid, grad_postgain, grads = pl.pallas_call(
        functools.partial(ff_kernel, width),
        grid=(tiles + rows,),
        in_specs=[anywhere, anywhere, pl.BlockSpec((1, width, span), last), pl.BlockSpec((width, 1), fixed)]
        + [anywhere] * 3,
        out_specs=(
            pl.BlockSpec((1, width, span), last),
            pl.BlockSpec((1, width, span), last),
            pl.BlockSpec((width, 1), fixed),
            pl.BlockSpec((1, 3, width, TILE), lambda s: (jnp.minimum(s, tiles - 1), 0, 0, 0)),
        ),
        out_shape=(
            shape_of((rows, width, span), BF),
            shape_of((rows, width, span), F32),
            shape_of((width, 1), F32),
            shape_of((tiles, 3, width, TILE), BF),
        ),
        scratch_shapes=[pltpu.VMEM((high, rows * span), BF)] * 2
        + [pltpu.VMEM((high, hidden), BF)] * 3
        + [pltpu.VMEM((hidden, rows * span), BF)] * 3
        + [pltpu.SemaphoreType.DMA((tiles, 3)), pltpu.SemaphoreType.DMA((rows, 2))],
        compiler_params=pltpu.CompilerParams(vmem_limit_bytes=VMEM),
    )(normed2, cot, middle, gain_two, gate_proj, up_proj, down_proj.T)

    dnum, dden, dstate, gup_o, gdown_o = row_call(
        functools.partial(pull_kernel, kv_heads, group),
        rows,
        [
            (grad_mid, 1), (mixed, 1), (den, 1), (phiq, 1), (segq, 1), (inner_o, 1), (wo, 0), (odown, 0),
        ],
        [
            ((rows, width, span), BF, 1),
            ((rows, slots, span), F32, 1),
            ((rows, kv_heads * AUG, feats), BF, 1),
            ((rank, width), F32, 0),
            ((rank, width), F32, 0),
        ],
    )
    dcon = carried_states(dstate, kept, index, count, True)
    dq, dkv, dtails, gqmap, gkmap = row_call(
        functools.partial(back_kernel, kv_heads, group),
        rows,
        [
            (qkv, 1), (tails, 1), (phik, 1), (phiq, 1), (state, 1), (dcon, 1), (dnum, 1), (dden, 1),
            (segq, 1), (segk, 1), (keep, 1), (query_map, 0), (key_map, 0),
        ],
        [
            ((rows, width, span), BF, 1),
            ((rows, 2 * kv_width, span), F32, 1),
            ((rows, kv_width, 2 * WINDOW), BF, 1),
            ((heads, head, head), F32, 0),
            ((kv_heads, head, head), F32, 0),
        ],
        biases,
    )
    returned = shifted(dtails, [(i, i - 1) for i in range(1, count)])
    grad_tok, grad_pregain, gdown, gup = row_call(
        final_kernel,
        rows,
        [
            (tok, 1), (grad_mid, 1), (gain_one, 0), (dq, 1), (dkv, 1), (returned, 1), (normed, 1), (inner, 1),
            (wq, 0), (wkv, 0), (down, 0),
        ],
        [
            ((rows, width, span), F32, 1),
            ((width, 1), F32, 0),
            ((3 * rank, width), F32, 0),
            ((3 * rank, width + 2 * kv_width), F32, 0),
        ],
    )

    both = ("batch", "seq")
    small = lax.psum(
        (grad_pregain, gdown, gup, gdown_o, gup_o, gqmap, gkmap, grad_postgain), both
    )
    grad_pregain, gdown, gup, gdown_o, gup_o, gqmap, gkmap, grad_postgain = small
    grads = lax.psum(grads, both).astype(F32)
    grads = jnp.moveaxis(grads, 0, 2).reshape(3, width, hidden)
    ends = (width, width + kv_width, width + 2 * kv_width)
    return (
        jnp.swapaxes(layer_out, 1, 2),
        jnp.swapaxes(grad_tok, 1, 2),
        grad_pregain[:, 0],
        gdown[:rank].T,
        gup[:rank, : ends[0]],
        gdown[rank : 2 * rank].T,
        gup[rank : 2 * rank, ends[0] : ends[1]],
        gdown[2 * rank :].T,
        gup[2 * rank :, ends[1] :],
        gdown_o.T,
        gup_o,
        gqmap,
        gkmap,
        grad_postgain[:, 0],
        grads[0],
        grads[1],
        grads[2].T,
    )


def solution(mesh):
    wide = P("batch", "seq", None)
    return jax.shard_map(
        body,
        mesh=mesh,
        in_specs=(wide, P("batch", None)) + (P(),) * 19 + (wide,),
        out_specs=(wide, wide) + (P(),) * 15,
        check_vma=False,
    )
```

```python
import functools

import jax
import jax.numpy as jnp
from jax import lax
from jax.experimental import pallas as pl
from jax.experimental.pallas import tpu as pltpu
from jax.sharding import PartitionSpec as P

WINDOW = 64
EPSILON = 1e-05
BF = jnp.bfloat16
F32 = jnp.float32
NN = (((1,), (0,)), ((), ()))
NT = (((1,), (1,)), ((), ()))
TN = (((0,), (0,)), ((), ()))
HI = 4
TILE = 256
AUG = 80
VMEM = 62 << 20
MESH = pl.DeviceIdType.MESH


def dot(left, right, dims=NN):
    return lax.dot_general(left, right, dims, preferred_element_type=F32)


def split_seq(index, count):
    low = max(count // HI, 1)
    return index // low, index % low, count // low, low


class Place:
    def __init__(self):
        batch, seq = lax.axis_index("batch"), lax.axis_index("seq")
        n_seq = lax.axis_size("seq")
        hi, lo, n_hi, n_lo = split_seq(seq, n_seq)
        self.batch, self.seq = batch, seq
        self.at = {"core": batch % 2, "y": batch // 2, "hi": hi, "lo": lo}
        self.size = axis_sizes()

    def peer(self, axis, distance):
        at = dict(self.at)
        at[axis] = (at[axis] + distance) % self.size[axis]
        return (at["y"] * 2 + at["core"], at["hi"] * self.size["lo"] + at["lo"])

    def along(self, distance):
        return (self.batch, self.seq + distance)

    def inside(self, distance):
        return (self.seq + distance >= 0) & (self.seq + distance < self.size["hi"] * self.size["lo"])

    def greet(self):
        barrier = pltpu.get_barrier_semaphore()
        total = 0
        for d in (-1, 1):

            @pl.when(self.inside(d))
            def _():
                pl.semaphore_signal(barrier, inc=1, device_id=self.along(d), device_id_type=MESH)

            total = total + jnp.where(self.inside(d), 1, 0)
        for axis, size in self.size.items():
            for d in range(1, size):
                pl.semaphore_signal(barrier, inc=1, device_id=self.peer(axis, d), device_id_type=MESH)
                total = total + 1
        pl.semaphore_wait(barrier, total)


def axis_sizes():
    _, _, n_hi, n_lo = split_seq(0, lax.axis_size("seq"))
    return {"core": 2, "y": lax.axis_size("batch") // 2, "hi": n_hi, "lo": n_lo}


def stream_plan(rows):
    size = axis_sizes()
    orders = [("lo", "y", "hi"), ("y", "lo", "hi")]
    devices = size["lo"] * size["y"] * size["hi"]
    if rows // (2 * devices) % 16:
        orders = orders[:1]
    part = rows // len(orders)
    plan = []
    for i, order in enumerate(orders):
        left, stages = part, []
        for axis in order:
            left = left // size[axis]
            stages.append((axis, left))
        plan.append((i * part, part, stages))
    return plan


def remote(src, dst, send, recv, peer):
    return pltpu.make_async_remote_copy(
        src_ref=src, dst_ref=dst, send_sem=send, recv_sem=recv, device_id=peer, device_id_type=MESH
    )


LAGS = (1, 3, 4, 5)


def stage_slots(k, slots):
    return 2 * slots if k == 1 else slots


def scatter_scratch(rows, kind, slots=2):
    size = axis_sizes()
    made = [
        pltpu.VMEM((slots, 2, rows, 128), kind),
        pltpu.VMEM((slots, rows, 128), kind),
        pltpu.VMEM((stage_slots(1, slots), rows, 128), kind),
        pltpu.SemaphoreType.DMA((2, slots)),
    ]
    for _, _, stages in stream_plan(rows):
        for k, (axis, left) in enumerate(stages, 1):
            peers = max(size[axis] - 1, 1)
            made.append(pltpu.VMEM((stage_slots(k, slots), peers, left, 128), kind))
            made.append(pltpu.VMEM((slots, left, 128), kind))
            made.append(pltpu.SemaphoreType.DMA((2, stage_slots(k, slots), peers)))
    return made


class Scatter:
    def __init__(self, place, rows, refs, slots=2):
        self.place, self.rows, self.slots = place, rows, slots
        self.mine, self.other, self.base, self.core_sem = refs[:4]
        self.streams = []
        at = 4
        for first, part, stages in stream_plan(rows):
            made = []
            for axis, left in stages:
                made.append((axis, left) + tuple(refs[at : at + 3]))
                at += 3
            self.streams.append((first, part, made))

    def core_copy(self, t):
        slot = t % self.slots
        core = self.place.at["core"]
        return remote(
            self.mine.at[slot, 1 - core], self.other.at[slot],
            self.core_sem.at[0, slot], self.core_sem.at[1, slot], self.place.peer("core", 1),
        )

    def copies(self, k, t):
        slot = t % stage_slots(k, self.slots)
        made = []
        for first, part, stages in self.streams:
            axis, left, got, _, sem = stages[k - 1]
            size = self.place.size[axis]
            for d in range(1, size):
                to = (self.place.at[axis] + d) % size
                if k == 1:
                    src = self.base.at[slot, pl.ds(pl.multiple_of(first + to * left, 16), left)]
                else:
                    src = stages[k - 2][3].at[t % self.slots, pl.ds(pl.multiple_of(to * left, 16), left)]
                made.append(
                    remote(
                        src, got.at[slot, d - 1], sem.at[0, slot, d - 1], sem.at[1, slot, d - 1],
                        self.place.peer(axis, d),
                    )
                )
        return made

    def start(self, k, t):
        for copy in [self.core_copy(t)] if k == 0 else self.copies(k, t):
            copy.start()

    def finish(self, k, t, into=None):
        slot = t % self.slots
        ahead = t % stage_slots(k, self.slots)
        if k == 0:
            self.core_copy(t).wait()
            core = self.place.at["core"]
            self.base[t % stage_slots(1, self.slots)] = (self.mine[slot, core].astype(F32) + self.other[slot].astype(F32)).astype(self.base.dtype)
            return
        for copy in self.copies(k, t):
            copy.wait()
        for i, (first, part, stages) in enumerate(self.streams):
            axis, left, got, out, _ = stages[k - 1]
            at = self.place.at[axis] * left
            if k == 1:
                own = self.base[ahead, pl.ds(pl.multiple_of(first + at, 16), left)]
            else:
                own = stages[k - 2][3][slot, pl.ds(pl.multiple_of(at, 16), left)]
            total = own.astype(F32)
            for d in range(1, self.place.size[axis]):
                total = total + got[ahead, d - 1].astype(F32)
            if k == 3:
                into(i, total)
            else:
                out[slot] = total.astype(out.dtype)

    def run(self, into):
        self.start(0, 0)
        for k in range(4):
            self.finish(k, 0, into)
            if k < 3:
                self.start(k + 1, 0)

    def turn(self, step, tiles, into):
        for k in (3, 2, 1, 0):
            t = step - LAGS[k]

            @pl.when((t >= 0) & (t < tiles))
            def _():
                self.finish(k, t, functools.partial(into, t))
                if k < 3:
                    self.start(k + 1, t)

        @pl.when(step < tiles)
        def _():
            self.start(0, step)


WAYS = (6, 5, 3, 1)


def gather_scratch(rows, tiles):
    size = axis_sizes()
    made = [pltpu.SemaphoreType.DMA((2, tiles)), pltpu.SemaphoreType.DMA((tiles, len(stream_plan(rows))))]
    for _, _, stages in stream_plan(rows):
        for axis, left in stages:
            made.append(pltpu.SemaphoreType.DMA((2, tiles, max(size[axis] - 1, 1))))
    return made


class Gather:
    def __init__(self, place, rows, shards, whole, refs):
        self.place, self.rows, self.shards, self.whole = place, rows, shards, whole
        self.core_sem, self.own_sem = refs[:2]
        self.streams = []
        at = 2
        for first, part, stages in stream_plan(rows):
            self.streams.append((first, part, [st + (refs[at + i],) for i, st in enumerate(stages)]))
            at += len(stages)

    def region(self, t, stream, k):
        first, _, stages = self.streams[stream]
        at = first
        for axis, left, _ in stages[:k]:
            at = at + self.place.at[axis] * left
        return self.whole.at[t, self.place.at["core"], pl.ds(pl.multiple_of(at, 16), stages[k - 1][1])]

    def own_copies(self, t):
        return [
            pltpu.make_async_copy(self.shards.at[t, i], self.region(t, i, 3), self.own_sem.at[t, i])
            for i in range(len(self.streams))
        ]

    def copies(self, k, t):
        if k == 0:
            half = self.whole.at[t, self.place.at["core"]]
            return [remote(half, half, self.core_sem.at[0, t], self.core_sem.at[1, t], self.place.peer("core", 1))]
        made = []
        for i, (_, _, stages) in enumerate(self.streams):
            axis, left, sem = stages[k - 1]
            dst = self.region(t, i, k)
            src = self.shards.at[t, i] if k == 3 else dst
            for d in range(1, self.place.size[axis]):
                made.append(remote(src, dst, sem.at[0, t, d - 1], sem.at[1, t, d - 1], self.place.peer(axis, d)))
        return made

    def run(self):
        for copy in self.own_copies(0) + self.copies(3, 0):
            copy.start()
        for k in (3, 2, 1, 0):
            for copy in self.copies(k, 0) + (self.own_copies(0) if k == 3 else []):
                copy.wait()
            if k > 0:
                for copy in self.copies(k - 1, 0):
                    copy.start()

    def turn(self, step, tiles):
        for k in (0, 1, 2, 3):
            t = step - WAYS[k]

            @pl.when((t >= 0) & (t < tiles))
            def _():
                for copy in self.copies(k, t):
                    copy.wait()
                if k == 3:
                    for copy in self.own_copies(t):
                        copy.wait()
                if k > 0:
                    for copy in self.copies(k - 1, t):
                        copy.start()

        @pl.when(step < tiles)
        def _():
            for copy in self.own_copies(step) + self.copies(3, step):
                copy.start()


class Chain:
    def __init__(self, place, reverse, kept, own, around, total, before, leaving, entering, result, lo_sem, hi_sem):
        self.place, self.reverse, self.kept = place, reverse, kept
        self.own, self.around, self.total, self.before = own, around, total, before
        self.leaving, self.entering, self.result = leaving, entering, result
        self.lo_sem, self.hi_sem = lo_sem, hi_sem
        self.n_hi, self.n_lo = place.size["hi"], place.size["lo"]
        hi = place.at["hi"]
        self.rank = self.n_hi - 1 - hi if reverse else hi

    def lo_copies(self, r):
        return [
            remote(
                self.own.at[r], self.around.at[d - 1, r], self.lo_sem.at[0, r, d - 1], self.lo_sem.at[1, r, d - 1],
                self.place.peer("lo", d),
            )
            for d in range(1, self.n_lo)
        ]

    def hi_copy(self, r):
        return remote(
            self.leaving.at[r], self.entering.at[r], self.hi_sem.at[0, r], self.hi_sem.at[1, r],
            self.place.peer("hi", -1 if self.reverse else 1),
        )

    def keep(self, r, pos):
        return self.kept[r, self.place.at["hi"] * self.n_lo + pos]

    def order(self):
        return list(range(self.n_lo))[:: -1 if self.reverse else 1]

    def begin(self, r):
        for copy in self.lo_copies(r):
            copy.start()

    def leave(self, r, value):
        @pl.when(self.rank < self.n_hi - 1)
        def _():
            self.leaving[r] = value.astype(BF)
            self.hi_copy(r).start()

    def join(self, r):
        for copy in self.lo_copies(r):
            copy.wait()
        lo = self.place.at["lo"]
        total = jnp.zeros(self.own.shape[1:], F32)
        before = total
        for pos in self.order():
            part = self.own[r].astype(F32)
            before = jnp.where(lo == pos, total, before)
            for d in range(1, self.n_lo):
                part = jnp.where((lo - pos) % self.n_lo == d, self.around[d - 1, r].astype(F32), part)
            total = part + self.keep(r, pos) * total
        self.total[r] = total
        self.before[r] = before

        @pl.when(self.rank == 0)
        def _():
            self.leave(r, total)
            self.result[r] = before.astype(BF)

    def hop(self, r):
        self.hi_copy(r).wait_recv()
        entering = self.entering[r].astype(F32)
        lo = self.place.at["lo"]
        keep_all, keep_before = jnp.float32(1), jnp.float32(1)
        for pos in self.order():
            keep_before = jnp.where(lo == pos, keep_all, keep_before)
            keep_all = keep_all * self.keep(r, pos)
        self.leave(r, self.total[r] + keep_all * entering)
        self.result[r] = (self.before[r] + keep_before * entering).astype(BF)

    def turn(self, step, rows):
        for q in range(self.n_hi - 1, 0, -1):
            r = step - 1 - q

            @pl.when((r >= 0) & (r < rows) & (self.rank == q))
            def _():
                self.hop(r)

        r = step - 1

        @pl.when((r >= 0) & (r < rows))
        def _():
            self.join(r)

        @pl.when(step < rows)
        def _():
            self.begin(step)

    def close(self, rows):
        @pl.when(self.rank < self.n_hi - 1)
        def _():
            for r in range(rows):
                self.hi_copy(r).wait_send()


def chain_scratch(rows, height, feats):
    size = axis_sizes()
    peers = max(size["lo"] - 1, 1)
    shape = (rows, height, feats)
    return [
        pltpu.VMEM(shape, BF),
        pltpu.VMEM((peers,) + shape, BF),
        pltpu.VMEM(shape, F32),
        pltpu.VMEM(shape, F32),
        pltpu.VMEM(shape, BF),
        pltpu.VMEM(shape, BF),
        pltpu.VMEM(shape, BF),
        pltpu.SemaphoreType.DMA((2, rows, peers)),
        pltpu.SemaphoreType.DMA((2, rows)),
    ]


class Small:
    def __init__(self, rank, width, kv_width, heads, kv_heads, head):
        def chunks(lanes):
            return -(-lanes // 128)

        tall = -(-(3 * rank + 2) // 16) * 16
        flat = -(-2 * rank // 16) * 16
        sections = [
            ("down", tall, chunks(width)),
            ("out", flat, chunks(width)),
            ("q_up", -(-rank // 16) * 16, chunks(width)),
            ("kv_up", -(-2 * rank // 16) * 16, chunks(kv_width)),
            ("qmap", head, (heads + 1) // 2),
            ("kmap", head, (kv_heads + 1) // 2),
        ]
        need = sum(rows * n for _, rows, n in sections)
        size = axis_sizes()
        grain = 16 * size["lo"] * size["y"] * size["hi"]
        self.rows = -(-(need + 64) // (2 * grain)) * grain
        self.place = {}
        half, at = 0, 0
        for name, rows, n in sections:
            self.place[name] = []
            for _ in range(n):
                if at + rows > self.rows:
                    half, at = half + 1, 0
                self.place[name].append((half, at, rows))
                at += rows

    def put(self, ref, name, value):
        for c, (half, at, rows) in enumerate(self.place[name]):
            part = value[:, c * 128 : (c + 1) * 128]
            ref[0, half, at : at + part.shape[0], 0 : part.shape[1]] = part.astype(ref.dtype)

    def put_heads(self, ref, name, maps):
        for c, (half, at, rows) in enumerate(self.place[name]):
            pair = [maps[h] for h in range(2 * c, min(2 * c + 2, maps.shape[0]))]
            pair = jnp.concatenate(pair, axis=1) if len(pair) > 1 else pair[0]
            ref[0, half, at : at + rows, 0 : pair.shape[1]] = pair.astype(ref.dtype)

    def take(self, ref, name, lanes):
        parts = [ref[0, half, at : at + rows].astype(F32) for half, at, rows in self.place[name]]
        return jnp.concatenate(parts, axis=1)[:, :lanes]


def widen_kernel(width, high, rank, layout, whole, small, gate, up, down, *outs):
    for i, out in enumerate((gate, up, down)):
        out[...] = whole[0, 0, i * high : i * high + width].astype(F32)

    @pl.when(pl.program_id(0) == 0)
    def _():
        pre, post, qd, kd, vd, qu, ku, vu, od, ou, qmap, kmap = outs
        downs = layout.take(small, "down", width)
        for i, out in enumerate((qd, kd, vd)):
            out[...] = downs[i * rank : (i + 1) * rank]
        pre[...] = downs[3 * rank : 3 * rank + 1]
        post[...] = downs[3 * rank + 1 : 3 * rank + 2]
        pair = layout.take(small, "out", width)
        od[...] = pair[:rank]
        ou[...] = pair[rank : 2 * rank]
        qu[...] = layout.take(small, "q_up", width)[:rank]
        pair = layout.take(small, "kv_up", ku.shape[1])
        ku[...] = pair[:rank]
        vu[...] = pair[rank : 2 * rank]
        head = qmap.shape[1]
        for name, out in (("qmap", qmap), ("kmap", kmap)):
            for h in range(out.shape[0]):
                half, at, rows = layout.place[name][h // 2]
                both = small[0, half, at : at + rows].astype(F32)
                out[h] = both[:, (h % 2) * head : (h % 2 + 1) * head]


def row_sum(value):
    return dot(jnp.ones((8, value.shape[1]), BF), value.astype(BF), NT)


def rms(value):
    return lax.rsqrt(jnp.mean(value * value, axis=0, keepdims=True) + EPSILON)


def soft_pair(logit):
    top = jnp.max(logit, axis=0, keepdims=True)
    low = jnp.min(logit, axis=0, keepdims=True)
    up = jnp.exp(logit - top)
    down = jnp.exp(low - logit)
    up = up / jnp.sum(up, axis=0, keepdims=True)
    down = down / jnp.sum(down, axis=0, keepdims=True)
    return jnp.concatenate([up, down], axis=0).astype(BF)


def soft_pair_back(phi, grad):
    half = phi.shape[0] // 2
    up, down = phi[:half].astype(F32), phi[half:].astype(F32)
    gu, gd = grad[:half], grad[half:]
    gu = up * (gu - jnp.sum(up * gu, axis=0, keepdims=True))
    gd = down * (gd - jnp.sum(down * gd, axis=0, keepdims=True))
    return (gu - gd).astype(BF)


def qkv_kernel(tok, gain, wq, wkv, down, qkv, normed, inner, tails, ext):
    width = tok.shape[1]
    kv = wkv.shape[0]
    value = tok[0].astype(F32)
    norm = (value * rms(value) * gain[...]).astype(BF)
    normed[0] = norm
    low = dot(down[...], norm).astype(BF)
    inner[0] = low
    ext[0:width] = norm
    ext[width:] = jnp.zeros((ext.shape[0] - width, ext.shape[1]), BF)
    ext[width : width + low.shape[0]] = low
    qkv[0, 0:width] = dot(wq[...], ext[...], TN).astype(BF)
    both = dot(wkv[...], ext[...]).astype(BF)
    qkv[0, width:] = both
    span = tok.shape[2]
    tails[0] = jnp.concatenate(
        [both[: kv // 2, span - WINDOW :], both[kv // 2 :, span - WINDOW :]], axis=1
    )


def aug_value(value):
    extra = lax.broadcasted_iota(jnp.int32, (AUG - value.shape[0], value.shape[1]), 0) == 0
    return jnp.concatenate([value, jnp.where(extra, 1.0, 0.0).astype(BF)], axis=0)


def key_kernel(kv_heads, qkv, tails, kmap, keep, phi, con):
    head = kmap.shape[1]
    first = qkv.shape[1] - 2 * kv_heads * head
    keeping = keep[0].astype(BF)
    for k in range(kv_heads):
        at = first + k * head
        key = jnp.concatenate([qkv[0, at : at + head], tails[0, k * head : (k + 1) * head, :WINDOW]], axis=1)
        at += kv_heads * head
        val = jnp.concatenate([qkv[0, at : at + head], tails[0, k * head : (k + 1) * head, WINDOW:]], axis=1)
        feat = soft_pair(dot(kmap[k], key, TN))
        phi[0, k] = feat
        con[0, k * AUG : (k + 1) * AUG] = dot(aug_value(val), feat * keeping, NT).astype(BF)


def masks(segq, segk, span):
    extent = segk.shape[0]
    row = lax.broadcasted_iota(jnp.int32, (extent, span), 0)
    pos = jnp.where(row < span, row, row - extent)
    query = lax.broadcasted_iota(jnp.int32, (extent, span), 1)
    same = segk == segq
    far = pos + WINDOW <= query
    return same & far, same & (pos <= query) & jnp.logical_not(far)


def attend_kernel(
    kv_heads, group, qkv, tails, phik, state, segq, segk, qmap, tok, wo, down, gain,
    mixed, den, phiq, middle, normed, inner, ext, lin_bias, win_bias,
):
    head = qmap.shape[1]
    width = tok.shape[1]
    span = tok.shape[2]
    far, near = masks(segq[0], segk[0], span)
    lin_bias[...] = jnp.where(far, 1.0, 0.0)
    win_bias[...] = jnp.where(near, 0.0, -1e30)
    shown = jnp.where(segq[0] == 0, 1.0, 0.0)
    shown3 = jnp.concatenate([shown] * group, axis=1)
    den[0] = jnp.zeros_like(den[0])
    for k in range(kv_heads):
        at = width + k * head
        key = jnp.concatenate([qkv[0, at : at + head], tails[0, k * head : (k + 1) * head, :WINDOW]], axis=1)
        at += kv_heads * head
        val = jnp.concatenate([qkv[0, at : at + head], tails[0, k * head : (k + 1) * head, WINDOW:]], axis=1)
        queries, feats = [], []
        for h in range(k * group, (k + 1) * group):
            q = qkv[0, h * head : (h + 1) * head]
            f = soft_pair(dot(qmap[h], q, TN))
            phiq[0, h] = f
            queries.append(q)
            feats.append(f)
        query = jnp.concatenate(queries, axis=1) * (head**-0.5)
        feat = jnp.concatenate(feats, axis=1)
        lin = dot(phik[0, k], feat, TN)
        score = dot(key, query, TN)
        lb = jnp.concatenate([lin_bias[...]] * group, axis=1)
        wb = jnp.concatenate([win_bias[...]] * group, axis=1)
        weights = lin * lb + jnp.exp(score + wb)
        carried = dot(state[0, k * AUG : (k + 1) * AUG], feat) * shown3
        total = jnp.sum(weights, axis=0, keepdims=True) + carried[head : head + 1]
        numer = dot(val, weights.astype(BF)) + carried[:head]
        out = (numer / total).astype(BF)
        for g in range(group):
            h = k * group + g
            ext[h * head : (h + 1) * head] = out[:, g * span : (g + 1) * span]
            den[0, h : h + 1] = total[:, g * span : (g + 1) * span]
    got = ext[0:width]
    mixed[0] = got
    low = dot(down[...], got).astype(BF)
    inner[0] = low
    ext[width:] = jnp.zeros((ext.shape[0] - width, span), BF)
    ext[width : width + low.shape[0]] = low
    mid = tok[0].astype(F32) + dot(wo[...], ext[...], TN)
    middle[0] = mid
    normed[0] = (mid * rms(mid) * gain[...]).astype(BF)


def ff_kernel(
    width, normed_h, cot_h, middle, gain, gate_h, up_h, down_h,
    out, grad_mid, grad_gain, shards,
    normed, cot, gate_v, up_v, down_v, hid, dgate, dup, sem, act_sem, *refs,
):
    step = pl.program_id(0)
    rows = normed_h.shape[0]
    span = normed_h.shape[2]
    high = normed.shape[0]
    hidden = gate_h.shape[1]
    tiles = hidden // TILE
    place = Place()
    scatter = Scatter(place, 3 * high, refs)

    def act_copies():
        made = []
        for r in range(rows):
            at = pl.ds(r * span, span)
            made.append(pltpu.make_async_copy(normed_h.at[r], normed.at[0:width, at], act_sem.at[r, 0]))
            made.append(pltpu.make_async_copy(cot_h.at[r], cot.at[0:width, at], act_sem.at[r, 1]))
        return made

    def tile_copies(j):
        at = pl.ds(pl.multiple_of(j * TILE, TILE), TILE)
        return [
            pltpu.make_async_copy(gate_h.at[:, at], gate_v.at[0:width, at], sem.at[j, 0]),
            pltpu.make_async_copy(up_h.at[:, at], up_v.at[0:width, at], sem.at[j, 1]),
            pltpu.make_async_copy(down_h.at[:, at], down_v.at[0:width, at], sem.at[j, 2]),
        ]

    @pl.when(step == 0)
    def _():
        place.greet()
        for copy in act_copies():
            copy.start()
        for j in range(tiles):
            for copy in tile_copies(j):
                copy.start()
        for ref in (gate_v, up_v, down_v):
            ref[width:] = jnp.zeros((high - width, hidden), BF)
        for ref in (normed, cot):
            ref[width:] = jnp.zeros((high - width, rows * span), BF)
        for copy in act_copies():
            copy.wait()

    @pl.when(step < tiles)
    def _():
        for copy in tile_copies(step):
            copy.wait()
        at = pl.ds(pl.multiple_of(step * TILE, TILE), TILE)
        gate, up, down = gate_v[:, at], up_v[:, at], down_v[:, at]
        for r in range(rows):
            lane = pl.ds(r * span, span)
            n2 = normed[:, lane]
            g = dot(gate, n2, TN)
            u = dot(up, n2, TN)
            dh = dot(down, cot[:, lane], TN).astype(BF).astype(F32)
            sig = 1.0 / (1.0 + jnp.exp(-g))
            act = g * sig
            hid[at, lane] = (act * u).astype(BF)
            dup[at, lane] = (dh * act).astype(BF)
            dgate[at, lane] = (dh * u * (sig + act * (1.0 - sig))).astype(BF)
        slot = step % 2
        for i, (left, right) in enumerate(((normed, dgate), (normed, dup), (cot, hid))):
            grad = dot(left[...], right[at, :], NT).astype(BF)
            for half in range(2):
                scatter.mine[slot, half, i * high : (i + 1) * high] = grad[:, half * 128 : (half + 1) * 128]

    @pl.when(step >= tiles)
    def _():
        r = step - tiles
        lane = pl.ds(pl.multiple_of(r * span, span), span)
        back = dot(gate_v[0:width], dgate[:, lane]) + dot(up_v[0:width], dup[:, lane])
        mid = middle[0]
        scale = rms(mid)
        unit = mid * scale
        grad_unit = back * gain[...]
        grad_mid[0] = cot[0:width, lane].astype(F32) + scale * (
            grad_unit - unit * jnp.mean(grad_unit * unit, axis=0, keepdims=True)
        )

        @pl.when(r == 0)
        def _():
            grad_gain[...] = jnp.zeros_like(grad_gain)

        grad_gain[...] += row_sum(back * unit)
        out[0] = (mid + dot(down_v[0:width], hid[:, lane])).astype(BF)

    def into(tile, stream, total):
        shards[tile, stream] = total.astype(BF)

    scatter.turn(step, tiles, into)


def pull_kernel(
    kv_heads, group, grad_mid, mixed, den, phiq, segq, inner, wo, down,
    dnum, dden, dstate, gup, gdown,
):
    width = mixed.shape[1]
    span = mixed.shape[2]
    head = width // (kv_heads * group)
    low = inner.shape[1]

    branch = grad_mid[0].astype(BF)
    wide = dot(wo[...], branch)
    grad_inner = wide[width : width + low].astype(BF)
    grad = (wide[:width] + dot(down[...], grad_inner, TN)).astype(BF).astype(F32)
    gup[...] += 2.0 * dot(inner[0], branch, NT)
    gdown[...] += dot(grad_inner, mixed[0], NT)
    shown = jnp.where(segq[0] == 0, 1.0, 0.0)
    dden[0] = jnp.zeros_like(dden[0])
    pad = jnp.zeros((AUG - head - 1, span), F32)
    for k in range(kv_heads):
        total = None
        for g in range(group):
            h = k * group + g
            at = pl.ds(h * head, head)
            dm = grad[h * head : (h + 1) * head]
            inv = 1.0 / den[0, h : h + 1]
            dd = -jnp.sum(dm * mixed[0, at].astype(F32), axis=0, keepdims=True) * inv
            dn = (dm * inv).astype(BF)
            dnum[0, at] = dn
            dden[0, h : h + 1] = dd
            aug = (jnp.concatenate([dn.astype(F32), dd, pad], axis=0) * shown).astype(BF)
            part = dot(aug, phiq[0, h], NT)
            total = part if total is None else total + part
        dstate[0, k * AUG : (k + 1) * AUG] = total.astype(BF)


def back_kernel(
    kv_heads, group, qkv, tails, phik, phiq, state, dcon, dnum, dden, segq, segk, keep, qmap, kmap,
    dq_out, dkv_out, dtails, gqmap, gkmap, lin_bias, win_bias, between,
):
    head = qmap.shape[1]
    width = dq_out.shape[1]
    span = dq_out.shape[2]
    scale = head**-0.5

    far, near = masks(segq[0], segk[0], span)
    lin_bias[...] = jnp.where(far, 1.0, 0.0)
    win_bias[...] = jnp.where(near, 0.0, -1e30)
    shown = jnp.where(segq[0] == 0, 1.0, 0.0)
    shown3 = jnp.concatenate([shown] * group, axis=1)
    keeping = keep[0]
    pad = jnp.zeros((AUG - head - 1, group * span), F32)
    for k in range(kv_heads):
        at = width + k * head
        key = jnp.concatenate([qkv[0, at : at + head], tails[0, k * head : (k + 1) * head, :WINDOW]], axis=1)
        at += kv_heads * head
        val = jnp.concatenate([qkv[0, at : at + head], tails[0, k * head : (k + 1) * head, WINDOW:]], axis=1)
        hs = range(k * group, (k + 1) * group)
        queries = [qkv[0, h * head : (h + 1) * head] for h in hs]
        query = jnp.concatenate(queries, axis=1) * scale
        feat = jnp.concatenate([phiq[0, h] for h in hs], axis=1)
        dn = jnp.concatenate([dnum[0, h * head : (h + 1) * head] for h in hs], axis=1)
        dd = jnp.concatenate([dden[0, h : h + 1] for h in hs], axis=1)
        kfeat = phik[0, k]
        lb = jnp.concatenate([lin_bias[...]] * group, axis=1)
        wb = jnp.concatenate([win_bias[...]] * group, axis=1)
        growth = jnp.exp(dot(key, query, TN) + wb)
        weights = (dot(kfeat, feat, TN) * lb + growth).astype(BF)
        dw = dot(val, dn, TN) + dd
        dlin = (dw * lb).astype(BF)
        dscore = (dw * growth).astype(BF)
        dv = dot(dn, weights, NT)
        aug = (jnp.concatenate([dn.astype(F32), dd, pad], axis=0) * shown3).astype(BF)
        held = state[0, k * AUG : (k + 1) * AUG]
        dfeat = dot(kfeat, dlin) + dot(held, aug, TN)
        con = dcon[0, k * AUG : (k + 1) * AUG]
        dkfeat = dot(feat, dlin, NT) + dot(con, aug_value(val), TN) * keeping
        dv = dv + dot(con[:head], kfeat * keeping.astype(BF))
        dq = dot(key, dscore) * scale
        dk = dot(query, dscore, NT)
        dt = soft_pair_back(feat, dfeat.astype(BF).astype(F32))
        for g in range(group):
            h = k * group + g
            part = dt[:, g * span : (g + 1) * span]
            gqmap[h] += dot(queries[g], part, NT)
            full = dq[:, g * span : (g + 1) * span] + dot(qmap[h], part)
            dq_out[0, h * head : (h + 1) * head] = full.astype(BF)
        dtk = soft_pair_back(kfeat, dkfeat.astype(BF).astype(F32))
        gkmap[k] += dot(key, dtk, NT)
        dk = dk + dot(kmap[k], dtk)
        ks, vs = k * head, (kv_heads + k) * head
        dkv_out[0, ks : ks + head] = dk[:, :span]
        dkv_out[0, vs : vs + head] = dv[:, :span]
        dtails[0, ks : ks + head] = jnp.concatenate([dk[:, span:], dv[:, span:]], axis=1).astype(BF)
        between(k)


def final_kernel(
    tok, grad_mid, gain, dq, dkv, returned, normed, inner, wq, wkv, down,
    grad_tok, ggain, gdown, gup,
):
    width = tok.shape[1]
    span = tok.shape[2]
    low = down.shape[0]

    got = returned[0].astype(F32)
    got = jnp.concatenate([got[:, :WINDOW], got[:, WINDOW:]], axis=0)
    own = dkv[0]
    both = jnp.concatenate([own[:, : span - WINDOW], own[:, span - WINDOW :] + got], axis=1).astype(BF)
    grad_q = dq[0]
    wide = dot(wq[...], grad_q) + dot(wkv[...], both, TN)
    grad_inner = wide[width : width + low].astype(BF)
    back = wide[:width] + dot(down[...], grad_inner, TN)
    gdown[...] += dot(grad_inner, normed[0], NT)
    gup[:, :width] += 2.0 * dot(inner[0], grad_q, NT)
    gup[:, width:] += 2.0 * dot(inner[0], both, NT)
    value = tok[0].astype(F32)
    scale = rms(value)
    unit = value * scale
    grad_unit = back * gain[...]
    ggain[...] += row_sum(back * unit)
    grad_tok[0] = grad_mid[0] + scale * (
        grad_unit - unit * jnp.mean(grad_unit * unit, axis=0, keepdims=True)
    )


def backward_kernel(
    rows, kv_heads, group, tiles, shard_rows, layout,
    kept, grad_mid_p, mixed, den, phiq_p, segq_p, inner_o, wo, odown,
    qkv, tails, phik, phiq, state, segq, segk, keep, qmap, kmap,
    tok, grad_mid, gain, normed, inner, wq, wkv, down, gpost, shards,
    grad_tok, whole, small_out,
    dnum, dden, dq, dkv, dtails, returned, gup_o, gdown_o, gqmap, gkmap, ggain, gdown, gup, lin_bias, win_bias,
    tail_sem, small_shard, small, *refs,
):
    step = pl.program_id(0)
    place = Place()
    chain = Chain(place, True, kept, *refs[:9])
    refs = refs[9:]
    n_gather = len(gather_scratch(shard_rows, tiles))
    gather = Gather(place, shard_rows, shards, whole, refs[:n_gather])
    refs = refs[n_gather:]
    n_small = len(gather_scratch(layout.rows, 1))
    small_gather = Gather(place, layout.rows, small_shard, small, refs[:n_small])
    small_scatter = Scatter(place, layout.rows, refs[n_small:], 1)

    def row(ref, r):
        return ref.at[pl.ds(r, 1)]

    def tail_copy(r):
        return remote(dtails.at[r], returned.at[r], tail_sem.at[0, r], tail_sem.at[1, r], place.along(-1))

    @pl.when(step == 0)
    def _():
        place.greet()
        for ref in (gup_o, gdown_o, gqmap, gkmap, ggain, gdown, gup):
            ref[...] = jnp.zeros_like(ref)

        @pl.when(jnp.logical_not(place.inside(1)))
        def _():
            returned[...] = jnp.zeros_like(returned)

    @pl.when(step < rows)
    def _():
        pull_kernel(
            kv_heads, group, grad_mid_p, mixed, den, phiq_p, segq_p, inner_o, wo, odown,
            row(dnum, step), row(dden, step), row(chain.own, step), gup_o, gdown_o,
        )

    @pl.when((step >= rows) & (step < 2 * rows))
    def _():
        r = step - rows

        def between(k):
            if k == kv_heads // 2:
                gather.turn(2 * r, tiles)

        back_kernel(
            kv_heads, group, qkv, tails, phik, phiq, state, row(chain.result, r), row(dnum, r), row(dden, r),
            segq, segk, keep, qmap, kmap,
            row(dq, r), row(dkv, r), row(dtails, r), gqmap, gkmap, lin_bias, win_bias, between,
        )

        @pl.when(place.inside(-1))
        def _():
            tail_copy(r).start()

    @pl.when(step >= 2 * rows)
    def _():
        r = step - 2 * rows

        @pl.when(place.inside(1))
        def _():
            tail_copy(r).wait_recv()

        final_kernel(
            tok, grad_mid, gain, row(dq, r), row(dkv, r), row(returned, r), normed, inner, wq, wkv, down,
            grad_tok, ggain, gdown, gup,
        )

    chain.turn(step, rows)

    @pl.when(step >= rows)
    def _():
        gather.turn(jnp.where(step < 2 * rows, 2 * (step - rows) + 1, step), tiles)

    @pl.when(step == 3 * rows - 1)
    def _():
        chain.close(rows)

        @pl.when(place.inside(-1))
        def _():
            for r in range(rows):
                tail_copy(r).wait_send()

        rank = gdown_o.shape[0]
        width = gdown_o.shape[1]
        kv_width = kv_heads * qmap.shape[1]
        mine = small_scatter.mine
        mine[...] = jnp.zeros_like(mine)
        pad = [jnp.zeros((6, width), F32)]
        layout.put(mine, "down", jnp.concatenate([gdown[...], ggain[0:1], gpost[0:1]] + pad, axis=0))
        layout.put(mine, "out", jnp.concatenate([gdown_o[...], gup_o[...]], axis=0))
        layout.put(mine, "q_up", jnp.concatenate([gup[0:rank, :width], jnp.zeros((rank, width), F32)], axis=0))
        layout.put(
            mine, "kv_up",
            jnp.concatenate(
                [gup[rank : 2 * rank, width : width + kv_width], gup[2 * rank :, width + kv_width :]], axis=0
            ),
        )
        layout.put_heads(mine, "qmap", gqmap)
        layout.put_heads(mine, "kmap", gkmap)

        def into(stream, total):
            small_shard[0, stream] = total.astype(BF)

        small_scatter.run(into)
        small_gather.run()
        small_out[...] = small[...]
        for turn in range(3 * rows, tiles + WAYS[0]):
            gather.turn(jnp.int32(turn), tiles)


def row_spec(*shape):
    zeros = (0,) * len(shape)
    return pl.BlockSpec((1,) + shape, lambda r: (r,) + zeros)


def whole_spec(*shape):
    zeros = (0,) * len(shape)
    return pl.BlockSpec(shape, lambda r: zeros, pipeline_mode=pl.Buffered(1))


def shape_of(shape, kind):
    return jax.ShapeDtypeStruct(shape, kind)


def row_call(kernel, rows, args, outs, scratch=()):
    in_specs = [row_spec(*a.shape[1:]) if by_row else whole_spec(*a.shape) for a, by_row in args]
    out_specs = tuple(row_spec(*s[1:]) if by_row else pl.BlockSpec(s, functools.partial(lambda n, r: (0,) * n, len(s))) for s, _, by_row in outs)
    return pl.pallas_call(
        kernel,
        grid=(rows,),
        in_specs=in_specs,
        out_specs=out_specs,
        out_shape=tuple(shape_of(s, kind) for s, kind, _ in outs),
        scratch_shapes=list(scratch),
        compiler_params=pltpu.CompilerParams(vmem_limit_bytes=VMEM),
    )(*[a for a, _ in args])


def shifted(array, route):
    return lax.ppermute(array, "seq", route)


def fold(parts, keeps):
    total = None
    for part, keep in zip(parts, keeps):
        total = part if total is None else part + keep[:, None, None] * total
    return total


def carried_states(own, kept, index, count, reverse):
    hi, lo, n_hi, n_lo = split_seq(index, count)
    step = -1 if reverse else 1
    ranks = range(count)

    def keep_of(at):
        return lax.dynamic_slice_in_dim(kept, at, 1, 1)[:, 0]

    around = [own]
    for d in range(1, n_lo):
        route = [(i, i // n_lo * n_lo + (i % n_lo + d) % n_lo) for i in ranks]
        around.append(shifted(own, route))
    around = jnp.stack(around).astype(F32)
    order = list(range(n_lo))[::step]
    total = jnp.zeros_like(around[0])
    before = jnp.zeros_like(around[0])
    keep_all = jnp.ones_like(kept[:, 0])
    keep_before = keep_all
    for pos in order:
        here = lo == pos
        before = jnp.where(here, total, before)
        keep_before = jnp.where(here, keep_all, keep_before)
        part = lax.dynamic_index_in_dim(around, (lo - pos) % n_lo, 0, False)
        keep = keep_of(hi * n_lo + pos)
        total = part + keep[:, None, None] * total
        keep_all = keep * keep_all
    entering = jnp.zeros_like(total)
    for hop in range(n_hi - 1):
        leaving = (total + keep_all[:, None, None] * entering).astype(BF)
        route = [(i, i + step * n_lo) for i in ranks if 0 <= i + step * n_lo < count]
        got = shifted(leaving, route).astype(F32)
        at = n_hi - 2 - hop if reverse else hop + 1
        entering = jnp.where(hi == at, got, entering)
    return (before + keep_before[:, None, None] * entering).astype(BF)


def frames(doc_starts, index, count, span):
    rows = doc_starts.shape[0]
    padded = jnp.concatenate([jnp.zeros((rows, WINDOW), jnp.int32), doc_starts], axis=1)
    kept = jnp.sum(padded[:, : count * span].reshape(rows, count, span), axis=2) == 0
    marks = lax.dynamic_slice_in_dim(padded, index * span, span + WINDOW, 1)
    segment = jnp.cumsum(marks, axis=1)
    own, tail = segment[:, WINDOW:], segment[:, :WINDOW]
    last = own[:, span - WINDOW - 1 : span - WINDOW]
    keys = jnp.concatenate([own, tail], axis=1)
    valid = jnp.concatenate([jnp.arange(span) < span - WINDOW, jnp.full((WINDOW,), True)])
    keep = ((keys == last) & valid[None]).astype(F32)
    return kept.astype(F32), own[:, None, :], keys[:, :, None], keep[:, None, :]


def body(
    tokens, doc_starts, pregain, query_base, key_base, value_base, output_base, query_down, query_up,
    key_down, key_up, value_down, value_up, out_down, out_up, query_map, key_map, postgain, gate_proj,
    up_proj, down_proj, cotangent,
):
    rows, span, width = tokens.shape
    heads, head, _ = query_map.shape
    kv_heads = key_map.shape[0]
    group = heads // kv_heads
    kv_width = kv_heads * head
    rank = query_up.shape[0]
    extent = span + WINDOW
    hidden = gate_proj.shape[1]
    tiles = hidden // TILE
    high = -(-width // 256) * 256
    feats = 2 * head
    slots = -(-heads // 8) * 8
    count = lax.axis_size("seq")
    index = lax.axis_index("seq")

    tok = jnp.swapaxes(tokens, 1, 2)
    cot = jnp.swapaxes(cotangent, 1, 2)
    gain_one = pregain.astype(F32)[:, None]
    gain_two = postgain.astype(F32)[:, None]
    kept, segq, segk, keep = frames(doc_starts, index, count, span)

    zeros = functools.partial(jnp.zeros, dtype=BF)
    wq = jnp.concatenate([query_base, 2 * query_up, zeros((high - width - rank, width))], axis=0)
    kup = jnp.concatenate([zeros((kv_width, rank)), 2 * key_up.T, zeros((kv_width, high - width - 2 * rank))], axis=1)
    vup = jnp.concatenate([zeros((kv_width, 2 * rank)), 2 * value_up.T, zeros((kv_width, high - width - 3 * rank))], axis=1)
    wkv = jnp.concatenate(
        [jnp.concatenate([key_base.T, value_base.T], axis=0), jnp.concatenate([kup, vup], axis=0)], axis=1
    )
    wo = jnp.concatenate([output_base, 2 * out_up, zeros((high - width - rank, width))], axis=0)
    down = jnp.concatenate([query_down.T, key_down.T, value_down.T], axis=0)
    odown = out_down.T

    ext = pltpu.VMEM((high, span), BF)
    biases = [pltpu.VMEM((extent, span), F32)] * 2
    qkv, normed, inner, tails = row_call(
        qkv_kernel,
        rows,
        [(tok, 1), (gain_one, 0), (wq, 0), (wkv, 0), (down, 0)],
        [
            ((rows, width + 2 * kv_width, span), BF, 1),
            ((rows, width, span), BF, 1),
            ((rows, 3 * rank, span), BF, 1),
            ((rows, kv_width, 2 * WINDOW), BF, 1),
        ],
        [ext],
    )
    tails = shifted(tails, [(i, i + 1) for i in range(count - 1)])
    phik, con = row_call(
        functools.partial(key_kernel, kv_heads),
        rows,
        [(qkv, 1), (tails, 1), (key_map, 0), (keep, 1)],
        [((rows, kv_heads, feats, extent), BF, 1), ((rows, kv_heads * AUG, feats), BF, 1)],
    )
    state = carried_states(con, kept, index, count, False)
    mixed, den, phiq, middle, normed2, inner_o = row_call(
        functools.partial(attend_kernel, kv_heads, group),
        rows,
        [
            (qkv, 1), (tails, 1), (phik, 1), (state, 1), (segq, 1), (segk, 1), (query_map, 0), (tok, 1),
            (wo, 0), (odown, 0), (gain_two, 0),
        ],
        [
            ((rows, width, span), BF, 1),
            ((rows, slots, span), F32, 1),
            ((rows, heads, feats, span), BF, 1),
            ((rows, width, span), F32, 1),
            ((rows, width, span), BF, 1),
            ((rows, rank, span), BF, 1),
        ],
        [ext] + biases,
    )

    last = lambda s: (jnp.maximum(s - tiles, 0), 0, 0)
    fixed = lambda s: (0, 0)
    anywhere = pl.BlockSpec(memory_space=pl.ANY)
    streams = stream_plan(3 * high)
    shard_shape = (tiles, len(streams), streams[0][2][-1][1], 128)
    layer_out, grad_mid, gpost, shards = pl.pallas_call(
        functools.partial(ff_kernel, width),
        grid=(tiles + rows,),
        in_specs=[anywhere, anywhere, pl.BlockSpec((1, width, span), last), pl.BlockSpec((width, 1), fixed)]
        + [anywhere] * 3,
        out_specs=(
            pl.BlockSpec((1, width, span), last),
            pl.BlockSpec((1, width, span), last),
            pl.BlockSpec((8, width), fixed),
            pl.BlockSpec(shard_shape, lambda s: (0, 0, 0, 0)),
        ),
        out_shape=(
            shape_of((rows, width, span), BF),
            shape_of((rows, width, span), F32),
            shape_of((8, width), F32),
            shape_of(shard_shape, BF),
        ),
        scratch_shapes=[pltpu.VMEM((high, rows * span), BF)] * 2
        + [pltpu.VMEM((high, hidden), BF)] * 3
        + [pltpu.VMEM((hidden, rows * span), BF)] * 3
        + [pltpu.SemaphoreType.DMA((tiles, 3)), pltpu.SemaphoreType.DMA((rows, 2))]
        + scatter_scratch(3 * high, BF),
        compiler_params=pltpu.CompilerParams(vmem_limit_bytes=VMEM, collective_id=0, has_side_effects=True),
    )(normed2, cot, middle, gain_two, gate_proj, up_proj, down_proj.T)

    layout = Small(rank, width, kv_width, heads, kv_heads, head)
    args, specs = [kept], [pl.BlockSpec(memory_space=pltpu.SMEM)]
    for phase, arrays in enumerate(
        (
            (grad_mid, mixed, den, phiq, segq, inner_o),
            (qkv, tails, phik, phiq, state, segq, segk, keep),
            (tok, grad_mid, normed, inner),
        )
    ):
        def at(s, *, phase=phase, n=0):
            return (jnp.clip(s - phase * rows, 0, rows - 1),) + (0,) * n

        for array in arrays:
            args.append(array)
            specs.append(
                pl.BlockSpec((1,) + array.shape[1:], functools.partial(at, n=array.ndim - 1))
            )
        fixed_args = ((wo, odown), (query_map, key_map), (wq, wkv, down, gpost))[phase]
        if phase == 2:
            args.insert(len(args) - 2, gain_one)
            specs.insert(len(specs) - 2, whole_spec(*gain_one.shape))
        for array in fixed_args:
            args.append(array)
            specs.append(whole_spec(*array.shape))
    args.append(shards)
    specs.append(anywhere)
    last = lambda s: (jnp.maximum(s - 2 * rows, 0), 0, 0)
    small_streams = stream_plan(layout.rows)
    grad_tok, whole, small = pl.pallas_call(
        functools.partial(backward_kernel, rows, kv_heads, group, tiles, 3 * high, layout),
        grid=(3 * rows,),
        in_specs=specs,
        out_specs=(
            pl.BlockSpec((1, width, span), last),
            anywhere,
            pl.BlockSpec((1, 2, layout.rows, 128), lambda s: (0, 0, 0, 0)),
        ),
        out_shape=(
            shape_of((rows, width, span), F32),
            shape_of((tiles, 2, 3 * high, 128), BF),
            shape_of((1, 2, layout.rows, 128), BF),
        ),
        scratch_shapes=[
            pltpu.VMEM((rows, width, span), BF),
            pltpu.VMEM((rows, slots, span), F32),
            pltpu.VMEM((rows, width, span), BF),
            pltpu.VMEM((rows, 2 * kv_width, span), F32),
            pltpu.VMEM((rows, kv_width, 2 * WINDOW), BF),
            pltpu.VMEM((rows, kv_width, 2 * WINDOW), BF),
            pltpu.VMEM((rank, width), F32),
            pltpu.VMEM((rank, width), F32),
            pltpu.VMEM((heads, head, head), F32),
            pltpu.VMEM((kv_heads, head, head), F32),
            pltpu.VMEM((8, width), F32),
            pltpu.VMEM((3 * rank, width), F32),
            pltpu.VMEM((3 * rank, width + 2 * kv_width), F32),
        ]
        + biases
        + [
            pltpu.SemaphoreType.DMA((2, rows)),
            pltpu.VMEM((1, len(small_streams), small_streams[0][2][-1][1], 128), BF),
            pltpu.VMEM((1, 2, layout.rows, 128), BF),
        ]
        + chain_scratch(rows, kv_heads * AUG, feats)
        + gather_scratch(3 * high, tiles)
        + gather_scratch(layout.rows, 1)
        + scatter_scratch(layout.rows, BF, 1),
        compiler_params=pltpu.CompilerParams(vmem_limit_bytes=VMEM, collective_id=1, has_side_effects=True),
    )(*args)

    column = pl.BlockSpec((width, 128), lambda j: (0, j))
    flat = [(1, width)] * 2 + [(rank, width)] * 4 + [(rank, kv_width)] * 2 + [(rank, width)] * 2
    flat += [query_map.shape, key_map.shape]
    outs = pl.pallas_call(
        functools.partial(widen_kernel, width, high, rank, layout),
        grid=(2 * tiles,),
        in_specs=[
            pl.BlockSpec((1, 1, 3 * high, 128), lambda j: (j // 2, j % 2, 0, 0)),
            pl.BlockSpec((1, 2, layout.rows, 128), lambda j: (0, 0, 0, 0)),
        ],
        out_specs=(column,) * 3 + tuple(pl.BlockSpec(f, functools.partial(lambda n, j: (0,) * n, len(f))) for f in flat),
        out_shape=(shape_of((width, hidden), F32),) * 3 + tuple(shape_of(f, F32) for f in flat),
        compiler_params=pltpu.CompilerParams(vmem_limit_bytes=VMEM),
    )(whole, small)
    gate, up, down_t, pre, post, qd, kd, vd, qu, ku, vu, od, ou, gq, gk = outs
    return (
        jnp.swapaxes(layer_out, 1, 2),
        jnp.swapaxes(grad_tok, 1, 2),
        pre[0],
        qd.T,
        qu,
        kd.T,
        ku,
        vd.T,
        vu,
        od.T,
        ou,
        gq,
        gk,
        post[0],
        gate,
        up,
        down_t.T,
    )


def solution(mesh):
    wide = P("batch", "seq", None)
    return jax.shard_map(
        body,
        mesh=mesh,
        in_specs=(wide, P("batch", None)) + (P(),) * 19 + (wide,),
        out_specs=(wide, wide) + (P(),) * 15,
        check_vma=False,
    )
```

```python
import functools

import jax
import jax.numpy as jnp
from jax import lax
from jax.experimental import pallas as pl
from jax.experimental.pallas import tpu as pltpu
from jax.sharding import PartitionSpec as P

WINDOW = 64
EPSILON = 1e-05
BF = jnp.bfloat16
F32 = jnp.float32
NN = (((1,), (0,)), ((), ()))
NT = (((1,), (1,)), ((), ()))
TN = (((0,), (0,)), ((), ()))
HI = 4
TILE = 256
AUG = 80
VMEM = 62 << 20
MESH = pl.DeviceIdType.MESH


def dot(left, right, dims=NN):
    return lax.dot_general(left, right, dims, preferred_element_type=F32)


def split_seq(index, count):
    low = max(count // HI, 1)
    return index // low, index % low, count // low, low


class Place:
    def __init__(self):
        batch, seq = lax.axis_index("batch"), lax.axis_index("seq")
        n_seq = lax.axis_size("seq")
        hi, lo, n_hi, n_lo = split_seq(seq, n_seq)
        self.batch, self.seq = batch, seq
        self.at = {"core": batch % 2, "y": batch // 2, "hi": hi, "lo": lo}
        self.size = axis_sizes()

    def peer(self, axis, distance):
        at = dict(self.at)
        at[axis] = (at[axis] + distance) % self.size[axis]
        return (at["y"] * 2 + at["core"], at["hi"] * self.size["lo"] + at["lo"])

    def along(self, distance):
        return (self.batch, self.seq + distance)

    def inside(self, distance):
        return (self.seq + distance >= 0) & (self.seq + distance < self.size["hi"] * self.size["lo"])

    def greet(self):
        barrier = pltpu.get_barrier_semaphore()
        total = 0
        for d in (-1, 1):

            @pl.when(self.inside(d))
            def _():
                pl.semaphore_signal(barrier, inc=1, device_id=self.along(d), device_id_type=MESH)

            total = total + jnp.where(self.inside(d), 1, 0)
        for axis, size in self.size.items():
            for d in range(1, size):
                pl.semaphore_signal(barrier, inc=1, device_id=self.peer(axis, d), device_id_type=MESH)
                total = total + 1
        pl.semaphore_wait(barrier, total)


def axis_sizes():
    _, _, n_hi, n_lo = split_seq(0, lax.axis_size("seq"))
    return {"core": 2, "y": lax.axis_size("batch") // 2, "hi": n_hi, "lo": n_lo}


def stream_plan(rows):
    size = axis_sizes()
    orders = [("lo", "y", "hi"), ("y", "lo", "hi")]
    devices = size["lo"] * size["y"] * size["hi"]
    if rows // (2 * devices) % 16:
        orders = orders[:1]
    part = rows // len(orders)
    plan = []
    for i, order in enumerate(orders):
        left, stages = part, []
        for axis in order:
            left = left // size[axis]
            stages.append((axis, left))
        plan.append((i * part, part, stages))
    return plan


def remote(src, dst, send, recv, peer):
    return pltpu.make_async_remote_copy(
        src_ref=src, dst_ref=dst, send_sem=send, recv_sem=recv, device_id=peer, device_id_type=MESH
    )


LAGS = (1, 3, 4, 5)


def stage_slots(k, slots):
    return 2 * slots if k == 1 else slots


def scatter_scratch(rows, kind, slots=2):
    size = axis_sizes()
    made = [
        pltpu.VMEM((slots, 2, rows, 128), kind),
        pltpu.VMEM((slots, rows, 128), kind),
        pltpu.VMEM((stage_slots(1, slots), rows, 128), kind),
        pltpu.SemaphoreType.DMA((2, slots)),
    ]
    for _, _, stages in stream_plan(rows):
        for k, (axis, left) in enumerate(stages, 1):
            peers = max(size[axis] - 1, 1)
            made.append(pltpu.VMEM((stage_slots(k, slots), peers, left, 128), kind))
            made.append(pltpu.VMEM((slots, left, 128), kind))
            made.append(pltpu.SemaphoreType.DMA((2, stage_slots(k, slots), peers)))
    return made


class Scatter:
    def __init__(self, place, rows, refs, slots=2):
        self.place, self.rows, self.slots = place, rows, slots
        self.mine, self.other, self.base, self.core_sem = refs[:4]
        self.streams = []
        at = 4
        for first, part, stages in stream_plan(rows):
            made = []
            for axis, left in stages:
                made.append((axis, left) + tuple(refs[at : at + 3]))
                at += 3
            self.streams.append((first, part, made))

    def core_copy(self, t):
        slot = t % self.slots
        core = self.place.at["core"]
        return remote(
            self.mine.at[slot, 1 - core], self.other.at[slot],
            self.core_sem.at[0, slot], self.core_sem.at[1, slot], self.place.peer("core", 1),
        )

    def copies(self, k, t):
        slot = t % stage_slots(k, self.slots)
        made = []
        for first, part, stages in self.streams:
            axis, left, got, _, sem = stages[k - 1]
            size = self.place.size[axis]
            for d in range(1, size):
                to = (self.place.at[axis] + d) % size
                if k == 1:
                    src = self.base.at[slot, pl.ds(pl.multiple_of(first + to * left, 16), left)]
                else:
                    src = stages[k - 2][3].at[t % self.slots, pl.ds(pl.multiple_of(to * left, 16), left)]
                made.append(
                    remote(
                        src, got.at[slot, d - 1], sem.at[0, slot, d - 1], sem.at[1, slot, d - 1],
                        self.place.peer(axis, d),
                    )
                )
        return made

    def start(self, k, t):
        for copy in [self.core_copy(t)] if k == 0 else self.copies(k, t):
            copy.start()

    def finish(self, k, t, into=None):
        slot = t % self.slots
        ahead = t % stage_slots(k, self.slots)
        if k == 0:
            self.core_copy(t).wait()
            core = self.place.at["core"]
            self.base[t % stage_slots(1, self.slots)] = (self.mine[slot, core].astype(F32) + self.other[slot].astype(F32)).astype(self.base.dtype)
            return
        for copy in self.copies(k, t):
            copy.wait()
        for i, (first, part, stages) in enumerate(self.streams):
            axis, left, got, out, _ = stages[k - 1]
            at = self.place.at[axis] * left
            if k == 1:
                own = self.base[ahead, pl.ds(pl.multiple_of(first + at, 16), left)]
            else:
                own = stages[k - 2][3][slot, pl.ds(pl.multiple_of(at, 16), left)]
            total = own.astype(F32)
            for d in range(1, self.place.size[axis]):
                total = total + got[ahead, d - 1].astype(F32)
            if k == 3:
                into(i, total)
            else:
                out[slot] = total.astype(out.dtype)

    def run(self, into):
        self.start(0, 0)
        for k in range(4):
            self.finish(k, 0, into)
            if k < 3:
                self.start(k + 1, 0)

    def turn(self, step, tiles, into):
        for k in (3, 2, 1, 0):
            t = step - LAGS[k]

            @pl.when((t >= 0) & (t < tiles))
            def _():
                self.finish(k, t, functools.partial(into, t))
                if k < 3:
                    self.start(k + 1, t)

        @pl.when(step < tiles)
        def _():
            self.start(0, step)


WAYS = (6, 5, 3, 1)


def gather_scratch(rows, tiles):
    size = axis_sizes()
    made = [pltpu.SemaphoreType.DMA((2, tiles)), pltpu.SemaphoreType.DMA((tiles, len(stream_plan(rows))))]
    for _, _, stages in stream_plan(rows):
        for axis, left in stages:
            made.append(pltpu.SemaphoreType.DMA((2, tiles, max(size[axis] - 1, 1))))
    return made


class Gather:
    def __init__(self, place, rows, shards, whole, refs):
        self.place, self.rows, self.shards, self.whole = place, rows, shards, whole
        self.core_sem, self.own_sem = refs[:2]
        self.streams = []
        at = 2
        for first, part, stages in stream_plan(rows):
            self.streams.append((first, part, [st + (refs[at + i],) for i, st in enumerate(stages)]))
            at += len(stages)

    def region(self, t, stream, k):
        first, _, stages = self.streams[stream]
        at = first
        for axis, left, _ in stages[:k]:
            at = at + self.place.at[axis] * left
        return self.whole.at[t, self.place.at["core"], pl.ds(pl.multiple_of(at, 16), stages[k - 1][1])]

    def own_copies(self, t):
        return [
            pltpu.make_async_copy(self.shards.at[t, i], self.region(t, i, 3), self.own_sem.at[t, i])
            for i in range(len(self.streams))
        ]

    def copies(self, k, t):
        if k == 0:
            half = self.whole.at[t, self.place.at["core"]]
            return [remote(half, half, self.core_sem.at[0, t], self.core_sem.at[1, t], self.place.peer("core", 1))]
        made = []
        for i, (_, _, stages) in enumerate(self.streams):
            axis, left, sem = stages[k - 1]
            dst = self.region(t, i, k)
            src = self.shards.at[t, i] if k == 3 else dst
            for d in range(1, self.place.size[axis]):
                made.append(remote(src, dst, sem.at[0, t, d - 1], sem.at[1, t, d - 1], self.place.peer(axis, d)))
        return made

    def run(self):
        for copy in self.own_copies(0) + self.copies(3, 0):
            copy.start()
        for k in (3, 2, 1, 0):
            for copy in self.copies(k, 0) + (self.own_copies(0) if k == 3 else []):
                copy.wait()
            if k > 0:
                for copy in self.copies(k - 1, 0):
                    copy.start()

    def turn(self, step, tiles):
        for k in (0, 1, 2, 3):
            t = step - WAYS[k]

            @pl.when((t >= 0) & (t < tiles))
            def _():
                for copy in self.copies(k, t):
                    copy.wait()
                if k == 3:
                    for copy in self.own_copies(t):
                        copy.wait()
                if k > 0:
                    for copy in self.copies(k - 1, t):
                        copy.start()

        @pl.when(step < tiles)
        def _():
            for copy in self.own_copies(step) + self.copies(3, step):
                copy.start()


class Chain:
    def __init__(self, place, reverse, lag, kept, own, around, total, before, leaving, entering, result, lo_sem, hi_sem):
        self.place, self.reverse, self.lag, self.kept = place, reverse, lag, kept
        self.own, self.around, self.total, self.before = own, around, total, before
        self.leaving, self.entering, self.result = leaving, entering, result
        self.lo_sem, self.hi_sem = lo_sem, hi_sem
        self.n_hi, self.n_lo = place.size["hi"], place.size["lo"]
        hi = place.at["hi"]
        self.rank = self.n_hi - 1 - hi if reverse else hi

    def lo_copies(self, r):
        return [
            remote(
                self.own.at[r], self.around.at[d - 1, r], self.lo_sem.at[0, r, d - 1], self.lo_sem.at[1, r, d - 1],
                self.place.peer("lo", d),
            )
            for d in range(1, self.n_lo)
        ]

    def hi_copy(self, r):
        return remote(
            self.leaving.at[r], self.entering.at[r], self.hi_sem.at[0, r], self.hi_sem.at[1, r],
            self.place.peer("hi", -1 if self.reverse else 1),
        )

    def keep(self, r, pos):
        flags = self.kept[pl.ds(r, 1), :]
        here = lax.broadcasted_iota(jnp.int32, flags.shape, 1) == self.place.at["hi"] * self.n_lo + pos
        return jnp.sum(jnp.where(here, flags, 0.0), axis=1, keepdims=True)

    def order(self):
        return list(range(self.n_lo))[:: -1 if self.reverse else 1]

    def begin(self, r):
        for copy in self.lo_copies(r):
            copy.start()

    def leave(self, r, value):
        @pl.when(self.rank < self.n_hi - 1)
        def _():
            self.leaving[r] = value.astype(BF)
            self.hi_copy(r).start()

    def join(self, r):
        for copy in self.lo_copies(r):
            copy.wait()
        lo = self.place.at["lo"]
        total = jnp.zeros(self.own.shape[1:], F32)
        before = total
        for pos in self.order():
            part = self.own[r].astype(F32)
            before = jnp.where(lo == pos, total, before)
            for d in range(1, self.n_lo):
                part = jnp.where((lo - pos) % self.n_lo == d, self.around[d - 1, r].astype(F32), part)
            total = part + self.keep(r, pos) * total
        self.total[r] = total
        self.before[r] = before

        @pl.when(self.rank == 0)
        def _():
            self.leave(r, total)
            self.result[r] = before.astype(BF)

    def hop(self, r):
        self.hi_copy(r).wait_recv()
        entering = self.entering[r].astype(F32)
        lo = self.place.at["lo"]
        keep_all = keep_before = jnp.ones((1, 1), F32)
        for pos in self.order():
            keep_before = jnp.where(lo == pos, keep_all, keep_before)
            keep_all = keep_all * self.keep(r, pos)
        self.leave(r, self.total[r] + keep_all * entering)
        self.result[r] = (self.before[r] + keep_before * entering).astype(BF)

    def turn(self, step, rows, starts=True):
        for q in range(self.n_hi - 1, 0, -1):
            r = step - self.lag * (1 + q)

            @pl.when((r >= 0) & (r < rows) & (self.rank == q))
            def _():
                self.hop(r)

        r = step - self.lag

        @pl.when((r >= 0) & (r < rows))
        def _():
            self.join(r)

        if starts:

            @pl.when(step < rows)
            def _():
                self.begin(step)

    def close(self, rows):
        @pl.when(self.rank < self.n_hi - 1)
        def _():
            for r in range(rows):
                self.hi_copy(r).wait_send()


def chain_scratch(rows, height, feats):
    size = axis_sizes()
    peers = max(size["lo"] - 1, 1)
    shape = (rows, height, feats)
    return [
        pltpu.VMEM(shape, BF),
        pltpu.VMEM((peers,) + shape, BF),
        pltpu.VMEM(shape, F32),
        pltpu.VMEM(shape, F32),
        pltpu.VMEM(shape, BF),
        pltpu.VMEM(shape, BF),
        pltpu.VMEM(shape, BF),
        pltpu.SemaphoreType.DMA((2, rows, peers)),
        pltpu.SemaphoreType.DMA((2, rows)),
    ]


class Small:
    def __init__(self, rank, width, kv_width, heads, kv_heads, head):
        def chunks(lanes):
            return -(-lanes // 128)

        tall = -(-(3 * rank + 2) // 16) * 16
        flat = -(-2 * rank // 16) * 16
        sections = [
            ("down", tall, chunks(width)),
            ("out", flat, chunks(width)),
            ("q_up", -(-rank // 16) * 16, chunks(width)),
            ("kv_up", -(-2 * rank // 16) * 16, chunks(kv_width)),
            ("qmap", head, (heads + 1) // 2),
            ("kmap", head, (kv_heads + 1) // 2),
        ]
        need = sum(rows * n for _, rows, n in sections)
        size = axis_sizes()
        grain = 16 * size["lo"] * size["y"] * size["hi"]
        self.rows = -(-(need + 64) // (2 * grain)) * grain
        self.place = {}
        half, at = 0, 0
        for name, rows, n in sections:
            self.place[name] = []
            for _ in range(n):
                if at + rows > self.rows:
                    half, at = half + 1, 0
                self.place[name].append((half, at, rows))
                at += rows

    def put(self, ref, name, value):
        for c, (half, at, rows) in enumerate(self.place[name]):
            part = value[:, c * 128 : (c + 1) * 128]
            ref[0, half, at : at + part.shape[0], 0 : part.shape[1]] = part.astype(ref.dtype)

    def put_heads(self, ref, name, maps):
        for c, (half, at, rows) in enumerate(self.place[name]):
            pair = [maps[h] for h in range(2 * c, min(2 * c + 2, maps.shape[0]))]
            pair = jnp.concatenate(pair, axis=1) if len(pair) > 1 else pair[0]
            ref[0, half, at : at + rows, 0 : pair.shape[1]] = pair.astype(ref.dtype)

    def take(self, ref, name, lanes):
        parts = [ref[0, half, at : at + rows].astype(F32) for half, at, rows in self.place[name]]
        return jnp.concatenate(parts, axis=1)[:, :lanes]


def widen_kernel(width, high, rank, layout, whole, small, out_in, tok_in, out_out, tok_out, gate, up, down, *outs):
    out_out[...] = out_in[...]
    tok_out[...] = tok_in[...]
    for i, out in enumerate((gate, up, down)):
        for half in range(2):
            out[:, half * 128 : (half + 1) * 128] = whole[0, half, i * high : i * high + width].astype(F32)

    @pl.when(pl.program_id(0) == 0)
    def _():
        pre, post, qd, kd, vd, qu, ku, vu, od, ou, qmap, kmap = outs
        downs = layout.take(small, "down", width)
        for i, out in enumerate((qd, kd, vd)):
            out[...] = downs[i * rank : (i + 1) * rank]
        pre[...] = downs[3 * rank : 3 * rank + 1]
        post[...] = downs[3 * rank + 1 : 3 * rank + 2]
        pair = layout.take(small, "out", width)
        od[...] = pair[:rank]
        ou[...] = pair[rank : 2 * rank]
        qu[...] = layout.take(small, "q_up", width)[:rank]
        pair = layout.take(small, "kv_up", ku.shape[1])
        ku[...] = pair[:rank]
        vu[...] = pair[rank : 2 * rank]
        head = qmap.shape[1]
        for name, out in (("qmap", qmap), ("kmap", kmap)):
            for h in range(out.shape[0]):
                half, at, rows = layout.place[name][h // 2]
                both = small[0, half, at : at + rows].astype(F32)
                out[h] = both[:, (h % 2) * head : (h % 2 + 1) * head]


def row_sum(value):
    return dot(jnp.ones((8, value.shape[1]), BF), value.astype(BF), NT)


def rms(value):
    return lax.rsqrt(jnp.mean(value * value, axis=0, keepdims=True) + EPSILON)


def soft_pair(logit):
    top = jnp.max(logit, axis=0, keepdims=True)
    low = jnp.min(logit, axis=0, keepdims=True)
    up = jnp.exp(logit - top)
    down = jnp.exp(low - logit)
    up = up / jnp.sum(up, axis=0, keepdims=True)
    down = down / jnp.sum(down, axis=0, keepdims=True)
    return jnp.concatenate([up, down], axis=0).astype(BF)


def soft_pair_back(phi, grad):
    half = phi.shape[0] // 2
    up, down = phi[:half].astype(F32), phi[half:].astype(F32)
    gu, gd = grad[:half], grad[half:]
    gu = up * (gu - jnp.sum(up * gu, axis=0, keepdims=True))
    gd = down * (gd - jnp.sum(down * gd, axis=0, keepdims=True))
    return (gu - gd).astype(BF)


def frame(place, span, doc, seg, kept):
    rows, length = doc.shape
    index = place.seq
    high = seg.shape[0]
    more = jnp.zeros((high - rows, span), F32)
    own = doc[:, pl.ds(pl.multiple_of(index * span, span), span)].astype(F32)
    prev = doc[:, pl.ds(pl.multiple_of(jnp.maximum(index - 1, 0) * span, span), span)].astype(F32)
    lane = lax.broadcasted_iota(jnp.int32, (rows, span), 1)
    prev = jnp.where((lane >= span - WINDOW) & (index > 0), prev, 0.0)
    upper = lax.broadcasted_iota(jnp.int32, (span, span), 0) <= lax.broadcasted_iota(jnp.int32, (span, span), 1)
    upper = jnp.where(upper, 1.0, 0.0).astype(BF)
    before = jnp.concatenate([prev, more], axis=0)
    tail = dot(before.astype(BF), upper)
    mine = dot(jnp.concatenate([own, more], axis=0).astype(BF), upper) + jnp.sum(before, axis=1, keepdims=True)
    seg[:, :span] = mine
    seg[:, span:] = tail[:, span - WINDOW :]
    total = jnp.zeros(kept.shape, F32)
    for b in range(length // span):
        at = lax.broadcasted_iota(jnp.int32, (span, 128), 0)
        block = lax.broadcasted_iota(jnp.int32, (span, 128), 1)
        here = jnp.where(at < span - WINDOW, b, b + 1) == block
        marks = jnp.concatenate([doc[:, b * span : (b + 1) * span].astype(F32), more], axis=0)
        total = total + dot(marks.astype(BF), jnp.where(here, 1.0, 0.0).astype(BF))
    kept[...] = jnp.where(total == 0, 1.0, 0.0)


def frame_row(seg, r, span):
    keys = seg[pl.ds(r, 1), :]
    query = keys[:, :span]
    column = jnp.broadcast_to(keys, (8, keys.shape[1])).T[:, :1]
    lane = lax.broadcasted_iota(jnp.int32, keys.shape, 1)
    last = jnp.sum(jnp.where(lane == span - WINDOW - 1, keys, 0.0), axis=1, keepdims=True)
    keep = (keys == last) & ((lane < span - WINDOW) | (lane >= span))
    return query, column, jnp.where(keep, 1.0, 0.0)


def assemble(width, bases, gains, wq, wkv, wo, down, columns):
    qb, kb, vb, ob, qu, ku, vu, ou, qd, kd, vd = bases
    rank = qu.shape[0]
    high = wq.shape[0]
    extra = high - width
    for out, base, up in ((wq, qb, qu), (wo, ob, ou)):
        out[0:width] = base[...]
        rows = jnp.concatenate([2.0 * up[...].astype(F32), jnp.zeros((extra - rank, width), F32)], axis=0)
        out[width:] = rows.astype(BF)
    kv = kb.shape[0]
    wkv[0:kv, 0:width] = kb[...]
    wkv[kv:, 0:width] = vb[...]
    none = jnp.zeros((rank, kv), F32)
    pair = jnp.concatenate(
        [
            jnp.concatenate([none, none], axis=1),
            jnp.concatenate([2.0 * ku[...].astype(F32), none], axis=1),
            jnp.concatenate([none, 2.0 * vu[...].astype(F32)], axis=1),
            jnp.zeros((extra - 3 * rank, 2 * kv), F32),
        ],
        axis=0,
    )
    wkv[:, width:] = pair.T.astype(BF)
    down[...] = jnp.concatenate([qd[...].astype(F32), kd[...].astype(F32), vd[...].astype(F32)], axis=0).astype(BF)
    wide = gains[...]
    wide = jnp.concatenate([wide, jnp.zeros((8 - wide.shape[0], width), F32)], axis=0).T
    columns[0] = wide[:, 0:1]
    columns[1] = wide[:, 1:2]


def qkv_kernel(tok, gain, wq, wkv, down, qkv, normed, inner, tails, ext):
    width = tok.shape[1]
    kv = wkv.shape[0]
    value = tok[0].astype(F32)
    norm = (value * rms(value) * gain[...]).astype(BF)
    normed[0] = norm
    low = dot(down[...], norm).astype(BF)
    inner[0] = low
    ext[0:width] = norm
    ext[width:] = jnp.zeros((ext.shape[0] - width, ext.shape[1]), BF)
    ext[width : width + low.shape[0]] = low
    qkv[0, 0:width] = dot(wq[...], ext[...], TN).astype(BF)
    both = dot(wkv[...], ext[...]).astype(BF)
    qkv[0, width:] = both
    span = tok.shape[2]
    tails[0] = jnp.concatenate(
        [both[: kv // 2, span - WINDOW :], both[kv // 2 :, span - WINDOW :]], axis=1
    )


def aug_value(value):
    extra = lax.broadcasted_iota(jnp.int32, (AUG - value.shape[0], value.shape[1]), 0) == 0
    return jnp.concatenate([value, jnp.where(extra, 1.0, 0.0).astype(BF)], axis=0)


def key_kernel(kv_heads, qkv, tails, kmap, keep, phi, con):
    head = kmap.shape[1]
    first = qkv.shape[1] - 2 * kv_heads * head
    keeping = keep.astype(BF)
    for k in range(kv_heads):
        at = first + k * head
        key = jnp.concatenate([qkv[0, at : at + head], tails[0, k * head : (k + 1) * head, :WINDOW]], axis=1)
        at += kv_heads * head
        val = jnp.concatenate([qkv[0, at : at + head], tails[0, k * head : (k + 1) * head, WINDOW:]], axis=1)
        feat = soft_pair(dot(kmap[k], key, TN))
        phi[0, k] = feat
        con[0, k * AUG : (k + 1) * AUG] = dot(aug_value(val), feat * keeping, NT).astype(BF)


def masks(segq, segk, span):
    extent = segk.shape[0]
    row = lax.broadcasted_iota(jnp.int32, (extent, span), 0)
    pos = jnp.where(row < span, row, row - extent)
    query = lax.broadcasted_iota(jnp.int32, (extent, span), 1)
    same = segk == segq
    far = pos + WINDOW <= query
    return same & far, same & (pos <= query) & jnp.logical_not(far)


def local_kernel(
    kv_heads, group, qkv, tails, phik, frames, qmap, phiq, numer, den, lin_bias, win_bias, between,
):
    head = qmap.shape[1]
    span = qkv.shape[2]
    width = kv_heads * group * head
    segq, segk, _ = frames
    far, near = masks(segq, segk, span)
    lin_bias[...] = jnp.where(far, 1.0, 0.0)
    win_bias[...] = jnp.where(near, 0.0, -1e30)
    for k in range(kv_heads):
        at = width + k * head
        key = jnp.concatenate([qkv[0, at : at + head], tails[0, k * head : (k + 1) * head, :WINDOW]], axis=1)
        at += kv_heads * head
        val = jnp.concatenate([qkv[0, at : at + head], tails[0, k * head : (k + 1) * head, WINDOW:]], axis=1)
        queries, feats = [], []
        for h in range(k * group, (k + 1) * group):
            q = qkv[0, h * head : (h + 1) * head]
            f = soft_pair(dot(qmap[h], q, TN))
            phiq[0, h] = f
            queries.append(q)
            feats.append(f)
        query = jnp.concatenate(queries, axis=1) * (head**-0.5)
        feat = jnp.concatenate(feats, axis=1)
        lin = dot(phik[0, k], feat, TN)
        score = dot(key, query, TN)
        lb = jnp.concatenate([lin_bias[...]] * group, axis=1)
        wb = jnp.concatenate([win_bias[...]] * group, axis=1)
        weights = lin * lb + jnp.exp(score + wb)
        total = jnp.sum(weights, axis=0, keepdims=True)
        out = dot(val, weights.astype(BF))
        for g in range(group):
            h = k * group + g
            numer[0, h * head : (h + 1) * head] = out[:, g * span : (g + 1) * span]
            den[0, h : h + 1] = total[:, g * span : (g + 1) * span]
        between(k)


def join_kernel(
    kv_heads, group, phiq, numer, den_local, state, frames, tok, wo, down, gain,
    mixed, den, middle, normed, inner, ext,
):
    width = tok.shape[1]
    span = tok.shape[2]
    head = width // (kv_heads * group)
    shown = jnp.where(frames[0] == 0, 1.0, 0.0)
    den[0] = jnp.zeros_like(den[0])
    for h in range(kv_heads * group):
        k = h // group
        carried = dot(state[0, k * AUG : (k + 1) * AUG], phiq[0, h]) * shown
        total = den_local[0, h : h + 1] + carried[head : head + 1]
        at = pl.ds(h * head, head)
        ext[at] = ((numer[0, at] + carried[:head]) * (1.0 / total)).astype(BF)
        den[0, h : h + 1] = total
    got = ext[0:width]
    mixed[0] = got
    low = dot(down[...], got).astype(BF)
    inner[0] = low
    ext[width:] = jnp.zeros((ext.shape[0] - width, span), BF)
    ext[width : width + low.shape[0]] = low
    mid = tok[0].astype(F32) + dot(wo[...], ext[...], TN)
    middle[0] = mid
    normed[0] = (mid * rms(mid) * gain[...]).astype(BF)


def forward_kernel(
    rows, kv_heads, group,
    tok, tok_again, doc, gains, qb, kb, vb, ob, qu, ku, vu, ou, qd, kd, vd, od, qmap, kmap,
    qkv_out, normed, inner, tails_out, phik_out, phiq_out, state_out, mixed, den, middle, normed2, inner_o,
    wq, wkv, wo, down, columns,
    seg, kept, ext, qkv, sent, tails, phik, phiq, numer, den_local, lin_bias, win_bias, tail_sem, *refs,
):
    step = pl.program_id(0)
    place = Place()
    chain = Chain(place, False, 2, kept, *refs)
    width, span = tok.shape[1], tok.shape[2]

    def row(ref, r):
        return ref.at[pl.ds(r, 1)]

    def tail_copy(r):
        return remote(sent.at[r], tails.at[r], tail_sem.at[0, r], tail_sem.at[1, r], place.along(1))

    @pl.when(step == 0)
    def _():
        place.greet()

        @pl.when(jnp.logical_not(place.inside(-1)))
        def _():
            tails[...] = jnp.zeros_like(tails)

        frame(place, span, doc, seg, kept)
        assemble(width, (qb, kb, vb, ob, qu, ku, vu, ou, qd, kd, vd), gains, wq, wkv, wo, down, columns)

    @pl.when(step < rows)
    def _():
        qkv_kernel(tok, columns.at[0], wq, wkv, down, row(qkv, step), normed, inner, row(sent, step), ext)
        qkv_out[...] = qkv[pl.ds(step, 1)]

        @pl.when(place.inside(1))
        def _():
            tail_copy(step).start()

    @pl.when((step >= rows) & (step < 2 * rows))
    def _():
        r = step - rows

        @pl.when(place.inside(-1))
        def _():
            tail_copy(r).wait_recv()

        tails_out[...] = tails[pl.ds(r, 1)]
        keep = frame_row(seg, r, span)[2]
        key_kernel(kv_heads, row(qkv, r), row(tails, r), kmap, keep, row(phik, r), row(chain.own, r))
        phik_out[...] = phik[pl.ds(r, 1)]
        chain.turn(r, rows)

    @pl.when((step >= 2 * rows) & (step < 3 * rows))
    def _():
        r = step - 2 * rows

        def between(k):
            if k == kv_heads // 2 - 1:
                chain.turn(rows + 2 * r, rows, False)

        local_kernel(
            kv_heads, group, row(qkv, r), row(tails, r), row(phik, r), frame_row(seg, r, span), qmap,
            row(phiq, r), row(numer, r), row(den_local, r), lin_bias, win_bias, between,
        )
        phiq_out[...] = phiq[pl.ds(r, 1)]
        chain.turn(rows + 2 * r + 1, rows, False)

    @pl.when(step >= 3 * rows)
    def _():
        r = step - 3 * rows
        state_out[...] = chain.result[pl.ds(r, 1)]
        join_kernel(
            kv_heads, group, row(phiq, r), row(numer, r), row(den_local, r), row(chain.result, r),
            frame_row(seg, r, span), tok_again, wo, od, columns.at[1],
            mixed, den, middle, normed2, inner_o, ext,
        )

    @pl.when(step == 4 * rows - 1)
    def _():
        chain.close(rows)

        @pl.when(place.inside(1))
        def _():
            for r in range(rows):
                tail_copy(r).wait_send()


def ff_kernel(
    width, normed_h, cot_h, middle, gain, gate_h, up_h, down_h,
    out, grad_mid, grad_gain, shards,
    normed, cot, gate_v, up_v, down_v, hid, dgate, dup, sem, act_sem, *refs,
):
    step = pl.program_id(0)
    rows = normed_h.shape[0]
    span = normed_h.shape[2]
    high = normed.shape[0]
    hidden = gate_h.shape[1]
    tiles = hidden // TILE
    place = Place()
    scatter = Scatter(place, 3 * high, refs)

    def act_copies():
        made = []
        for r in range(rows):
            at = pl.ds(r * span, span)
            made.append(pltpu.make_async_copy(normed_h.at[r], normed.at[0:width, at], act_sem.at[r, 0]))
            made.append(pltpu.make_async_copy(cot_h.at[r], cot.at[0:width, at], act_sem.at[r, 1]))
        return made

    def tile_copies(j):
        at = pl.ds(pl.multiple_of(j * TILE, TILE), TILE)
        return [
            pltpu.make_async_copy(gate_h.at[:, at], gate_v.at[0:width, at], sem.at[j, 0]),
            pltpu.make_async_copy(up_h.at[:, at], up_v.at[0:width, at], sem.at[j, 1]),
            pltpu.make_async_copy(down_h.at[:, at], down_v.at[0:width, at], sem.at[j, 2]),
        ]

    @pl.when(step == 0)
    def _():
        place.greet()
        for copy in act_copies():
            copy.start()
        for j in range(tiles):
            for copy in tile_copies(j):
                copy.start()
        for ref in (gate_v, up_v, down_v):
            ref[width:] = jnp.zeros((high - width, hidden), BF)
        for ref in (normed, cot):
            ref[width:] = jnp.zeros((high - width, rows * span), BF)
        for copy in act_copies():
            copy.wait()

    @pl.when(step < tiles)
    def _():
        for copy in tile_copies(step):
            copy.wait()
        at = pl.ds(pl.multiple_of(step * TILE, TILE), TILE)
        gate, up, down = gate_v[:, at], up_v[:, at], down_v[:, at]
        for r in range(rows):
            lane = pl.ds(r * span, span)
            n2 = normed[:, lane]
            g = dot(gate, n2, TN)
            u = dot(up, n2, TN)
            dh = dot(down, cot[:, lane], TN).astype(BF).astype(F32)
            sig = 1.0 / (1.0 + jnp.exp(-g))
            act = g * sig
            hid[at, lane] = (act * u).astype(BF)
            dup[at, lane] = (dh * act).astype(BF)
            dgate[at, lane] = (dh * u * (sig + act * (1.0 - sig))).astype(BF)
        slot = step % 2
        for i, (left, right) in enumerate(((normed, dgate), (normed, dup), (cot, hid))):
            grad = dot(left[...], right[at, :], NT).astype(BF)
            for half in range(2):
                scatter.mine[slot, half, i * high : (i + 1) * high] = grad[:, half * 128 : (half + 1) * 128]

    @pl.when(step >= tiles)
    def _():
        r = step - tiles
        lane = pl.ds(pl.multiple_of(r * span, span), span)
        back = dot(gate_v[0:width], dgate[:, lane]) + dot(up_v[0:width], dup[:, lane])
        mid = middle[0]
        scale = rms(mid)
        unit = mid * scale
        grad_unit = back * gain[0]
        grad_mid[0] = cot[0:width, lane].astype(F32) + scale * (
            grad_unit - unit * jnp.mean(grad_unit * unit, axis=0, keepdims=True)
        )

        @pl.when(r == 0)
        def _():
            grad_gain[...] = jnp.zeros_like(grad_gain)

        grad_gain[...] += row_sum(back * unit)
        out[0] = (mid + dot(down_v[0:width], hid[:, lane])).astype(BF)

    def into(tile, stream, total):
        shards[tile, stream] = total.astype(BF)

    scatter.turn(step, tiles, into)


def pull_kernel(
    kv_heads, group, grad_mid, mixed, den, phiq, frames, inner, wo, down,
    dnum, dden, dstate, gup, gdown,
):
    width = mixed.shape[1]
    span = mixed.shape[2]
    head = width // (kv_heads * group)
    low = inner.shape[1]

    branch = grad_mid[0].astype(BF)
    wide = dot(wo[...], branch)
    grad_inner = wide[width : width + low].astype(BF)
    grad = (wide[:width] + dot(down[...], grad_inner, TN)).astype(BF).astype(F32)
    gup[...] += 2.0 * dot(inner[0], branch, NT)
    gdown[...] += dot(grad_inner, mixed[0], NT)
    shown = jnp.where(frames[0] == 0, 1.0, 0.0)
    dden[0] = jnp.zeros_like(dden[0])
    pad = jnp.zeros((AUG - head - 1, span), F32)
    for k in range(kv_heads):
        total = None
        for g in range(group):
            h = k * group + g
            at = pl.ds(h * head, head)
            dm = grad[h * head : (h + 1) * head]
            inv = 1.0 / den[0, h : h + 1]
            dd = -jnp.sum(dm * mixed[0, at].astype(F32), axis=0, keepdims=True) * inv
            dn = (dm * inv).astype(BF)
            dnum[0, at] = dn
            dden[0, h : h + 1] = dd
            aug = (jnp.concatenate([dn.astype(F32), dd, pad], axis=0) * shown).astype(BF)
            part = dot(aug, phiq[0, h], NT)
            total = part if total is None else total + part
        dstate[0, k * AUG : (k + 1) * AUG] = total.astype(BF)


def back_kernel(
    kv_heads, group, qkv, tails, phik, phiq, state, dcon, dnum, dden, frames, qmap, kmap,
    dq_out, dkv_out, dtails, gqmap, gkmap, lin_bias, win_bias, between,
):
    head = qmap.shape[1]
    width = dq_out.shape[1]
    span = dq_out.shape[2]
    scale = head**-0.5

    far, near = masks(frames[0], frames[1], span)
    lin_bias[...] = jnp.where(far, 1.0, 0.0)
    win_bias[...] = jnp.where(near, 0.0, -1e30)
    shown = jnp.where(frames[0] == 0, 1.0, 0.0)
    shown3 = jnp.concatenate([shown] * group, axis=1)
    keeping = frames[2]
    pad = jnp.zeros((AUG - head - 1, group * span), F32)
    for k in range(kv_heads):
        at = width + k * head
        key = jnp.concatenate([qkv[0, at : at + head], tails[0, k * head : (k + 1) * head, :WINDOW]], axis=1)
        at += kv_heads * head
        val = jnp.concatenate([qkv[0, at : at + head], tails[0, k * head : (k + 1) * head, WINDOW:]], axis=1)
        hs = range(k * group, (k + 1) * group)
        queries = [qkv[0, h * head : (h + 1) * head] for h in hs]
        query = jnp.concatenate(queries, axis=1) * scale
        feat = jnp.concatenate([phiq[0, h] for h in hs], axis=1)
        dn = jnp.concatenate([dnum[0, h * head : (h + 1) * head] for h in hs], axis=1)
        dd = jnp.concatenate([dden[0, h : h + 1] for h in hs], axis=1)
        kfeat = phik[0, k]
        lb = jnp.concatenate([lin_bias[...]] * group, axis=1)
        wb = jnp.concatenate([win_bias[...]] * group, axis=1)
        growth = jnp.exp(dot(key, query, TN) + wb)
        weights = (dot(kfeat, feat, TN) * lb + growth).astype(BF)
        dw = dot(val, dn, TN) + dd
        dlin = (dw * lb).astype(BF)
        dscore = (dw * growth).astype(BF)
        dv = dot(dn, weights, NT)
        aug = (jnp.concatenate([dn.astype(F32), dd, pad], axis=0) * shown3).astype(BF)
        held = state[0, k * AUG : (k + 1) * AUG]
        dfeat = dot(kfeat, dlin) + dot(held, aug, TN)
        con = dcon[0, k * AUG : (k + 1) * AUG]
        dkfeat = dot(feat, dlin, NT) + dot(con, aug_value(val), TN) * keeping
        dv = dv + dot(con[:head], kfeat * keeping.astype(BF))
        dq = dot(key, dscore) * scale
        dk = dot(query, dscore, NT)
        dt = soft_pair_back(feat, dfeat.astype(BF).astype(F32))
        for g in range(group):
            h = k * group + g
            part = dt[:, g * span : (g + 1) * span]
            gqmap[h] += dot(queries[g], part, NT)
            full = dq[:, g * span : (g + 1) * span] + dot(qmap[h], part)
            dq_out[0, h * head : (h + 1) * head] = full.astype(BF)
        dtk = soft_pair_back(kfeat, dkfeat.astype(BF).astype(F32))
        gkmap[k] += dot(key, dtk, NT)
        dk = dk + dot(kmap[k], dtk)
        ks, vs = k * head, (kv_heads + k) * head
        dkv_out[0, ks : ks + head] = dk[:, :span]
        dkv_out[0, vs : vs + head] = dv[:, :span]
        dtails[0, ks : ks + head] = jnp.concatenate([dk[:, span:], dv[:, span:]], axis=1).astype(BF)
        between(k)


def final_kernel(
    tok, grad_mid, gain, dq, dkv, returned, normed, inner, wq, wkv, down,
    grad_tok, ggain, gdown, gup,
):
    width = tok.shape[1]
    span = tok.shape[2]
    low = down.shape[0]

    got = returned[0].astype(F32)
    got = jnp.concatenate([got[:, :WINDOW], got[:, WINDOW:]], axis=0)
    own = dkv[0]
    both = jnp.concatenate([own[:, : span - WINDOW], own[:, span - WINDOW :] + got], axis=1).astype(BF)
    grad_q = dq[0]
    wide = dot(wq[...], grad_q) + dot(wkv[...], both, TN)
    grad_inner = wide[width : width + low].astype(BF)
    back = wide[:width] + dot(down[...], grad_inner, TN)
    gdown[...] += dot(grad_inner, normed[0], NT)
    gup[:, :width] += 2.0 * dot(inner[0], grad_q, NT)
    gup[:, width:] += 2.0 * dot(inner[0], both, NT)
    value = tok[0].astype(F32)
    scale = rms(value)
    unit = value * scale
    grad_unit = back * gain[...]
    ggain[...] += row_sum(back * unit)
    grad_tok[0] = grad_mid[0] + scale * (
        grad_unit - unit * jnp.mean(grad_unit * unit, axis=0, keepdims=True)
    )


def backward_kernel(
    rows, kv_heads, group, tiles, shard_rows, layout,
    doc, grad_mid_p, mixed, den, phiq_p, inner_o, wo, odown,
    qkv, tails, phik, phiq, state, qmap, kmap,
    tok, grad_mid, normed, inner, gain, wq, wkv, down, gpost, shards,
    grad_tok, whole, small_out,
    dnum, dden, dq, dkv, dtails, returned, gup_o, gdown_o, gqmap, gkmap, ggain, gdown, gup, lin_bias, win_bias,
    seg, kept, tail_sem, small_shard, small, *refs,
):
    step = pl.program_id(0)
    place = Place()
    chain = Chain(place, True, 1, kept, *refs[:9])
    refs = refs[9:]
    n_gather = len(gather_scratch(shard_rows, tiles))
    gather = Gather(place, shard_rows, shards, whole, refs[:n_gather])
    refs = refs[n_gather:]
    n_small = len(gather_scratch(layout.rows, 1))
    small_gather = Gather(place, layout.rows, small_shard, small, refs[:n_small])
    small_scatter = Scatter(place, layout.rows, refs[n_small:], 1)

    def row(ref, r):
        return ref.at[pl.ds(r, 1)]

    def tail_copy(r):
        return remote(dtails.at[r], returned.at[r], tail_sem.at[0, r], tail_sem.at[1, r], place.along(-1))

    @pl.when(step == 0)
    def _():
        place.greet()
        frame(place, tok.shape[2], doc, seg, kept)
        for ref in (gup_o, gdown_o, gqmap, gkmap, ggain, gdown, gup):
            ref[...] = jnp.zeros_like(ref)

        @pl.when(jnp.logical_not(place.inside(1)))
        def _():
            returned[...] = jnp.zeros_like(returned)

    @pl.when(step < rows)
    def _():
        pull_kernel(
            kv_heads, group, grad_mid_p, mixed, den, phiq_p, frame_row(seg, step, tok.shape[2]), inner_o, wo, odown,
            row(dnum, step), row(dden, step), row(chain.own, step), gup_o, gdown_o,
        )

    @pl.when((step >= rows) & (step < 2 * rows))
    def _():
        r = step - rows

        def between(k):
            if k == kv_heads // 2:
                gather.turn(2 * r, tiles)

        back_kernel(
            kv_heads, group, qkv, tails, phik, phiq, state, row(chain.result, r), row(dnum, r), row(dden, r),
            frame_row(seg, r, tok.shape[2]), qmap, kmap,
            row(dq, r), row(dkv, r), row(dtails, r), gqmap, gkmap, lin_bias, win_bias, between,
        )

        @pl.when(place.inside(-1))
        def _():
            tail_copy(r).start()

    @pl.when(step >= 2 * rows)
    def _():
        r = step - 2 * rows

        @pl.when(place.inside(1))
        def _():
            tail_copy(r).wait_recv()

        final_kernel(
            tok, grad_mid, gain.at[0], row(dq, r), row(dkv, r), row(returned, r), normed, inner, wq, wkv, down,
            grad_tok, ggain, gdown, gup,
        )

    chain.turn(step, rows)

    @pl.when(step >= rows)
    def _():
        gather.turn(jnp.where(step < 2 * rows, 2 * (step - rows) + 1, step), tiles)

    @pl.when(step == 3 * rows - 1)
    def _():
        chain.close(rows)

        @pl.when(place.inside(-1))
        def _():
            for r in range(rows):
                tail_copy(r).wait_send()

        rank = gdown_o.shape[0]
        width = gdown_o.shape[1]
        kv_width = kv_heads * qmap.shape[1]
        mine = small_scatter.mine
        mine[...] = jnp.zeros_like(mine)
        pad = [jnp.zeros((6, width), F32)]
        layout.put(mine, "down", jnp.concatenate([gdown[...], ggain[0:1], gpost[0:1]] + pad, axis=0))
        layout.put(mine, "out", jnp.concatenate([gdown_o[...], gup_o[...]], axis=0))
        layout.put(mine, "q_up", jnp.concatenate([gup[0:rank, :width], jnp.zeros((rank, width), F32)], axis=0))
        layout.put(
            mine, "kv_up",
            jnp.concatenate(
                [gup[rank : 2 * rank, width : width + kv_width], gup[2 * rank :, width + kv_width :]], axis=0
            ),
        )
        layout.put_heads(mine, "qmap", gqmap)
        layout.put_heads(mine, "kmap", gkmap)

        def into(stream, total):
            small_shard[0, stream] = total.astype(BF)

        small_scatter.run(into)
        small_gather.run()
        small_out[...] = small[...]
        for turn in range(3 * rows, tiles + WAYS[0]):
            gather.turn(jnp.int32(turn), tiles)


def row_spec(*shape):
    zeros = (0,) * len(shape)
    return pl.BlockSpec((1,) + shape, lambda r: (r,) + zeros)


def whole_spec(*shape):
    zeros = (0,) * len(shape)
    return pl.BlockSpec(shape, lambda r: zeros, pipeline_mode=pl.Buffered(1))


def shape_of(shape, kind):
    return jax.ShapeDtypeStruct(shape, kind)


def body(
    tokens, doc_starts, pregain, query_base, key_base, value_base, output_base, query_down, query_up,
    key_down, key_up, value_down, value_up, out_down, out_up, query_map, key_map, postgain, gate_proj,
    up_proj, down_proj, cotangent,
):
    rows, span, width = tokens.shape
    heads, head, _ = query_map.shape
    kv_heads = key_map.shape[0]
    group = heads // kv_heads
    kv_width = kv_heads * head
    rank = query_up.shape[0]
    extent = span + WINDOW
    hidden = gate_proj.shape[1]
    tiles = hidden // TILE
    high = -(-width // 256) * 256
    feats = 2 * head
    slots = -(-heads // 8) * 8

    tok = jnp.swapaxes(tokens, 1, 2)
    cot = jnp.swapaxes(cotangent, 1, 2)
    gains = jnp.stack([pregain, postgain]).astype(F32)
    odown = out_down.T

    def phase_spec(shape, phase):
        tail = (0,) * (len(shape) - 1)
        return pl.BlockSpec((1,) + tuple(shape[1:]), lambda s: (jnp.clip(s - phase * rows, 0, rows - 1),) + tail)

    args = [
        (tok, 0), (tok, 3), (doc_starts, None), (gains, None), (query_base, None), (key_base.T, None),
        (value_base.T, None), (output_base, None), (query_up, None), (key_up, None), (value_up, None),
        (out_up, None), (query_down.T, None), (key_down.T, None), (value_down.T, None), (odown, None),
        (query_map, None), (key_map, None),
    ]
    made = [
        ((rows, width + 2 * kv_width, span), BF, 0),
        ((rows, width, span), BF, 0),
        ((rows, 3 * rank, span), BF, 0),
        ((rows, kv_width, 2 * WINDOW), BF, 1),
        ((rows, kv_heads, feats, extent), BF, 1),
        ((rows, heads, feats, span), BF, 2),
        ((rows, kv_heads * AUG, feats), BF, 3),
        ((rows, width, span), BF, 3),
        ((rows, slots, span), F32, 3),
        ((rows, width, span), F32, 3),
        ((rows, width, span), BF, 3),
        ((rows, rank, span), BF, 3),
        ((high, width), BF, None),
        ((2 * kv_width, high), BF, None),
        ((high, width), BF, None),
        ((3 * rank, width), BF, None),
        ((2, width, 1), F32, None),
    ]
    biases = [pltpu.VMEM((extent, span), F32)] * 2
    frame_scratch = [pltpu.VMEM((8, extent), F32), pltpu.VMEM((8, 128), F32)]
    (
        qkv, normed, inner, tails, phik, phiq, state, mixed, den, middle, normed2, inner_o, wq, wkv, wo, down, columns,
    ) = pl.pallas_call(
        functools.partial(forward_kernel, rows, kv_heads, group),
        grid=(4 * rows,),
        in_specs=[whole_spec(*a.shape) if phase is None else phase_spec(a.shape, phase) for a, phase in args],
        out_specs=tuple(
            pl.BlockSpec(shape, functools.partial(lambda n, s: (0,) * n, len(shape)))
            if phase is None
            else phase_spec(shape, phase)
            for shape, _, phase in made
        ),
        out_shape=tuple(shape_of(shape, kind) for shape, kind, _ in made),
        scratch_shapes=frame_scratch
        + [
            pltpu.VMEM((high, span), BF),
            pltpu.VMEM((rows, width + 2 * kv_width, span), BF),
            pltpu.VMEM((rows, kv_width, 2 * WINDOW), BF),
            pltpu.VMEM((rows, kv_width, 2 * WINDOW), BF),
            pltpu.VMEM((rows, kv_heads, feats, extent), BF),
            pltpu.VMEM((rows, heads, feats, span), BF),
            pltpu.VMEM((rows, width, span), F32),
            pltpu.VMEM((rows, slots, span), F32),
        ]
        + biases
        + [pltpu.SemaphoreType.DMA((2, rows))]
        + chain_scratch(rows, kv_heads * AUG, feats),
        compiler_params=pltpu.CompilerParams(vmem_limit_bytes=VMEM, collective_id=2, has_side_effects=True),
    )(*[a for a, _ in args])

    last = lambda s: (jnp.maximum(s - tiles, 0), 0, 0)
    fixed = lambda s: (0, 0)
    anywhere = pl.BlockSpec(memory_space=pl.ANY)
    streams = stream_plan(3 * high)
    shard_shape = (tiles, len(streams), streams[0][2][-1][1], 128)
    layer_out, grad_mid, gpost, shards = pl.pallas_call(
        functools.partial(ff_kernel, width),
        grid=(tiles + rows,),
        in_specs=[anywhere, anywhere, pl.BlockSpec((1, width, span), last), pl.BlockSpec((1, width, 1), lambda s: (1, 0, 0))]
        + [anywhere] * 3,
        out_specs=(
            pl.BlockSpec((1, width, span), last),
            pl.BlockSpec((1, width, span), last),
            pl.BlockSpec((8, width), fixed),
            pl.BlockSpec(shard_shape, lambda s: (0, 0, 0, 0)),
        ),
        out_shape=(
            shape_of((rows, width, span), BF),
            shape_of((rows, width, span), F32),
            shape_of((8, width), F32),
            shape_of(shard_shape, BF),
        ),
        scratch_shapes=[pltpu.VMEM((high, rows * span), BF)] * 2
        + [pltpu.VMEM((high, hidden), BF)] * 3
        + [pltpu.VMEM((hidden, rows * span), BF)] * 3
        + [pltpu.SemaphoreType.DMA((tiles, 3)), pltpu.SemaphoreType.DMA((rows, 2))]
        + scatter_scratch(3 * high, BF),
        compiler_params=pltpu.CompilerParams(vmem_limit_bytes=VMEM, collective_id=0, has_side_effects=True),
    )(normed2, cot, middle, columns, gate_proj, up_proj, down_proj.T)

    layout = Small(rank, width, kv_width, heads, kv_heads, head)
    args = [(doc_starts, None)]
    args += [(a, 0) for a in (grad_mid, mixed, den, phiq, inner_o)] + [(wo, None), (odown, None)]
    args += [(a, 1) for a in (qkv, tails, phik, phiq, state)] + [(query_map, None), (key_map, None)]
    args += [(a, 2) for a in (tok, grad_mid, normed, inner)] + [(a, None) for a in (columns, wq, wkv, down, gpost)]
    specs = [whole_spec(*a.shape) if phase is None else phase_spec(a.shape, phase) for a, phase in args]
    args = [a for a, _ in args]
    args.append(shards)
    specs.append(anywhere)
    last = lambda s: (jnp.maximum(s - 2 * rows, 0), 0, 0)
    small_streams = stream_plan(layout.rows)
    grad_tok, whole, small = pl.pallas_call(
        functools.partial(backward_kernel, rows, kv_heads, group, tiles, 3 * high, layout),
        grid=(3 * rows,),
        in_specs=specs,
        out_specs=(
            pl.BlockSpec((1, width, span), last),
            anywhere,
            pl.BlockSpec((1, 2, layout.rows, 128), lambda s: (0, 0, 0, 0)),
        ),
        out_shape=(
            shape_of((rows, width, span), F32),
            shape_of((tiles, 2, 3 * high, 128), BF),
            shape_of((1, 2, layout.rows, 128), BF),
        ),
        scratch_shapes=[
            pltpu.VMEM((rows, width, span), BF),
            pltpu.VMEM((rows, slots, span), F32),
            pltpu.VMEM((rows, width, span), BF),
            pltpu.VMEM((rows, 2 * kv_width, span), F32),
            pltpu.VMEM((rows, kv_width, 2 * WINDOW), BF),
            pltpu.VMEM((rows, kv_width, 2 * WINDOW), BF),
            pltpu.VMEM((rank, width), F32),
            pltpu.VMEM((rank, width), F32),
            pltpu.VMEM((heads, head, head), F32),
            pltpu.VMEM((kv_heads, head, head), F32),
            pltpu.VMEM((8, width), F32),
            pltpu.VMEM((3 * rank, width), F32),
            pltpu.VMEM((3 * rank, width + 2 * kv_width), F32),
        ]
        + biases
        + frame_scratch
        + [
            pltpu.SemaphoreType.DMA((2, rows)),
            pltpu.VMEM((1, len(small_streams), small_streams[0][2][-1][1], 128), BF),
            pltpu.VMEM((1, 2, layout.rows, 128), BF),
        ]
        + chain_scratch(rows, kv_heads * AUG, feats)
        + gather_scratch(3 * high, tiles)
        + gather_scratch(layout.rows, 1)
        + scatter_scratch(layout.rows, BF, 1),
        compiler_params=pltpu.CompilerParams(vmem_limit_bytes=VMEM, collective_id=1, has_side_effects=True),
    )(*args)

    column = pl.BlockSpec((width, TILE), lambda j: (0, j))
    flat = [(1, width)] * 2 + [(rank, width)] * 4 + [(rank, kv_width)] * 2 + [(rank, width)] * 2
    flat += [query_map.shape, key_map.shape]
    pieces = next(n for n in range(tiles // rows, 0, -1) if width % (16 * n) == 0 and tiles >= n * rows)
    part = pl.BlockSpec(
        (1, width // pieces, span),
        lambda j: (jnp.minimum(j // pieces, rows - 1), jnp.where(j < rows * pieces, j % pieces, pieces - 1), 0),
    )
    outs = pl.pallas_call(
        functools.partial(widen_kernel, width, high, rank, layout),
        grid=(tiles,),
        in_specs=[
            pl.BlockSpec((1, 2, 3 * high, 128), lambda j: (j, 0, 0, 0)),
            pl.BlockSpec((1, 2, layout.rows, 128), lambda j: (0, 0, 0, 0)),
            part,
            part,
        ],
        out_specs=(part, part)
        + (column,) * 3
        + tuple(pl.BlockSpec(f, functools.partial(lambda n, j: (0,) * n, len(f))) for f in flat),
        out_shape=(shape_of(layer_out.shape, BF), shape_of(grad_tok.shape, F32))
        + (shape_of((width, hidden), F32),) * 3
        + tuple(shape_of(f, F32) for f in flat),
        compiler_params=pltpu.CompilerParams(vmem_limit_bytes=VMEM),
    )(whole, small, layer_out, grad_tok)
    layer_out, grad_tok, gate, up, down_t, pre, post, qd, kd, vd, qu, ku, vu, od, ou, gq, gk = outs
    return (
        jnp.swapaxes(layer_out, 1, 2),
        jnp.swapaxes(grad_tok, 1, 2),
        pre[0],
        qd.T,
        qu,
        kd.T,
        ku,
        vd.T,
        vu,
        od.T,
        ou,
        gq,
        gk,
        post[0],
        gate,
        up,
        down_t.T,
    )


def solution(mesh):
    wide = P("batch", "seq", None)
    return jax.shard_map(
        body,
        mesh=mesh,
        in_specs=(wide, P("batch", None)) + (P(),) * 19 + (wide,),
        out_specs=(wide, wide) + (P(),) * 15,
        check_vma=False,
    )
```

```python
import functools

import jax
import jax.numpy as jnp
from jax import lax
from jax.experimental import pallas as pl
from jax.experimental.pallas import tpu as pltpu
from jax.sharding import PartitionSpec as P

WINDOW = 64
EPSILON = 1e-05
BF = jnp.bfloat16
F32 = jnp.float32
NN = (((1,), (0,)), ((), ()))
NT = (((1,), (1,)), ((), ()))
TN = (((0,), (0,)), ((), ()))
HI = 4
TILE = 256
AUG = 80
VMEM = 62 << 20
MESH = pl.DeviceIdType.MESH


def dot(left, right, dims=NN):
    return lax.dot_general(left, right, dims, preferred_element_type=F32)


def split_seq(index, count):
    low = max(count // HI, 1)
    return index // low, index % low, count // low, low


class Place:
    def __init__(self):
        batch, seq = lax.axis_index("batch"), lax.axis_index("seq")
        n_seq = lax.axis_size("seq")
        hi, lo, n_hi, n_lo = split_seq(seq, n_seq)
        self.batch, self.seq = batch, seq
        self.at = {"core": batch % 2, "y": batch // 2, "hi": hi, "lo": lo}
        self.size = axis_sizes()

    def peer(self, axis, distance):
        at = dict(self.at)
        at[axis] = (at[axis] + distance) % self.size[axis]
        return (at["y"] * 2 + at["core"], at["hi"] * self.size["lo"] + at["lo"])

    def along(self, distance):
        return (self.batch, self.seq + distance)

    def inside(self, distance):
        return (self.seq + distance >= 0) & (self.seq + distance < self.size["hi"] * self.size["lo"])

    def others(self):
        size = self.size
        return [
            (a, b, c)
            for a in range(size["lo"])
            for b in range(size["y"])
            for c in range(size["hi"])
            if a or b or c
        ]

    def other(self, offset):
        at = [(self.at[n] + d) % self.size[n] for n, d in zip(("lo", "y", "hi"), offset)]
        number = (at[0] * self.size["y"] + at[1]) * self.size["hi"] + at[2]
        return (at[1] * 2 + self.at["core"], at[2] * self.size["lo"] + at[0]), number

    def greet(self, everyone=False):
        barrier = pltpu.get_barrier_semaphore()
        total = 0
        for d in (-1, 1):

            @pl.when(self.inside(d))
            def _():
                pl.semaphore_signal(barrier, inc=1, device_id=self.along(d), device_id_type=MESH)

            total = total + jnp.where(self.inside(d), 1, 0)
        peers = [self.peer("core", 1)]
        if everyone:
            peers += [self.other(offset)[0] for offset in self.others()]
        else:
            peers += [self.peer(axis, d) for axis in ("lo", "y", "hi") for d in range(1, self.size[axis])]
        for peer in peers:
            pl.semaphore_signal(barrier, inc=1, device_id=peer, device_id_type=MESH)
            total = total + 1
        pl.semaphore_wait(barrier, total)


def axis_sizes():
    _, _, n_hi, n_lo = split_seq(0, lax.axis_size("seq"))
    return {"core": 2, "y": lax.axis_size("batch") // 2, "hi": n_hi, "lo": n_lo}


def stream_plan(rows):
    size = axis_sizes()
    grain = 16 * size["lo"] * size["y"] * size["hi"]
    part = rows // (2 * grain) * grain
    plan = []
    for i, order in enumerate((("lo", "y", "hi"), ("y", "lo", "hi"))):
        left, stages = part, []
        for axis in order:
            left = left // size[axis]
            stages.append((axis, left, True))
        plan.append((i * part, part, stages))
    rest = rows - 2 * part
    if rest:
        left = rest // size["hi"]
        plan.append((2 * part, rest, [("hi", left, True), ("lo", left, False), ("y", left, False)]))
    return plan


def shard_rows(rows):
    return max(stages[-1][1] for _, _, stages in stream_plan(rows))


def remote(src, dst, send, recv, peer):
    return pltpu.make_async_remote_copy(
        src_ref=src, dst_ref=dst, send_sem=send, recv_sem=recv, device_id=peer, device_id_type=MESH
    )


LAGS = (1, 3, 4, 5)


def stage_slots(k, slots):
    return 2 * slots if k == 1 else slots


def scatter_scratch(rows, kind, slots=2):
    size = axis_sizes()
    made = [
        pltpu.VMEM((slots, 2, rows, 128), kind),
        pltpu.VMEM((slots, rows, 128), kind),
        pltpu.VMEM((stage_slots(1, slots), rows, 128), kind),
        pltpu.SemaphoreType.DMA((2, slots)),
    ]
    for _, _, stages in stream_plan(rows):
        for k, (axis, left, _) in enumerate(stages, 1):
            peers = max(size[axis] - 1, 1)
            made.append(pltpu.VMEM((stage_slots(k, slots), peers, left, 128), kind))
            made.append(pltpu.VMEM((slots, left, 128), kind))
            made.append(pltpu.SemaphoreType.DMA((2, stage_slots(k, slots), peers)))
    return made


class Scatter:
    def __init__(self, place, rows, refs, slots=2):
        self.place, self.rows, self.slots = place, rows, slots
        self.mine, self.other, self.base, self.core_sem = refs[:4]
        self.streams = []
        at = 4
        for first, part, stages in stream_plan(rows):
            made = []
            for axis, left, divides in stages:
                made.append((axis, left) + tuple(refs[at : at + 3]) + (divides,))
                at += 3
            self.streams.append((first, part, made))

    def core_copy(self, t):
        slot = t % self.slots
        core = self.place.at["core"]
        return remote(
            self.mine.at[slot, 1 - core], self.other.at[slot],
            self.core_sem.at[0, slot], self.core_sem.at[1, slot], self.place.peer("core", 1),
        )

    def copies(self, k, t):
        slot = t % stage_slots(k, self.slots)
        made = []
        for first, part, stages in self.streams:
            axis, left, got, _, sem, divides = stages[k - 1]
            size = self.place.size[axis]
            for d in range(1, size):
                to = (self.place.at[axis] + d) % size if divides else 0
                if k == 1:
                    src = self.base.at[slot, pl.ds(pl.multiple_of(first + to * left, 16), left)]
                else:
                    src = stages[k - 2][3].at[t % self.slots, pl.ds(pl.multiple_of(to * left, 16), left)]
                made.append(
                    remote(
                        src, got.at[slot, d - 1], sem.at[0, slot, d - 1], sem.at[1, slot, d - 1],
                        self.place.peer(axis, d),
                    )
                )
        return made

    def start(self, k, t):
        for copy in [self.core_copy(t)] if k == 0 else self.copies(k, t):
            copy.start()

    def finish(self, k, t, into=None):
        slot = t % self.slots
        ahead = t % stage_slots(k, self.slots)
        if k == 0:
            self.core_copy(t).wait()
            core = self.place.at["core"]
            total = self.mine[slot, core].astype(F32) + self.other[slot].astype(F32)
            self.base[t % stage_slots(1, self.slots)] = total.astype(self.base.dtype)
            return
        for copy in self.copies(k, t):
            copy.wait()
        for i, (first, part, stages) in enumerate(self.streams):
            axis, left, got, out, _, divides = stages[k - 1]
            size = self.place.size[axis]
            at = self.place.at[axis] * left if divides else 0
            if k == 1:
                own = self.base[ahead, pl.ds(pl.multiple_of(first + at, 16), left)]
            else:
                own = stages[k - 2][3][slot, pl.ds(pl.multiple_of(at, 16), left)]
            if divides or size == 2:
                total = own.astype(F32)
                for d in range(1, size):
                    total = total + got[ahead, d - 1].astype(F32)
            else:
                total = jnp.zeros(own.shape, F32)
                for p in range(size):
                    d = (self.place.at[axis] - p) % size
                    part = jnp.where(d == 0, own, got[ahead, jnp.maximum(d - 1, 0)])
                    total = total + part.astype(F32)
            if k == 3:
                into(i, total)
            else:
                out[slot] = total.astype(out.dtype)

    def turn(self, step, tiles, into):
        for k in (3, 2, 1, 0):
            t = step - LAGS[k]

            @pl.when((t >= 0) & (t < tiles))
            def _():
                self.finish(k, t, functools.partial(into, t))
                if k < 3:
                    self.start(k + 1, t)

        @pl.when(step < tiles)
        def _():
            self.start(0, step)


WAYS = (6, 5, 3, 1)


def gather_scratch(rows, tiles):
    size = axis_sizes()
    made = [pltpu.SemaphoreType.DMA((2, tiles)), pltpu.SemaphoreType.DMA((tiles, len(stream_plan(rows))))]
    for _, _, stages in stream_plan(rows):
        for axis, left, _ in stages:
            made.append(pltpu.SemaphoreType.DMA((2, tiles, max(size[axis] - 1, 1))))
    return made


class Gather:
    def __init__(self, place, rows, shards, whole, refs):
        self.place, self.rows, self.shards, self.whole = place, rows, shards, whole
        self.core_sem, self.own_sem = refs[:2]
        self.streams = []
        at = 2
        for first, part, stages in stream_plan(rows):
            self.streams.append((first, part, [st + (refs[at + i],) for i, st in enumerate(stages)]))
            at += len(stages)

    def region(self, t, stream, k):
        first, _, stages = self.streams[stream]
        at = first
        for axis, left, divides, _ in stages[:k]:
            at = at + (self.place.at[axis] * left if divides else 0)
        return self.whole.at[t, self.place.at["core"], pl.ds(pl.multiple_of(at, 16), stages[k - 1][1])]

    def shard(self, t, stream):
        return self.shards.at[t, stream, 0 : self.streams[stream][2][-1][1]]

    def own_copies(self, t):
        return [
            pltpu.make_async_copy(self.shard(t, i), self.region(t, i, 3), self.own_sem.at[t, i])
            for i in range(len(self.streams))
        ]

    def copies(self, k, t):
        if k == 0:
            half = self.whole.at[t, self.place.at["core"]]
            return [remote(half, half, self.core_sem.at[0, t], self.core_sem.at[1, t], self.place.peer("core", 1))]
        made = []
        for i, (_, _, stages) in enumerate(self.streams):
            axis, left, divides, sem = stages[k - 1]
            if not divides:
                continue
            dst = self.region(t, i, k)
            src = self.shard(t, i) if k == 3 else dst
            for d in range(1, self.place.size[axis]):
                made.append(remote(src, dst, sem.at[0, t, d - 1], sem.at[1, t, d - 1], self.place.peer(axis, d)))
        return made

    def turn(self, step, tiles):
        for k in (0, 1, 2, 3):
            t = step - WAYS[k]

            @pl.when((t >= 0) & (t < tiles))
            def _():
                for copy in self.copies(k, t):
                    copy.wait()
                if k == 3:
                    for copy in self.own_copies(t):
                        copy.wait()
                if k > 0:
                    for copy in self.copies(k - 1, t):
                        copy.start()

        @pl.when(step < tiles)
        def _():
            for copy in self.own_copies(step) + self.copies(3, step):
                copy.start()


class Chain:
    def __init__(self, place, reverse, lag, kept, own, around, total, before, leaving, entering, result, lo_sem, hi_sem):
        self.place, self.reverse, self.lag, self.kept = place, reverse, lag, kept
        self.own, self.around, self.total, self.before = own, around, total, before
        self.leaving, self.entering, self.result = leaving, entering, result
        self.lo_sem, self.hi_sem = lo_sem, hi_sem
        self.n_hi, self.n_lo = place.size["hi"], place.size["lo"]
        hi = place.at["hi"]
        self.rank = self.n_hi - 1 - hi if reverse else hi

    def lo_copies(self, r):
        return [
            remote(
                self.own.at[r], self.around.at[d - 1, r], self.lo_sem.at[0, r, d - 1], self.lo_sem.at[1, r, d - 1],
                self.place.peer("lo", d),
            )
            for d in range(1, self.n_lo)
        ]

    def hi_copy(self, r):
        return remote(
            self.leaving.at[r], self.entering.at[r], self.hi_sem.at[0, r], self.hi_sem.at[1, r],
            self.place.peer("hi", -1 if self.reverse else 1),
        )

    def keep(self, r, pos):
        flags = self.kept[pl.ds(r, 1), :]
        here = lax.broadcasted_iota(jnp.int32, flags.shape, 1) == self.place.at["hi"] * self.n_lo + pos
        return jnp.sum(jnp.where(here, flags, 0.0), axis=1, keepdims=True)

    def order(self):
        return list(range(self.n_lo))[:: -1 if self.reverse else 1]

    def begin(self, r):
        for copy in self.lo_copies(r):
            copy.start()

    def leave(self, r, value):
        @pl.when(self.rank < self.n_hi - 1)
        def _():
            self.leaving[r] = value.astype(BF)
            self.hi_copy(r).start()

    def join(self, r):
        for copy in self.lo_copies(r):
            copy.wait()
        lo = self.place.at["lo"]
        total = jnp.zeros(self.own.shape[1:], F32)
        before = total
        for pos in self.order():
            part = self.own[r].astype(F32)
            before = jnp.where(lo == pos, total, before)
            for d in range(1, self.n_lo):
                part = jnp.where((lo - pos) % self.n_lo == d, self.around[d - 1, r].astype(F32), part)
            total = part + self.keep(r, pos) * total
        self.total[r] = total
        self.before[r] = before

        @pl.when(self.rank == 0)
        def _():
            self.leave(r, total)
            self.result[r] = before.astype(BF)

    def hop(self, r):
        self.hi_copy(r).wait_recv()
        entering = self.entering[r].astype(F32)
        lo = self.place.at["lo"]
        keep_all = keep_before = jnp.ones((1, 1), F32)
        for pos in self.order():
            keep_before = jnp.where(lo == pos, keep_all, keep_before)
            keep_all = keep_all * self.keep(r, pos)
        self.leave(r, self.total[r] + keep_all * entering)
        self.result[r] = (self.before[r] + keep_before * entering).astype(BF)

    def turn(self, step, rows, starts=True):
        for q in range(self.n_hi - 1, 0, -1):
            r = step - self.lag * (1 + q)

            @pl.when((r >= 0) & (r < rows) & (self.rank == q))
            def _():
                self.hop(r)

        r = step - self.lag

        @pl.when((r >= 0) & (r < rows))
        def _():
            self.join(r)

        if starts:

            @pl.when(step < rows)
            def _():
                self.begin(step)

    def close(self, rows):
        @pl.when(self.rank < self.n_hi - 1)
        def _():
            for r in range(rows):
                self.hi_copy(r).wait_send()


def chain_scratch(rows, height, feats):
    size = axis_sizes()
    peers = max(size["lo"] - 1, 1)
    shape = (rows, height, feats)
    return [
        pltpu.VMEM(shape, BF),
        pltpu.VMEM((peers,) + shape, BF),
        pltpu.VMEM(shape, F32),
        pltpu.VMEM(shape, F32),
        pltpu.VMEM(shape, BF),
        pltpu.VMEM(shape, BF),
        pltpu.VMEM(shape, BF),
        pltpu.SemaphoreType.DMA((2, rows, peers)),
        pltpu.SemaphoreType.DMA((2, rows)),
    ]


class Direct:
    def __init__(self, place, whole, mine, other, base, got, core_sem, out_sem, back_sem):
        self.place, self.whole = place, whole
        self.mine, self.other, self.base, self.got = mine, other, base, got
        self.core_sem, self.out_sem, self.back_sem = core_sem, out_sem, back_sem
        self.offsets = place.others()
        self.rows = base.shape[0] // (len(self.offsets) + 1)
        self.own = self.region(place.other((0, 0, 0))[1])

    def region(self, number):
        return pl.ds(pl.multiple_of(number * self.rows, 16), self.rows)

    def copies(self, k):
        core = self.place.at["core"]
        made = []
        if k == 0:
            partner = self.place.peer("core", 1)
            made.append(
                remote(self.mine.at[0, 1 - core], self.other, self.core_sem.at[0, 0], self.core_sem.at[1, 0], partner)
            )
        elif k == 3:
            half = self.whole.at[0, core]
            made.append(
                remote(half, half, self.core_sem.at[0, 1], self.core_sem.at[1, 1], self.place.peer("core", 1))
            )
        else:
            for i, offset in enumerate(self.offsets):
                peer, number = self.place.other(offset)
                if k == 1:
                    src, dst, sem = self.base.at[self.region(number)], self.got.at[i], self.out_sem
                else:
                    src = dst = self.whole.at[0, core, self.own]
                    sem = self.back_sem
                made.append(remote(src, dst, sem.at[0, i], sem.at[1, i], peer))
        return made

    def start(self, k):
        for copy in self.copies(k):
            copy.start()

    def finish(self, k):
        for copy in self.copies(k):
            copy.wait()
        core = self.place.at["core"]
        if k == 0:
            self.base[...] = self.mine[0, core] + self.other[...]
        elif k == 1:
            total = self.base[self.own].astype(F32)
            for i in range(len(self.offsets)):
                total = total + self.got[i].astype(F32)
            self.whole[0, core, self.own] = total.astype(BF)


def direct_scratch(rows):
    size = axis_sizes()
    peers = size["lo"] * size["y"] * size["hi"] - 1
    return [
        pltpu.VMEM((1, 2, rows, 128), BF),
        pltpu.VMEM((rows, 128), BF),
        pltpu.VMEM((rows, 128), BF),
        pltpu.VMEM((peers, rows // (peers + 1), 128), BF),
        pltpu.SemaphoreType.DMA((2, 2)),
        pltpu.SemaphoreType.DMA((2, peers)),
        pltpu.SemaphoreType.DMA((2, peers)),
    ]


class Small:
    def __init__(self, rank, width, kv_width, heads, kv_heads, head):
        def chunks(lanes):
            return -(-lanes // 128)

        tall = -(-(3 * rank + 2) // 16) * 16
        flat = -(-2 * rank // 16) * 16
        sections = [
            ("down", tall, chunks(width)),
            ("out", flat, chunks(width)),
            ("q_up", -(-rank // 16) * 16, chunks(width)),
            ("kv_up", -(-2 * rank // 16) * 16, chunks(kv_width)),
            ("qmap", head, (heads + 1) // 2),
            ("kmap", head, (kv_heads + 1) // 2),
        ]
        need = sum(rows * n for _, rows, n in sections)
        size = axis_sizes()
        grain = 16 * size["lo"] * size["y"] * size["hi"]
        self.rows = -(-(need + 64) // (2 * grain)) * grain
        self.place = {}
        half, at = 0, 0
        for name, rows, n in sections:
            self.place[name] = []
            for _ in range(n):
                if at + rows > self.rows:
                    half, at = half + 1, 0
                self.place[name].append((half, at, rows))
                at += rows

    def put(self, ref, name, value):
        for c, (half, at, rows) in enumerate(self.place[name]):
            part = value[:, c * 128 : (c + 1) * 128]
            ref[0, half, at : at + part.shape[0], 0 : part.shape[1]] = part.astype(ref.dtype)

    def put_heads(self, ref, name, maps):
        for c, (half, at, rows) in enumerate(self.place[name]):
            pair = [maps[h] for h in range(2 * c, min(2 * c + 2, maps.shape[0]))]
            pair = jnp.concatenate(pair, axis=1) if len(pair) > 1 else pair[0]
            ref[0, half, at : at + rows, 0 : pair.shape[1]] = pair.astype(ref.dtype)

    def take(self, ref, name, lanes):
        parts = [ref[0, half, at : at + rows].astype(F32) for half, at, rows in self.place[name]]
        return jnp.concatenate(parts, axis=1)[:, :lanes]


def widen_kernel(width, high, rank, layout, whole, small, out_in, tok_in, out_out, tok_out, gate, up, down, *outs):
    out_out[...] = out_in[...]
    tok_out[...] = tok_in[...]
    for i, out in enumerate((gate, up, down)):
        for half in range(2):
            out[:, half * 128 : (half + 1) * 128] = whole[0, half, i * width : (i + 1) * width].astype(F32)

    @pl.when(pl.program_id(0) == 0)
    def _():
        pre, post, qd, kd, vd, qu, ku, vu, od, ou, qmap, kmap = outs
        downs = layout.take(small, "down", width)
        for i, out in enumerate((qd, kd, vd)):
            out[...] = downs[i * rank : (i + 1) * rank]
        pre[...] = downs[3 * rank : 3 * rank + 1]
        post[...] = downs[3 * rank + 1 : 3 * rank + 2]
        pair = layout.take(small, "out", width)
        od[...] = pair[:rank]
        ou[...] = pair[rank : 2 * rank]
        qu[...] = layout.take(small, "q_up", width)[:rank]
        pair = layout.take(small, "kv_up", ku.shape[1])
        ku[...] = pair[:rank]
        vu[...] = pair[rank : 2 * rank]
        head = qmap.shape[1]
        for name, out in (("qmap", qmap), ("kmap", kmap)):
            for h in range(out.shape[0]):
                half, at, rows = layout.place[name][h // 2]
                both = small[0, half, at : at + rows].astype(F32)
                out[h] = both[:, (h % 2) * head : (h % 2 + 1) * head]


def row_sum(value):
    return dot(jnp.ones((8, value.shape[1]), BF), value.astype(BF), NT)


def rms(value):
    return lax.rsqrt(jnp.mean(value * value, axis=0, keepdims=True) + EPSILON)


def soft_pair(logit):
    top = jnp.max(logit, axis=0, keepdims=True)
    low = jnp.min(logit, axis=0, keepdims=True)
    up = jnp.exp(logit - top)
    down = jnp.exp(low - logit)
    up = up / jnp.sum(up, axis=0, keepdims=True)
    down = down / jnp.sum(down, axis=0, keepdims=True)
    return jnp.concatenate([up, down], axis=0).astype(BF)


def soft_pair_back(phi, grad):
    half = phi.shape[0] // 2
    up, down = phi[:half].astype(F32), phi[half:].astype(F32)
    gu, gd = grad[:half], grad[half:]
    gu = up * (gu - jnp.sum(up * gu, axis=0, keepdims=True))
    gd = down * (gd - jnp.sum(down * gd, axis=0, keepdims=True))
    return (gu - gd).astype(BF)


def frame(place, span, doc, seg, kept):
    rows, length = doc.shape
    index = place.seq
    high = seg.shape[0]
    more = jnp.zeros((high - rows, span), F32)
    own = doc[:, pl.ds(pl.multiple_of(index * span, span), span)].astype(F32)
    prev = doc[:, pl.ds(pl.multiple_of(jnp.maximum(index - 1, 0) * span, span), span)].astype(F32)
    lane = lax.broadcasted_iota(jnp.int32, (rows, span), 1)
    prev = jnp.where((lane >= span - WINDOW) & (index > 0), prev, 0.0)
    upper = lax.broadcasted_iota(jnp.int32, (span, span), 0) <= lax.broadcasted_iota(jnp.int32, (span, span), 1)
    upper = jnp.where(upper, 1.0, 0.0).astype(BF)
    before = jnp.concatenate([prev, more], axis=0)
    tail = dot(before.astype(BF), upper)
    mine = dot(jnp.concatenate([own, more], axis=0).astype(BF), upper) + jnp.sum(before, axis=1, keepdims=True)
    seg[:, :span] = mine
    seg[:, span:] = tail[:, span - WINDOW :]
    total = jnp.zeros(kept.shape, F32)
    for b in range(length // span):
        at = lax.broadcasted_iota(jnp.int32, (span, 128), 0)
        block = lax.broadcasted_iota(jnp.int32, (span, 128), 1)
        here = jnp.where(at < span - WINDOW, b, b + 1) == block
        marks = jnp.concatenate([doc[:, b * span : (b + 1) * span].astype(F32), more], axis=0)
        total = total + dot(marks.astype(BF), jnp.where(here, 1.0, 0.0).astype(BF))
    kept[...] = jnp.where(total == 0, 1.0, 0.0)


def frame_row(seg, r, span):
    keys = seg[pl.ds(r, 1), :]
    query = keys[:, :span]
    column = jnp.broadcast_to(keys, (8, keys.shape[1])).T[:, :1]
    lane = lax.broadcasted_iota(jnp.int32, keys.shape, 1)
    last = jnp.sum(jnp.where(lane == span - WINDOW - 1, keys, 0.0), axis=1, keepdims=True)
    keep = (keys == last) & ((lane < span - WINDOW) | (lane >= span))
    return query, column, jnp.where(keep, 1.0, 0.0)


def assemble(width, bases, gains, wq, wkv, wo, down, columns):
    qb, kb, vb, ob, qu, ku, vu, ou, qd, kd, vd = bases
    rank = qu.shape[0]
    high = wq.shape[0]
    extra = high - width
    for out, base, up in ((wq, qb, qu), (wo, ob, ou)):
        out[0:width] = base[...]
        rows = jnp.concatenate([2.0 * up[...].astype(F32), jnp.zeros((extra - rank, width), F32)], axis=0)
        out[width:] = rows.astype(BF)
    kv = kb.shape[0]
    wkv[0:kv, 0:width] = kb[...]
    wkv[kv:, 0:width] = vb[...]
    none = jnp.zeros((rank, kv), F32)
    pair = jnp.concatenate(
        [
            jnp.concatenate([none, none], axis=1),
            jnp.concatenate([2.0 * ku[...].astype(F32), none], axis=1),
            jnp.concatenate([none, 2.0 * vu[...].astype(F32)], axis=1),
            jnp.zeros((extra - 3 * rank, 2 * kv), F32),
        ],
        axis=0,
    )
    wkv[:, width:] = pair.T.astype(BF)
    down[...] = jnp.concatenate([qd[...].astype(F32), kd[...].astype(F32), vd[...].astype(F32)], axis=0).astype(BF)
    wide = gains[...]
    wide = jnp.concatenate([wide, jnp.zeros((8 - wide.shape[0], width), F32)], axis=0).T
    columns[0] = wide[:, 0:1]
    columns[1] = wide[:, 1:2]


def qkv_kernel(tok, gain, wq, wkv, down, qkv, normed, inner, tails, ext):
    width = tok.shape[1]
    kv = wkv.shape[0]
    value = tok[0].astype(F32)
    norm = (value * rms(value) * gain[...]).astype(BF)
    normed[0] = norm
    low = dot(down[...], norm).astype(BF)
    inner[0] = low
    ext[0:width] = norm
    ext[width:] = jnp.zeros((ext.shape[0] - width, ext.shape[1]), BF)
    ext[width : width + low.shape[0]] = low
    qkv[0, 0:width] = dot(wq[...], ext[...], TN).astype(BF)
    both = dot(wkv[...], ext[...]).astype(BF)
    qkv[0, width:] = both
    span = tok.shape[2]
    tails[0] = jnp.concatenate(
        [both[: kv // 2, span - WINDOW :], both[kv // 2 :, span - WINDOW :]], axis=1
    )


def aug_value(value):
    extra = lax.broadcasted_iota(jnp.int32, (AUG - value.shape[0], value.shape[1]), 0) == 0
    return jnp.concatenate([value, jnp.where(extra, 1.0, 0.0).astype(BF)], axis=0)


def key_kernel(kv_heads, qkv, tails, kmap, keep, phi, con):
    head = kmap.shape[1]
    first = qkv.shape[1] - 2 * kv_heads * head
    keeping = keep.astype(BF)
    for k in range(kv_heads):
        at = first + k * head
        key = jnp.concatenate([qkv[0, at : at + head], tails[0, k * head : (k + 1) * head, :WINDOW]], axis=1)
        at += kv_heads * head
        val = jnp.concatenate([qkv[0, at : at + head], tails[0, k * head : (k + 1) * head, WINDOW:]], axis=1)
        feat = soft_pair(dot(kmap[k], key, TN))
        phi[0, k] = feat
        con[0, k * AUG : (k + 1) * AUG] = dot(aug_value(val), feat * keeping, NT).astype(BF)


def masks(segq, segk, span):
    extent = segk.shape[0]
    row = lax.broadcasted_iota(jnp.int32, (extent, span), 0)
    pos = jnp.where(row < span, row, row - extent)
    query = lax.broadcasted_iota(jnp.int32, (extent, span), 1)
    same = segk == segq
    far = pos + WINDOW <= query
    return same & far, same & (pos <= query) & jnp.logical_not(far)


def local_kernel(
    kv_heads, group, qkv, tails, phik, frames, qmap, phiq, numer, den, lin_bias, win_bias, between,
):
    head = qmap.shape[1]
    span = qkv.shape[2]
    width = kv_heads * group * head
    segq, segk, _ = frames
    far, near = masks(segq, segk, span)
    lin_bias[...] = jnp.where(far, 1.0, 0.0)
    win_bias[...] = jnp.where(near, 0.0, -1e30)
    for k in range(kv_heads):
        at = width + k * head
        key = jnp.concatenate([qkv[0, at : at + head], tails[0, k * head : (k + 1) * head, :WINDOW]], axis=1)
        at += kv_heads * head
        val = jnp.concatenate([qkv[0, at : at + head], tails[0, k * head : (k + 1) * head, WINDOW:]], axis=1)
        queries, feats = [], []
        for h in range(k * group, (k + 1) * group):
            q = qkv[0, h * head : (h + 1) * head]
            f = soft_pair(dot(qmap[h], q, TN))
            phiq[0, h] = f
            queries.append(q)
            feats.append(f)
        query = jnp.concatenate(queries, axis=1) * (head**-0.5)
        feat = jnp.concatenate(feats, axis=1)
        lin = dot(phik[0, k], feat, TN)
        score = dot(key, query, TN)
        lb = jnp.concatenate([lin_bias[...]] * group, axis=1)
        wb = jnp.concatenate([win_bias[...]] * group, axis=1)
        weights = lin * lb + jnp.exp(score + wb)
        total = jnp.sum(weights, axis=0, keepdims=True)
        out = dot(val, weights.astype(BF))
        for g in range(group):
            h = k * group + g
            numer[0, h * head : (h + 1) * head] = out[:, g * span : (g + 1) * span]
            den[0, h : h + 1] = total[:, g * span : (g + 1) * span]
        between(k)


def join_kernel(
    kv_heads, group, phiq, numer, den_local, state, frames, tok, wo, down, gain,
    mixed, den, middle, normed, inner, ext,
):
    width = tok.shape[1]
    span = tok.shape[2]
    head = width // (kv_heads * group)
    shown = jnp.where(frames[0] == 0, 1.0, 0.0)
    den[0] = jnp.zeros_like(den[0])
    for h in range(kv_heads * group):
        k = h // group
        carried = dot(state[0, k * AUG : (k + 1) * AUG], phiq[0, h]) * shown
        total = den_local[0, h : h + 1] + carried[head : head + 1]
        at = pl.ds(h * head, head)
        ext[at] = ((numer[0, at] + carried[:head]) * (1.0 / total)).astype(BF)
        den[0, h : h + 1] = total
    got = ext[0:width]
    mixed[0] = got
    low = dot(down[...], got).astype(BF)
    inner[0] = low
    ext[width:] = jnp.zeros((ext.shape[0] - width, span), BF)
    ext[width : width + low.shape[0]] = low
    mid = tok[0].astype(F32) + dot(wo[...], ext[...], TN)
    middle[0] = mid
    normed[0] = (mid * rms(mid) * gain[...]).astype(BF)


def forward_kernel(
    rows, kv_heads, group,
    tok, tok_again, doc, gains, qb, kb, vb, ob, qu, ku, vu, ou, qd, kd, vd, od, qmap, kmap,
    qkv_out, normed, inner, tails_out, phik_out, phiq_out, state_out, mixed, den, middle, normed2, inner_o,
    wq, wkv, wo, down, columns,
    seg, kept, ext, qkv, sent, tails, phik, phiq, numer, den_local, lin_bias, win_bias, tail_sem, *refs,
):
    step = pl.program_id(0)
    place = Place()
    chain = Chain(place, False, 2, kept, *refs)
    width, span = tok.shape[1], tok.shape[2]

    def row(ref, r):
        return ref.at[pl.ds(r, 1)]

    def tail_copy(r):
        return remote(sent.at[r], tails.at[r], tail_sem.at[0, r], tail_sem.at[1, r], place.along(1))

    @pl.when(step == 0)
    def _():
        place.greet()

        @pl.when(jnp.logical_not(place.inside(-1)))
        def _():
            tails[...] = jnp.zeros_like(tails)

        frame(place, span, doc, seg, kept)
        assemble(width, (qb, kb, vb, ob, qu, ku, vu, ou, qd, kd, vd), gains, wq, wkv, wo, down, columns)

    @pl.when(step < rows)
    def _():
        qkv_kernel(tok, columns.at[0], wq, wkv, down, row(qkv, step), normed, inner, row(sent, step), ext)
        qkv_out[...] = qkv[pl.ds(step, 1)]

        @pl.when(place.inside(1))
        def _():
            tail_copy(step).start()

    @pl.when((step >= rows) & (step < 2 * rows))
    def _():
        r = step - rows

        @pl.when(place.inside(-1))
        def _():
            tail_copy(r).wait_recv()

        tails_out[...] = tails[pl.ds(r, 1)]
        keep = frame_row(seg, r, span)[2]
        key_kernel(kv_heads, row(qkv, r), row(tails, r), kmap, keep, row(phik, r), row(chain.own, r))
        phik_out[...] = phik[pl.ds(r, 1)]
        chain.turn(r, rows)

    @pl.when((step >= 2 * rows) & (step < 3 * rows))
    def _():
        r = step - 2 * rows

        def between(k):
            if k == kv_heads // 2 - 1:
                chain.turn(rows + 2 * r, rows, False)

        local_kernel(
            kv_heads, group, row(qkv, r), row(tails, r), row(phik, r), frame_row(seg, r, span), qmap,
            row(phiq, r), row(numer, r), row(den_local, r), lin_bias, win_bias, between,
        )
        phiq_out[...] = phiq[pl.ds(r, 1)]
        chain.turn(rows + 2 * r + 1, rows, False)

    @pl.when(step >= 3 * rows)
    def _():
        r = step - 3 * rows
        state_out[...] = chain.result[pl.ds(r, 1)]
        join_kernel(
            kv_heads, group, row(phiq, r), row(numer, r), row(den_local, r), row(chain.result, r),
            frame_row(seg, r, span), tok_again, wo, od, columns.at[1],
            mixed, den, middle, normed2, inner_o, ext,
        )

    @pl.when(step == 4 * rows - 1)
    def _():
        chain.close(rows)

        @pl.when(place.inside(1))
        def _():
            for r in range(rows):
                tail_copy(r).wait_send()


def ff_kernel(
    width, normed_h, cot_h, middle, gain, gate_h, up_h, down_h,
    hid_out, grad_mid, grad_gain, shards,
    normed, cot, gate_v, up_v, down_v, hid, dgate, dup, sem, act_sem, hid_sem, *refs,
):
    step = pl.program_id(0)
    rows = normed_h.shape[0]
    span = normed_h.shape[2]
    high = normed.shape[0]
    hidden = gate_h.shape[1]
    tiles = hidden // TILE
    place = Place()
    scatter = Scatter(place, 3 * width, refs)

    def act_copies():
        made = []
        for r in range(rows):
            at = pl.ds(r * span, span)
            made.append(pltpu.make_async_copy(normed_h.at[r], normed.at[0:width, at], act_sem.at[r, 0]))
            made.append(pltpu.make_async_copy(cot_h.at[r], cot.at[0:width, at], act_sem.at[r, 1]))
        return made

    def tile_copies(j):
        at = pl.ds(pl.multiple_of(j * TILE, TILE), TILE)
        return [
            pltpu.make_async_copy(gate_h.at[:, at], gate_v.at[0:width, at], sem.at[j, 0]),
            pltpu.make_async_copy(up_h.at[:, at], up_v.at[0:width, at], sem.at[j, 1]),
            pltpu.make_async_copy(down_h.at[:, at], down_v.at[0:width, at], sem.at[j, 2]),
        ]

    @pl.when(step == 0)
    def _():
        place.greet()
        for copy in act_copies():
            copy.start()
        for j in range(tiles):
            for copy in tile_copies(j):
                copy.start()
        for ref in (gate_v, up_v, down_v):
            ref[width:] = jnp.zeros((high - width, hidden), BF)
        for ref in (normed, cot):
            ref[width:] = jnp.zeros((high - width, rows * span), BF)
        for copy in act_copies():
            copy.wait()

    @pl.when(step < tiles)
    def _():
        for copy in tile_copies(step):
            copy.wait()
        at = pl.ds(pl.multiple_of(step * TILE, TILE), TILE)
        gate, up, down = gate_v[:, at], up_v[:, at], down_v[:, at]
        for r in range(rows):
            lane = pl.ds(r * span, span)
            n2 = normed[:, lane]
            g = dot(gate, n2, TN)
            u = dot(up, n2, TN)
            dh = dot(down, cot[:, lane], TN).astype(BF).astype(F32)
            sig = 1.0 / (1.0 + jnp.exp(-g))
            act = g * sig
            hid[at, lane] = (act * u).astype(BF)
            dup[at, lane] = (dh * act).astype(BF)
            dgate[at, lane] = (dh * u * (sig + act * (1.0 - sig))).astype(BF)
        slot = step % 2
        for i, (left, right) in enumerate(((normed, dgate), (normed, dup), (cot, hid))):
            grad = dot(left[...], right[at, :], NT)[:width].astype(BF)
            for half in range(2):
                scatter.mine[slot, half, i * width : (i + 1) * width] = grad[:, half * 128 : (half + 1) * 128]

    @pl.when(step >= tiles)
    def _():
        r = step - tiles
        lane = pl.ds(pl.multiple_of(r * span, span), span)
        back = dot(gate_v[0:width], dgate[:, lane]) + dot(up_v[0:width], dup[:, lane])
        mid = middle[0]
        scale = rms(mid)
        unit = back * mid
        column = gain[0]
        pull = jnp.mean(unit * column, axis=0, keepdims=True) * (scale * scale * scale)
        grad_mid[0] = cot[0:width, lane].astype(F32) + (back * column) * scale - mid * pull

        @pl.when(r == 0)
        def _():
            grad_gain[...] = jnp.zeros_like(grad_gain)

        grad_gain[...] += row_sum(unit * scale)

        @pl.when(r == 0)
        def _():
            pltpu.make_async_copy(hid, hid_out, hid_sem).start()

        @pl.when(r == rows - 1)
        def _():
            pltpu.make_async_copy(hid, hid_out, hid_sem).wait()

    def into(tile, stream, total):
        shards[tile, stream, 0 : total.shape[0]] = total.astype(BF)

    scatter.turn(step, tiles, into)


def pull_kernel(
    kv_heads, group, grad_mid, mixed, den, phiq, frames, inner, wo, down,
    dnum, dden, dstate, gup, gdown,
):
    width = mixed.shape[1]
    span = mixed.shape[2]
    head = width // (kv_heads * group)
    low = inner.shape[1]

    branch = grad_mid[0].astype(BF)
    wide = dot(wo[...], branch)
    grad_inner = wide[width : width + low].astype(BF)
    grad = (wide[:width] + dot(down[...], grad_inner, TN)).astype(BF).astype(F32)
    gup[...] += 2.0 * dot(inner[0], branch, NT)
    gdown[...] += dot(grad_inner, mixed[0], NT)
    shown = jnp.where(frames[0] == 0, 1.0, 0.0)
    dden[0] = jnp.zeros_like(dden[0])
    pad = jnp.zeros((AUG - head - 1, span), F32)
    for k in range(kv_heads):
        total = None
        for g in range(group):
            h = k * group + g
            at = pl.ds(h * head, head)
            dm = grad[h * head : (h + 1) * head]
            inv = 1.0 / den[0, h : h + 1]
            dd = -jnp.sum(dm * mixed[0, at].astype(F32), axis=0, keepdims=True) * inv
            dn = (dm * inv).astype(BF)
            dnum[0, at] = dn
            dden[0, h : h + 1] = dd
            aug = (jnp.concatenate([dn.astype(F32), dd, pad], axis=0) * shown).astype(BF)
            part = dot(aug, phiq[0, h], NT)
            total = part if total is None else total + part
        dstate[0, k * AUG : (k + 1) * AUG] = total.astype(BF)


def back_kernel(
    kv_heads, group, qkv, tails, phik, phiq, state, dcon, dnum, dden, frames, qmap, kmap,
    dq_out, dkv_out, dtails, gqmap, gkmap, lin_bias, win_bias, between,
):
    head = qmap.shape[1]
    width = dq_out.shape[1]
    span = dq_out.shape[2]
    scale = head**-0.5

    far, near = masks(frames[0], frames[1], span)
    lin_bias[...] = jnp.where(far, 1.0, 0.0)
    win_bias[...] = jnp.where(near, 0.0, -1e30)
    shown = jnp.where(frames[0] == 0, 1.0, 0.0)
    shown3 = jnp.concatenate([shown] * group, axis=1)
    keeping = frames[2]
    pad = jnp.zeros((AUG - head - 1, group * span), F32)
    for k in range(kv_heads):
        at = width + k * head
        key = jnp.concatenate([qkv[0, at : at + head], tails[0, k * head : (k + 1) * head, :WINDOW]], axis=1)
        at += kv_heads * head
        val = jnp.concatenate([qkv[0, at : at + head], tails[0, k * head : (k + 1) * head, WINDOW:]], axis=1)
        hs = range(k * group, (k + 1) * group)
        queries = [qkv[0, h * head : (h + 1) * head] for h in hs]
        query = jnp.concatenate(queries, axis=1) * scale
        feat = jnp.concatenate([phiq[0, h] for h in hs], axis=1)
        dn = jnp.concatenate([dnum[0, h * head : (h + 1) * head] for h in hs], axis=1)
        dd = jnp.concatenate([dden[0, h : h + 1] for h in hs], axis=1)
        kfeat = phik[0, k]
        lb = jnp.concatenate([lin_bias[...]] * group, axis=1)
        wb = jnp.concatenate([win_bias[...]] * group, axis=1)
        growth = jnp.exp(dot(key, query, TN) + wb)
        weights = (dot(kfeat, feat, TN) * lb + growth).astype(BF)
        dw = dot(val, dn, TN) + dd
        dlin = (dw * lb).astype(BF)
        dscore = (dw * growth).astype(BF)
        dv = dot(dn, weights, NT)
        aug = (jnp.concatenate([dn.astype(F32), dd, pad], axis=0) * shown3).astype(BF)
        held = state[0, k * AUG : (k + 1) * AUG]
        dfeat = dot(kfeat, dlin) + dot(held, aug, TN)
        con = dcon[0, k * AUG : (k + 1) * AUG]
        dkfeat = dot(feat, dlin, NT) + dot(con, aug_value(val), TN) * keeping
        dv = dv + dot(con[:head], kfeat * keeping.astype(BF))
        dq = dot(key, dscore) * scale
        dk = dot(query, dscore, NT)
        dt = soft_pair_back(feat, dfeat.astype(BF).astype(F32))
        for g in range(group):
            h = k * group + g
            part = dt[:, g * span : (g + 1) * span]
            gqmap[h] += dot(queries[g], part, NT)
            full = dq[:, g * span : (g + 1) * span] + dot(qmap[h], part)
            dq_out[0, h * head : (h + 1) * head] = full.astype(BF)
        dtk = soft_pair_back(kfeat, dkfeat.astype(BF).astype(F32))
        gkmap[k] += dot(key, dtk, NT)
        dk = dk + dot(kmap[k], dtk)
        ks, vs = k * head, (kv_heads + k) * head
        dkv_out[0, ks : ks + head] = dk[:, :span]
        dkv_out[0, vs : vs + head] = dv[:, :span]
        dtails[0, ks : ks + head] = jnp.concatenate([dk[:, span:], dv[:, span:]], axis=1).astype(BF)
        between(k)


def final_kernel(
    tok, grad_mid, gain, dq, dkv, returned, normed, inner, wq, wkv, down,
    grad_tok, ggain, gdown, gup,
):
    width = tok.shape[1]
    span = tok.shape[2]
    low = down.shape[0]

    got = returned[0].astype(F32)
    got = jnp.concatenate([got[:, :WINDOW], got[:, WINDOW:]], axis=0)
    own = dkv[0]
    both = jnp.concatenate([own[:, : span - WINDOW], own[:, span - WINDOW :] + got], axis=1).astype(BF)
    grad_q = dq[0]
    wide = dot(wq[...], grad_q) + dot(wkv[...], both, TN)
    grad_inner = wide[width : width + low].astype(BF)
    back = wide[:width] + dot(down[...], grad_inner, TN)
    gdown[...] += dot(grad_inner, normed[0], NT)
    gup[:, :width] += 2.0 * dot(inner[0], grad_q, NT)
    gup[:, width:] += 2.0 * dot(inner[0], both, NT)
    value = tok[0].astype(F32)
    scale = rms(value)
    unit = value * scale
    grad_unit = back * gain[...]
    ggain[...] += row_sum(back * unit)
    grad_tok[0] = grad_mid[0] + scale * (
        grad_unit - unit * jnp.mean(grad_unit * unit, axis=0, keepdims=True)
    )


def backward_kernel(
    rows, kv_heads, group, tiles, shard_rows, layout,
    doc, grad_mid_p, mixed, den, phiq_p, inner_o, wo, odown,
    qkv, tails, phik, phiq, state, qmap, kmap,
    tok, grad_mid, normed, inner, gain, wq, wkv, down, gpost, shards, hid_h, down_h, middle_h,
    grad_tok, whole, small_out, layer_out,
    dnum, dden, dq, dkv, dtails, returned, gup_o, gdown_o, gqmap, gkmap, ggain, gdown, gup, lin_bias, win_bias,
    seg, kept, tail_sem, small, hid, down_v, middle, out, in_sem, out_sem, *refs,
):
    step = pl.program_id(0)
    early = 3
    place = Place()
    chain = Chain(place, True, 1, kept, *refs[:9])
    refs = refs[9:]
    n_gather = len(gather_scratch(shard_rows, tiles))
    gather = Gather(place, shard_rows, shards, whole, refs[:n_gather])
    direct = Direct(place, small, *refs[n_gather:])

    def row(ref, r):
        return ref.at[pl.ds(r, 1)]

    def tail_copy(r):
        return remote(dtails.at[r], returned.at[r], tail_sem.at[0, r], tail_sem.at[1, r], place.along(-1))

    def fetches():
        pairs = ((hid_h, hid), (down_h, down_v), (middle_h, middle))
        return [pltpu.make_async_copy(src, dst, in_sem.at[i]) for i, (src, dst) in enumerate(pairs)]

    def out_copy(r):
        return pltpu.make_async_copy(out.at[r], layer_out.at[r], out_sem.at[r])

    def make_out(r):
        lane = slice(r * tok.shape[2], (r + 1) * tok.shape[2])
        out[r] = (middle[r] + dot(down_v[...], hid[:, lane])).astype(BF)
        out_copy(r).start()

    @pl.when(step == 0)
    def _():
        for copy in fetches():
            copy.start()
        place.greet(True)
        frame(place, tok.shape[2], doc, seg, kept)
        for ref in (gup_o, gdown_o, gqmap, gkmap, ggain, gdown, gup):
            ref[...] = jnp.zeros_like(ref)

        @pl.when(jnp.logical_not(place.inside(1)))
        def _():
            returned[...] = jnp.zeros_like(returned)

    @pl.when(step < rows)
    def _():
        pull_kernel(
            kv_heads, group, grad_mid_p, mixed, den, phiq_p, frame_row(seg, step, tok.shape[2]), inner_o, wo, odown,
            row(dnum, step), row(dden, step), row(chain.own, step), gup_o, gdown_o,
        )

    @pl.when((step >= rows) & (step < 2 * rows))
    def _():
        r = step - rows

        def between(k):
            if k == kv_heads // 2:

                @pl.when(r % 2 == 1)
                def _():
                    gather.turn(early + r + r // 2, tiles)

        back_kernel(
            kv_heads, group, qkv, tails, phik, phiq, state, row(chain.result, r), row(dnum, r), row(dden, r),
            frame_row(seg, r, tok.shape[2]), qmap, kmap,
            row(dq, r), row(dkv, r), row(dtails, r), gqmap, gkmap, lin_bias, win_bias, between,
        )

        @pl.when(place.inside(-1))
        def _():
            tail_copy(r).start()

    @pl.when(step >= 2 * rows)
    def _():
        r = step - 2 * rows

        @pl.when(place.inside(1))
        def _():
            tail_copy(r).wait_recv()

        final_kernel(
            tok, grad_mid, gain.at[0], row(dq, r), row(dkv, r), row(returned, r), normed, inner, wq, wkv, down,
            grad_tok, ggain, gdown, gup,
        )

    chain.turn(step, rows)

    r = step - rows
    late = early + rows + rows // 2
    turn = jnp.where(step < rows, step - (rows - early), jnp.where(r < rows, early + r + (r + 1) // 2, late + (r - rows) // 2))

    @pl.when((step >= rows - early) & ((r < rows) | ((r - rows) % 2 == 0)))
    def _():
        gather.turn(turn, tiles)

    @pl.when(step == 3 * rows - 1)
    def _():
        chain.close(rows)

        @pl.when(place.inside(-1))
        def _():
            for r in range(rows):
                tail_copy(r).wait_send()

        rank = gdown_o.shape[0]
        width = gdown_o.shape[1]
        kv_width = kv_heads * qmap.shape[1]
        mine = direct.mine
        mine[...] = jnp.zeros_like(mine)
        pad = [jnp.zeros((6, width), F32)]
        layout.put(mine, "down", jnp.concatenate([gdown[...], ggain[0:1], gpost[0:1]] + pad, axis=0))
        layout.put(mine, "out", jnp.concatenate([gdown_o[...], gup_o[...]], axis=0))
        layout.put(mine, "q_up", jnp.concatenate([gup[0:rank, :width], jnp.zeros((rank, width), F32)], axis=0))
        layout.put(
            mine, "kv_up",
            jnp.concatenate(
                [gup[rank : 2 * rank, width : width + kv_width], gup[2 * rank :, width + kv_width :]], axis=0
            ),
        )
        layout.put_heads(mine, "qmap", gqmap)
        layout.put_heads(mine, "kmap", gkmap)

        turns = list(range(late + rows // 2 + 1, tiles + WAYS[0]))
        for copy in fetches():
            copy.wait()
        shares = [list(range(rows))[n::4] for n in range(4)]
        for k in range(4):
            direct.start(k)
            for r in shares[k]:
                make_out(r)
            for turn in turns[k : k + 1] if k < 3 else turns[3:]:
                gather.turn(jnp.int32(turn), tiles)
            direct.finish(k)
        small_out[...] = small[...]
        for r in range(rows):
            out_copy(r).wait()


def row_spec(*shape):
    zeros = (0,) * len(shape)
    return pl.BlockSpec((1,) + shape, lambda r: (r,) + zeros)


def whole_spec(*shape):
    zeros = (0,) * len(shape)
    return pl.BlockSpec(shape, lambda r: zeros, pipeline_mode=pl.Buffered(1))


def shape_of(shape, kind):
    return jax.ShapeDtypeStruct(shape, kind)


def body(
    tokens, doc_starts, pregain, query_base, key_base, value_base, output_base, query_down, query_up,
    key_down, key_up, value_down, value_up, out_down, out_up, query_map, key_map, postgain, gate_proj,
    up_proj, down_proj, cotangent,
):
    rows, span, width = tokens.shape
    heads, head, _ = query_map.shape
    kv_heads = key_map.shape[0]
    group = heads // kv_heads
    kv_width = kv_heads * head
    rank = query_up.shape[0]
    extent = span + WINDOW
    hidden = gate_proj.shape[1]
    tiles = hidden // TILE
    high = -(-width // 256) * 256
    feats = 2 * head
    slots = -(-heads // 8) * 8

    tok = jnp.swapaxes(tokens, 1, 2)
    cot = jnp.swapaxes(cotangent, 1, 2)
    gains = jnp.stack([pregain, postgain]).astype(F32)
    odown = out_down.T

    def phase_spec(shape, phase):
        tail = (0,) * (len(shape) - 1)
        return pl.BlockSpec((1,) + tuple(shape[1:]), lambda s: (jnp.clip(s - phase * rows, 0, rows - 1),) + tail)

    args = [
        (tok, 0), (tok, 3), (doc_starts, None), (gains, None), (query_base, None), (key_base.T, None),
        (value_base.T, None), (output_base, None), (query_up, None), (key_up, None), (value_up, None),
        (out_up, None), (query_down.T, None), (key_down.T, None), (value_down.T, None), (odown, None),
        (query_map, None), (key_map, None),
    ]
    made = [
        ((rows, width + 2 * kv_width, span), BF, 0),
        ((rows, width, span), BF, 0),
        ((rows, 3 * rank, span), BF, 0),
        ((rows, kv_width, 2 * WINDOW), BF, 1),
        ((rows, kv_heads, feats, extent), BF, 1),
        ((rows, heads, feats, span), BF, 2),
        ((rows, kv_heads * AUG, feats), BF, 3),
        ((rows, width, span), BF, 3),
        ((rows, slots, span), F32, 3),
        ((rows, width, span), F32, 3),
        ((rows, width, span), BF, 3),
        ((rows, rank, span), BF, 3),
        ((high, width), BF, None),
        ((2 * kv_width, high), BF, None),
        ((high, width), BF, None),
        ((3 * rank, width), BF, None),
        ((2, width, 1), F32, None),
    ]
    biases = [pltpu.VMEM((extent, span), F32)] * 2
    frame_scratch = [pltpu.VMEM((8, extent), F32), pltpu.VMEM((8, 128), F32)]
    (
        qkv, normed, inner, tails, phik, phiq, state, mixed, den, middle, normed2, inner_o, wq, wkv, wo, down, columns,
    ) = pl.pallas_call(
        functools.partial(forward_kernel, rows, kv_heads, group),
        grid=(4 * rows,),
        in_specs=[whole_spec(*a.shape) if phase is None else phase_spec(a.shape, phase) for a, phase in args],
        out_specs=tuple(
            pl.BlockSpec(shape, functools.partial(lambda n, s: (0,) * n, len(shape)))
            if phase is None
            else phase_spec(shape, phase)
            for shape, _, phase in made
        ),
        out_shape=tuple(shape_of(shape, kind) for shape, kind, _ in made),
        scratch_shapes=frame_scratch
        + [
            pltpu.VMEM((high, span), BF),
            pltpu.VMEM((rows, width + 2 * kv_width, span), BF),
            pltpu.VMEM((rows, kv_width, 2 * WINDOW), BF),
            pltpu.VMEM((rows, kv_width, 2 * WINDOW), BF),
            pltpu.VMEM((rows, kv_heads, feats, extent), BF),
            pltpu.VMEM((rows, heads, feats, span), BF),
            pltpu.VMEM((rows, width, span), F32),
            pltpu.VMEM((rows, slots, span), F32),
        ]
        + biases
        + [pltpu.SemaphoreType.DMA((2, rows))]
        + chain_scratch(rows, kv_heads * AUG, feats),
        compiler_params=pltpu.CompilerParams(vmem_limit_bytes=VMEM, collective_id=2, has_side_effects=True),
    )(*[a for a, _ in args])

    last = lambda s: (jnp.maximum(s - tiles, 0), 0, 0)
    fixed = lambda s: (0, 0)
    anywhere = pl.BlockSpec(memory_space=pl.ANY)
    shard_shape = (tiles, len(stream_plan(3 * width)), shard_rows(3 * width), 128)
    hid, grad_mid, gpost, shards = pl.pallas_call(
        functools.partial(ff_kernel, width),
        grid=(tiles + rows,),
        in_specs=[anywhere, anywhere, pl.BlockSpec((1, width, span), last), pl.BlockSpec((1, width, 1), lambda s: (1, 0, 0))]
        + [anywhere] * 3,
        out_specs=(
            anywhere,
            pl.BlockSpec((1, width, span), last),
            pl.BlockSpec((8, width), fixed),
            pl.BlockSpec(shard_shape, lambda s: (0, 0, 0, 0)),
        ),
        out_shape=(
            shape_of((hidden, rows * span), BF),
            shape_of((rows, width, span), F32),
            shape_of((8, width), F32),
            shape_of(shard_shape, BF),
        ),
        scratch_shapes=[pltpu.VMEM((high, rows * span), BF)] * 2
        + [pltpu.VMEM((high, hidden), BF)] * 3
        + [pltpu.VMEM((hidden, rows * span), BF)] * 3
        + [pltpu.SemaphoreType.DMA((tiles, 3)), pltpu.SemaphoreType.DMA((rows, 2)), pltpu.SemaphoreType.DMA(())]
        + scatter_scratch(3 * width, BF),
        compiler_params=pltpu.CompilerParams(vmem_limit_bytes=VMEM, collective_id=0, has_side_effects=True),
    )(normed2, cot, middle, columns, gate_proj, up_proj, down_proj.T)

    layout = Small(rank, width, kv_width, heads, kv_heads, head)
    args = [(doc_starts, None)]
    args += [(a, 0) for a in (grad_mid, mixed, den, phiq, inner_o)] + [(wo, None), (odown, None)]
    args += [(a, 1) for a in (qkv, tails, phik, phiq, state)] + [(query_map, None), (key_map, None)]
    args += [(a, 2) for a in (tok, grad_mid, normed, inner)] + [(a, None) for a in (columns, wq, wkv, down, gpost)]
    specs = [whole_spec(*a.shape) if phase is None else phase_spec(a.shape, phase) for a, phase in args]
    args = [a for a, _ in args]
    args += [shards, hid, down_proj.T, middle]
    specs += [anywhere] * 4
    last = lambda s: (jnp.maximum(s - 2 * rows, 0), 0, 0)
    grad_tok, whole, small, layer_out = pl.pallas_call(
        functools.partial(backward_kernel, rows, kv_heads, group, tiles, 3 * width, layout),
        grid=(3 * rows,),
        in_specs=specs,
        out_specs=(
            pl.BlockSpec((1, width, span), last),
            anywhere,
            pl.BlockSpec((1, 2, layout.rows, 128), lambda s: (0, 0, 0, 0)),
            anywhere,
        ),
        out_shape=(
            shape_of((rows, width, span), F32),
            shape_of((tiles, 2, 3 * width, 128), BF),
            shape_of((1, 2, layout.rows, 128), BF),
            shape_of((rows, width, span), BF),
        ),
        scratch_shapes=[
            pltpu.VMEM((rows, width, span), BF),
            pltpu.VMEM((rows, slots, span), F32),
            pltpu.VMEM((rows, width, span), BF),
            pltpu.VMEM((rows, 2 * kv_width, span), F32),
            pltpu.VMEM((rows, kv_width, 2 * WINDOW), BF),
            pltpu.VMEM((rows, kv_width, 2 * WINDOW), BF),
            pltpu.VMEM((rank, width), F32),
            pltpu.VMEM((rank, width), F32),
            pltpu.VMEM((heads, head, head), F32),
            pltpu.VMEM((kv_heads, head, head), F32),
            pltpu.VMEM((8, width), F32),
            pltpu.VMEM((3 * rank, width), F32),
            pltpu.VMEM((3 * rank, width + 2 * kv_width), F32),
        ]
        + biases
        + frame_scratch
        + [
            pltpu.SemaphoreType.DMA((2, rows)),
            pltpu.VMEM((1, 2, layout.rows, 128), BF),
            pltpu.VMEM((hidden, rows * span), BF),
            pltpu.VMEM((width, hidden), BF),
            pltpu.VMEM((rows, width, span), F32),
            pltpu.VMEM((rows, width, span), BF),
            pltpu.SemaphoreType.DMA((3,)),
            pltpu.SemaphoreType.DMA((rows,)),
        ]
        + chain_scratch(rows, kv_heads * AUG, feats)
        + gather_scratch(3 * width, tiles)
        + direct_scratch(layout.rows),
        compiler_params=pltpu.CompilerParams(vmem_limit_bytes=VMEM, collective_id=1, has_side_effects=True),
    )(*args)

    column = pl.BlockSpec((width, TILE), lambda j: (0, j))
    flat = [(1, width)] * 2 + [(rank, width)] * 4 + [(rank, kv_width)] * 2 + [(rank, width)] * 2
    flat += [query_map.shape, key_map.shape]
    pieces = next(n for n in range(tiles // rows, 0, -1) if width % (16 * n) == 0 and tiles >= n * rows)
    part = pl.BlockSpec(
        (1, width // pieces, span),
        lambda j: (jnp.minimum(j // pieces, rows - 1), jnp.where(j < rows * pieces, j % pieces, pieces - 1), 0),
    )
    outs = pl.pallas_call(
        functools.partial(widen_kernel, width, high, rank, layout),
        grid=(tiles,),
        in_specs=[
            pl.BlockSpec((1, 2, 3 * width, 128), lambda j: (j, 0, 0, 0)),
            pl.BlockSpec((1, 2, layout.rows, 128), lambda j: (0, 0, 0, 0)),
            part,
            part,
        ],
        out_specs=(part, part)
        + (column,) * 3
        + tuple(pl.BlockSpec(f, functools.partial(lambda n, j: (0,) * n, len(f))) for f in flat),
        out_shape=(shape_of(layer_out.shape, BF), shape_of(grad_tok.shape, F32))
        + (shape_of((width, hidden), F32),) * 3
        + tuple(shape_of(f, F32) for f in flat),
        compiler_params=pltpu.CompilerParams(vmem_limit_bytes=VMEM),
    )(whole, small, layer_out, grad_tok)
    layer_out, grad_tok, gate, up, down_t, pre, post, qd, kd, vd, qu, ku, vu, od, ou, gq, gk = outs
    return (
        jnp.swapaxes(layer_out, 1, 2),
        jnp.swapaxes(grad_tok, 1, 2),
        pre[0],
        qd.T,
        qu,
        kd.T,
        ku,
        vd.T,
        vu,
        od.T,
        ou,
        gq,
        gk,
        post[0],
        gate,
        up,
        down_t.T,
    )


def solution(mesh):
    wide = P("batch", "seq", None)
    return jax.shard_map(
        body,
        mesh=mesh,
        in_specs=(wide, P("batch", None)) + (P(),) * 19 + (wide,),
        out_specs=(wide, wide) + (P(),) * 15,
        check_vma=False,
    )
```

```python
import functools

import jax
import jax.numpy as jnp
from jax import lax
from jax.experimental import pallas as pl
from jax.experimental.pallas import tpu as pltpu
from jax.sharding import PartitionSpec as P

WINDOW = 64
EPSILON = 1e-05
BF = jnp.bfloat16
F32 = jnp.float32
NN = (((1,), (0,)), ((), ()))
NT = (((1,), (1,)), ((), ()))
TN = (((0,), (0,)), ((), ()))
HI = 4
TILE = 256
AUG = 80
VMEM = 62 << 20
MESH = pl.DeviceIdType.MESH


def dot(left, right, dims=NN):
    return lax.dot_general(left, right, dims, preferred_element_type=F32)


def split_seq(index, count):
    low = max(count // HI, 1)
    return index // low, index % low, count // low, low


class Place:
    def __init__(self):
        batch, seq = lax.axis_index("batch"), lax.axis_index("seq")
        n_seq = lax.axis_size("seq")
        hi, lo, n_hi, n_lo = split_seq(seq, n_seq)
        self.batch, self.seq = batch, seq
        self.at = {"core": batch % 2, "y": batch // 2, "hi": hi, "lo": lo}
        self.size = axis_sizes()

    def peer(self, axis, distance):
        at = dict(self.at)
        at[axis] = (at[axis] + distance) % self.size[axis]
        return (at["y"] * 2 + at["core"], at["hi"] * self.size["lo"] + at["lo"])

    def along(self, distance):
        return (self.batch, self.seq + distance)

    def inside(self, distance):
        return (self.seq + distance >= 0) & (self.seq + distance < self.size["hi"] * self.size["lo"])

    def others(self):
        size = self.size
        return [
            (a, b, c)
            for a in range(size["lo"])
            for b in range(size["y"])
            for c in range(size["hi"])
            if a or b or c
        ]

    def other(self, offset):
        at = [(self.at[n] + d) % self.size[n] for n, d in zip(("lo", "y", "hi"), offset)]
        number = (at[0] * self.size["y"] + at[1]) * self.size["hi"] + at[2]
        return (at[1] * 2 + self.at["core"], at[2] * self.size["lo"] + at[0]), number

    def greet(self, everyone=False):
        barrier = pltpu.get_barrier_semaphore()
        total = 0
        for d in (-1, 1):

            @pl.when(self.inside(d))
            def _():
                pl.semaphore_signal(barrier, inc=1, device_id=self.along(d), device_id_type=MESH)

            total = total + jnp.where(self.inside(d), 1, 0)
        peers = [self.peer("core", 1)]
        if everyone:
            peers += [self.other(offset)[0] for offset in self.others()]
        else:
            peers += [self.peer(axis, d) for axis in ("lo", "y", "hi") for d in range(1, self.size[axis])]
        for peer in peers:
            pl.semaphore_signal(barrier, inc=1, device_id=peer, device_id_type=MESH)
            total = total + 1
        pl.semaphore_wait(barrier, total)


def axis_sizes():
    _, _, n_hi, n_lo = split_seq(0, lax.axis_size("seq"))
    return {"core": 2, "y": lax.axis_size("batch") // 2, "hi": n_hi, "lo": n_lo}


def stream_plan(rows):
    size = axis_sizes()
    grain = 16 * size["lo"] * size["y"] * size["hi"]
    part = rows // (2 * grain) * grain
    plan = []
    for i, order in enumerate((("lo", "y", "hi"), ("y", "lo", "hi"))):
        left, stages = part, []
        for axis in order:
            left = left // size[axis]
            stages.append((axis, left, True))
        plan.append((i * part, part, stages))
    rest = rows - 2 * part
    if rest:
        left = rest // size["hi"]
        plan.append((2 * part, rest, [("hi", left, True), ("lo", left, False), ("y", left, False)]))
    return plan


def shard_rows(rows):
    return max(stages[-1][1] for _, _, stages in stream_plan(rows))


def remote(src, dst, send, recv, peer):
    return pltpu.make_async_remote_copy(
        src_ref=src, dst_ref=dst, send_sem=send, recv_sem=recv, device_id=peer, device_id_type=MESH
    )


LAGS = (1, 3, 4, 5)


def stage_slots(k, slots):
    return 2 * slots if k == 1 else slots


def scatter_scratch(rows, kind, slots=2):
    size = axis_sizes()
    made = [
        pltpu.VMEM((slots, 2, rows, 128), kind),
        pltpu.VMEM((slots, rows, 128), kind),
        pltpu.VMEM((stage_slots(1, slots), rows, 128), kind),
        pltpu.SemaphoreType.DMA((2, slots)),
    ]
    for _, _, stages in stream_plan(rows):
        for k, (axis, left, _) in enumerate(stages, 1):
            peers = max(size[axis] - 1, 1)
            made.append(pltpu.VMEM((stage_slots(k, slots), peers, left, 128), kind))
            made.append(pltpu.VMEM((slots, left, 128), kind))
            made.append(pltpu.SemaphoreType.DMA((2, stage_slots(k, slots), peers)))
    return made


class Scatter:
    def __init__(self, place, rows, refs, slots=2):
        self.place, self.rows, self.slots = place, rows, slots
        self.mine, self.other, self.base, self.core_sem = refs[:4]
        self.streams = []
        at = 4
        for first, part, stages in stream_plan(rows):
            made = []
            for axis, left, divides in stages:
                made.append((axis, left) + tuple(refs[at : at + 3]) + (divides,))
                at += 3
            self.streams.append((first, part, made))

    def core_copy(self, t):
        slot = t % self.slots
        core = self.place.at["core"]
        return remote(
            self.mine.at[slot, 1 - core], self.other.at[slot],
            self.core_sem.at[0, slot], self.core_sem.at[1, slot], self.place.peer("core", 1),
        )

    def copies(self, k, t):
        slot = t % stage_slots(k, self.slots)
        made = []
        for first, part, stages in self.streams:
            axis, left, got, _, sem, divides = stages[k - 1]
            size = self.place.size[axis]
            for d in range(1, size):
                to = (self.place.at[axis] + d) % size if divides else 0
                if k == 1:
                    src = self.base.at[slot, pl.ds(pl.multiple_of(first + to * left, 16), left)]
                else:
                    src = stages[k - 2][3].at[t % self.slots, pl.ds(pl.multiple_of(to * left, 16), left)]
                made.append(
                    remote(
                        src, got.at[slot, d - 1], sem.at[0, slot, d - 1], sem.at[1, slot, d - 1],
                        self.place.peer(axis, d),
                    )
                )
        return made

    def start(self, k, t):
        for copy in [self.core_copy(t)] if k == 0 else self.copies(k, t):
            copy.start()

    def finish(self, k, t, into=None):
        slot = t % self.slots
        ahead = t % stage_slots(k, self.slots)
        if k == 0:
            self.core_copy(t).wait()
            core = self.place.at["core"]
            total = self.mine[slot, core].astype(F32) + self.other[slot].astype(F32)
            self.base[t % stage_slots(1, self.slots)] = total.astype(self.base.dtype)
            return
        for copy in self.copies(k, t):
            copy.wait()
        for i, (first, part, stages) in enumerate(self.streams):
            axis, left, got, out, _, divides = stages[k - 1]
            size = self.place.size[axis]
            at = self.place.at[axis] * left if divides else 0
            if k == 1:
                own = self.base[ahead, pl.ds(pl.multiple_of(first + at, 16), left)]
            else:
                own = stages[k - 2][3][slot, pl.ds(pl.multiple_of(at, 16), left)]
            if divides or size == 2:
                total = own.astype(F32)
                for d in range(1, size):
                    total = total + got[ahead, d - 1].astype(F32)
            else:
                total = jnp.zeros(own.shape, F32)
                for p in range(size):
                    d = (self.place.at[axis] - p) % size
                    part = jnp.where(d == 0, own, got[ahead, jnp.maximum(d - 1, 0)])
                    total = total + part.astype(F32)
            if k == 3:
                into(i, total)
            else:
                out[slot] = total.astype(out.dtype)

    def turn(self, step, tiles, into):
        for k in (3, 2, 1, 0):
            t = step - LAGS[k]

            @pl.when((t >= 0) & (t < tiles))
            def _():
                self.finish(k, t, functools.partial(into, t))
                if k < 3:
                    self.start(k + 1, t)

        @pl.when(step < tiles)
        def _():
            self.start(0, step)


WAYS = (6, 5, 3, 1)


def gather_scratch(rows, tiles):
    size = axis_sizes()
    made = [pltpu.SemaphoreType.DMA((2, tiles)), pltpu.SemaphoreType.DMA((tiles, len(stream_plan(rows))))]
    for _, _, stages in stream_plan(rows):
        for axis, left, _ in stages:
            made.append(pltpu.SemaphoreType.DMA((2, tiles, max(size[axis] - 1, 1))))
    return made


class Gather:
    def __init__(self, place, rows, shards, whole, refs):
        self.place, self.rows, self.shards, self.whole = place, rows, shards, whole
        self.core_sem, self.own_sem = refs[:2]
        self.streams = []
        at = 2
        for first, part, stages in stream_plan(rows):
            self.streams.append((first, part, [st + (refs[at + i],) for i, st in enumerate(stages)]))
            at += len(stages)

    def region(self, t, stream, k):
        first, _, stages = self.streams[stream]
        at = first
        for axis, left, divides, _ in stages[:k]:
            at = at + (self.place.at[axis] * left if divides else 0)
        return self.whole.at[t, self.place.at["core"], pl.ds(pl.multiple_of(at, 16), stages[k - 1][1])]

    def shard(self, t, stream):
        return self.shards.at[t, stream, 0 : self.streams[stream][2][-1][1]]

    def own_copies(self, t):
        return [
            pltpu.make_async_copy(self.shard(t, i), self.region(t, i, 3), self.own_sem.at[t, i])
            for i in range(len(self.streams))
        ]

    def copies(self, k, t):
        if k == 0:
            half = self.whole.at[t, self.place.at["core"]]
            return [remote(half, half, self.core_sem.at[0, t], self.core_sem.at[1, t], self.place.peer("core", 1))]
        made = []
        for i, (_, _, stages) in enumerate(self.streams):
            axis, left, divides, sem = stages[k - 1]
            if not divides:
                continue
            dst = self.region(t, i, k)
            src = self.shard(t, i) if k == 3 else dst
            for d in range(1, self.place.size[axis]):
                made.append(remote(src, dst, sem.at[0, t, d - 1], sem.at[1, t, d - 1], self.place.peer(axis, d)))
        return made

    def turn(self, step, tiles):
        for k in (0, 1, 2, 3):
            t = step - WAYS[k]

            @pl.when((t >= 0) & (t < tiles))
            def _():
                for copy in self.copies(k, t):
                    copy.wait()
                if k == 3:
                    for copy in self.own_copies(t):
                        copy.wait()
                if k > 0:
                    for copy in self.copies(k - 1, t):
                        copy.start()

        @pl.when(step < tiles)
        def _():
            for copy in self.own_copies(step) + self.copies(3, step):
                copy.start()


class Chain:
    def __init__(self, place, reverse, lag, kept, own, around, total, before, leaving, entering, result, lo_sem, hi_sem):
        self.place, self.reverse, self.lag, self.kept = place, reverse, lag, kept
        self.own, self.around, self.total, self.before = own, around, total, before
        self.leaving, self.entering, self.result = leaving, entering, result
        self.lo_sem, self.hi_sem = lo_sem, hi_sem
        self.n_hi, self.n_lo = place.size["hi"], place.size["lo"]
        hi = place.at["hi"]
        self.rank = self.n_hi - 1 - hi if reverse else hi

    def lo_copies(self, r):
        return [
            remote(
                self.own.at[r], self.around.at[d - 1, r], self.lo_sem.at[0, r, d - 1], self.lo_sem.at[1, r, d - 1],
                self.place.peer("lo", d),
            )
            for d in range(1, self.n_lo)
        ]

    def hi_copy(self, r):
        return remote(
            self.leaving.at[r], self.entering.at[r], self.hi_sem.at[0, r], self.hi_sem.at[1, r],
            self.place.peer("hi", -1 if self.reverse else 1),
        )

    def keep(self, r, pos):
        flags = self.kept[pl.ds(r, 1), :]
        here = lax.broadcasted_iota(jnp.int32, flags.shape, 1) == self.place.at["hi"] * self.n_lo + pos
        return jnp.sum(jnp.where(here, flags, 0.0), axis=1, keepdims=True)

    def order(self):
        return list(range(self.n_lo))[:: -1 if self.reverse else 1]

    def begin(self, r):
        for copy in self.lo_copies(r):
            copy.start()

    def leave(self, r, value):
        @pl.when(self.rank < self.n_hi - 1)
        def _():
            self.leaving[r] = value.astype(BF)
            self.hi_copy(r).start()

    def join(self, r):
        for copy in self.lo_copies(r):
            copy.wait()
        lo = self.place.at["lo"]
        total = jnp.zeros(self.own.shape[1:], F32)
        before = total
        for pos in self.order():
            part = self.own[r].astype(F32)
            before = jnp.where(lo == pos, total, before)
            for d in range(1, self.n_lo):
                part = jnp.where((lo - pos) % self.n_lo == d, self.around[d - 1, r].astype(F32), part)
            total = part + self.keep(r, pos) * total
        self.total[r] = total
        self.before[r] = before

        @pl.when(self.rank == 0)
        def _():
            self.leave(r, total)
            self.result[r] = before.astype(BF)

    def hop(self, r):
        self.hi_copy(r).wait_recv()
        entering = self.entering[r].astype(F32)
        lo = self.place.at["lo"]
        keep_all = keep_before = jnp.ones((1, 1), F32)
        for pos in self.order():
            keep_before = jnp.where(lo == pos, keep_all, keep_before)
            keep_all = keep_all * self.keep(r, pos)
        self.leave(r, self.total[r] + keep_all * entering)
        self.result[r] = (self.before[r] + keep_before * entering).astype(BF)

    def turn(self, step, rows, starts=True):
        for q in range(self.n_hi - 1, 0, -1):
            r = step - self.lag * (1 + q)

            @pl.when((r >= 0) & (r < rows) & (self.rank == q))
            def _():
                self.hop(r)

        r = step - self.lag

        @pl.when((r >= 0) & (r < rows))
        def _():
            self.join(r)

        if starts:

            @pl.when(step < rows)
            def _():
                self.begin(step)

    def close(self, rows):
        @pl.when(self.rank < self.n_hi - 1)
        def _():
            for r in range(rows):
                self.hi_copy(r).wait_send()


def chain_scratch(rows, height, feats):
    size = axis_sizes()
    peers = max(size["lo"] - 1, 1)
    shape = (rows, height, feats)
    return [
        pltpu.VMEM(shape, BF),
        pltpu.VMEM((peers,) + shape, BF),
        pltpu.VMEM(shape, F32),
        pltpu.VMEM(shape, F32),
        pltpu.VMEM(shape, BF),
        pltpu.VMEM(shape, BF),
        pltpu.VMEM(shape, BF),
        pltpu.SemaphoreType.DMA((2, rows, peers)),
        pltpu.SemaphoreType.DMA((2, rows)),
    ]


class Direct:
    def __init__(self, place, whole, mine, other, base, got, core_sem, out_sem, back_sem):
        self.place, self.whole = place, whole
        self.mine, self.other, self.base, self.got = mine, other, base, got
        self.core_sem, self.out_sem, self.back_sem = core_sem, out_sem, back_sem
        self.offsets = place.others()
        self.rows = base.shape[0] // (len(self.offsets) + 1)
        self.own = self.region(place.other((0, 0, 0))[1])

    def region(self, number):
        return pl.ds(pl.multiple_of(number * self.rows, 16), self.rows)

    def copies(self, k):
        core = self.place.at["core"]
        made = []
        if k == 0:
            partner = self.place.peer("core", 1)
            made.append(
                remote(self.mine.at[0, 1 - core], self.other, self.core_sem.at[0, 0], self.core_sem.at[1, 0], partner)
            )
        elif k == 3:
            half = self.whole.at[0, core]
            made.append(
                remote(half, half, self.core_sem.at[0, 1], self.core_sem.at[1, 1], self.place.peer("core", 1))
            )
        else:
            for i, offset in enumerate(self.offsets):
                peer, number = self.place.other(offset)
                if k == 1:
                    src, dst, sem = self.base.at[self.region(number)], self.got.at[i], self.out_sem
                else:
                    src = dst = self.whole.at[0, core, self.own]
                    sem = self.back_sem
                made.append(remote(src, dst, sem.at[0, i], sem.at[1, i], peer))
        return made

    def start(self, k):
        for copy in self.copies(k):
            copy.start()

    def finish(self, k):
        for copy in self.copies(k):
            copy.wait()
        core = self.place.at["core"]
        if k == 0:
            self.base[...] = self.mine[0, core] + self.other[...]
        elif k == 1:
            total = self.base[self.own].astype(F32)
            for i in range(len(self.offsets)):
                total = total + self.got[i].astype(F32)
            self.whole[0, core, self.own] = total.astype(BF)


def direct_scratch(rows):
    size = axis_sizes()
    peers = size["lo"] * size["y"] * size["hi"] - 1
    return [
        pltpu.VMEM((1, 2, rows, 128), BF),
        pltpu.VMEM((rows, 128), BF),
        pltpu.VMEM((rows, 128), BF),
        pltpu.VMEM((peers, rows // (peers + 1), 128), BF),
        pltpu.SemaphoreType.DMA((2, 2)),
        pltpu.SemaphoreType.DMA((2, peers)),
        pltpu.SemaphoreType.DMA((2, peers)),
    ]


class Small:
    def __init__(self, rank, width, kv_width, heads, kv_heads, head):
        def chunks(lanes):
            return -(-lanes // 128)

        tall = -(-(3 * rank + 2) // 16) * 16
        flat = -(-2 * rank // 16) * 16
        sections = [
            ("down", tall, chunks(width)),
            ("out", flat, chunks(width)),
            ("q_up", -(-rank // 16) * 16, chunks(width)),
            ("kv_up", -(-2 * rank // 16) * 16, chunks(kv_width)),
            ("qmap", head, (heads + 1) // 2),
            ("kmap", head, (kv_heads + 1) // 2),
        ]
        need = sum(rows * n for _, rows, n in sections)
        size = axis_sizes()
        grain = 16 * size["lo"] * size["y"] * size["hi"]
        self.rows = -(-(need + 64) // (2 * grain)) * grain
        self.place = {}
        half, at = 0, 0
        for name, rows, n in sections:
            self.place[name] = []
            for _ in range(n):
                if at + rows > self.rows:
                    half, at = half + 1, 0
                self.place[name].append((half, at, rows))
                at += rows

    def put(self, ref, name, value):
        for c, (half, at, rows) in enumerate(self.place[name]):
            part = value[:, c * 128 : (c + 1) * 128]
            ref[0, half, at : at + part.shape[0], 0 : part.shape[1]] = part.astype(ref.dtype)

    def put_heads(self, ref, name, maps):
        for c, (half, at, rows) in enumerate(self.place[name]):
            pair = [maps[h] for h in range(2 * c, min(2 * c + 2, maps.shape[0]))]
            pair = jnp.concatenate(pair, axis=1) if len(pair) > 1 else pair[0]
            ref[0, half, at : at + rows, 0 : pair.shape[1]] = pair.astype(ref.dtype)

    def take(self, ref, name, lanes):
        parts = [ref[0, half, at : at + rows].astype(F32) for half, at, rows in self.place[name]]
        return jnp.concatenate(parts, axis=1)[:, :lanes]


def widen_kernel(width, high, rank, layout, whole, small, out_in, tok_in, out_out, tok_out, gate, up, down, *outs):
    out_out[...] = out_in[...]
    tok_out[...] = tok_in[...]
    for i, out in enumerate((gate, up, down)):
        for half in range(2):
            out[:, half * 128 : (half + 1) * 128] = whole[0, half, i * width : (i + 1) * width].astype(F32)

    @pl.when(pl.program_id(0) == 0)
    def _():
        pre, post, qd, kd, vd, qu, ku, vu, od, ou, qmap, kmap = outs
        downs = layout.take(small, "down", width)
        for i, out in enumerate((qd, kd, vd)):
            out[...] = downs[i * rank : (i + 1) * rank]
        pre[...] = downs[3 * rank : 3 * rank + 1]
        post[...] = downs[3 * rank + 1 : 3 * rank + 2]
        pair = layout.take(small, "out", width)
        od[...] = pair[:rank]
        ou[...] = pair[rank : 2 * rank]
        qu[...] = layout.take(small, "q_up", width)[:rank]
        pair = layout.take(small, "kv_up", ku.shape[1])
        ku[...] = pair[:rank]
        vu[...] = pair[rank : 2 * rank]
        head = qmap.shape[1]
        for name, out in (("qmap", qmap), ("kmap", kmap)):
            for h in range(out.shape[0]):
                half, at, rows = layout.place[name][h // 2]
                both = small[0, half, at : at + rows].astype(F32)
                out[h] = both[:, (h % 2) * head : (h % 2 + 1) * head]


def row_sum(value):
    return dot(jnp.ones((8, value.shape[1]), BF), value.astype(BF), NT)


def rms(value):
    return lax.rsqrt(jnp.mean(value * value, axis=0, keepdims=True) + EPSILON)


def soft_pair(logit):
    top = jnp.max(logit, axis=0, keepdims=True)
    low = jnp.min(logit, axis=0, keepdims=True)
    up = jnp.exp(logit - top)
    down = jnp.exp(low - logit)
    up = up / jnp.sum(up, axis=0, keepdims=True)
    down = down / jnp.sum(down, axis=0, keepdims=True)
    return jnp.concatenate([up, down], axis=0).astype(BF)


def soft_pair_back(phi, grad):
    half = phi.shape[0] // 2
    up, down = phi[:half].astype(F32), phi[half:].astype(F32)
    gu, gd = grad[:half], grad[half:]
    gu = up * (gu - jnp.sum(up * gu, axis=0, keepdims=True))
    gd = down * (gd - jnp.sum(down * gd, axis=0, keepdims=True))
    return (gu - gd).astype(BF)


def frame(place, span, doc, seg, kept):
    rows, length = doc.shape
    index = place.seq
    high = seg.shape[0]
    more = jnp.zeros((high - rows, span), F32)
    own = doc[:, pl.ds(pl.multiple_of(index * span, span), span)].astype(F32)
    prev = doc[:, pl.ds(pl.multiple_of(jnp.maximum(index - 1, 0) * span, span), span)].astype(F32)
    lane = lax.broadcasted_iota(jnp.int32, (rows, span), 1)
    prev = jnp.where((lane >= span - WINDOW) & (index > 0), prev, 0.0)
    upper = lax.broadcasted_iota(jnp.int32, (span, span), 0) <= lax.broadcasted_iota(jnp.int32, (span, span), 1)
    upper = jnp.where(upper, 1.0, 0.0).astype(BF)
    before = jnp.concatenate([prev, more], axis=0)
    tail = dot(before.astype(BF), upper)
    mine = dot(jnp.concatenate([own, more], axis=0).astype(BF), upper) + jnp.sum(before, axis=1, keepdims=True)
    seg[:, :span] = mine
    seg[:, span:] = tail[:, span - WINDOW :]
    total = jnp.zeros(kept.shape, F32)
    for b in range(length // span):
        at = lax.broadcasted_iota(jnp.int32, (span, 128), 0)
        block = lax.broadcasted_iota(jnp.int32, (span, 128), 1)
        here = jnp.where(at < span - WINDOW, b, b + 1) == block
        marks = jnp.concatenate([doc[:, b * span : (b + 1) * span].astype(F32), more], axis=0)
        total = total + dot(marks.astype(BF), jnp.where(here, 1.0, 0.0).astype(BF))
    kept[...] = jnp.where(total == 0, 1.0, 0.0)


def frame_row(seg, r, span):
    keys = seg[pl.ds(r, 1), :]
    query = keys[:, :span]
    column = jnp.broadcast_to(keys, (8, keys.shape[1])).T[:, :1]
    lane = lax.broadcasted_iota(jnp.int32, keys.shape, 1)
    last = jnp.sum(jnp.where(lane == span - WINDOW - 1, keys, 0.0), axis=1, keepdims=True)
    keep = (keys == last) & ((lane < span - WINDOW) | (lane >= span))
    return query, column, jnp.where(keep, 1.0, 0.0)


def assemble(width, bases, gains, wq, wkv, wo, down, columns):
    qb, kb, vb, ob, qu, ku, vu, ou, qd, kd, vd = bases
    rank = qu.shape[0]
    high = wq.shape[0]
    extra = high - width
    for out, base, up in ((wq, qb, qu), (wo, ob, ou)):
        out[0:width] = base[...]
        rows = jnp.concatenate([2.0 * up[...].astype(F32), jnp.zeros((extra - rank, width), F32)], axis=0)
        out[width:] = rows.astype(BF)
    kv = kb.shape[0]
    wkv[0:kv, 0:width] = kb[...]
    wkv[kv:, 0:width] = vb[...]
    none = jnp.zeros((rank, kv), F32)
    pair = jnp.concatenate(
        [
            jnp.concatenate([none, none], axis=1),
            jnp.concatenate([2.0 * ku[...].astype(F32), none], axis=1),
            jnp.concatenate([none, 2.0 * vu[...].astype(F32)], axis=1),
            jnp.zeros((extra - 3 * rank, 2 * kv), F32),
        ],
        axis=0,
    )
    wkv[:, width:] = pair.T.astype(BF)
    down[...] = jnp.concatenate([qd[...].astype(F32), kd[...].astype(F32), vd[...].astype(F32)], axis=0).astype(BF)
    wide = gains[...]
    wide = jnp.concatenate([wide, jnp.zeros((8 - wide.shape[0], width), F32)], axis=0).T
    columns[0] = wide[:, 0:1]
    columns[1] = wide[:, 1:2]


def qkv_kernel(tok, gain, wq, wkv, down, qkv, normed, inner, tails, ext):
    width = tok.shape[1]
    kv = wkv.shape[0]
    value = tok[0].astype(F32)
    norm = (value * rms(value) * gain[...]).astype(BF)
    normed[0] = norm
    low = dot(down[...], norm).astype(BF)
    inner[0] = low
    ext[0:width] = norm
    ext[width:] = jnp.zeros((ext.shape[0] - width, ext.shape[1]), BF)
    ext[width : width + low.shape[0]] = low
    qkv[0, 0:width] = dot(wq[...], ext[...], TN).astype(BF)
    both = dot(wkv[...], ext[...]).astype(BF)
    qkv[0, width:] = both
    span = tok.shape[2]
    tails[0] = jnp.concatenate(
        [both[: kv // 2, span - WINDOW :], both[kv // 2 :, span - WINDOW :]], axis=1
    )


def aug_value(value):
    extra = lax.broadcasted_iota(jnp.int32, (AUG - value.shape[0], value.shape[1]), 0) == 0
    return jnp.concatenate([value, jnp.where(extra, 1.0, 0.0).astype(BF)], axis=0)


def key_kernel(kv_heads, qkv, tails, kmap, keep, phi, con):
    head = kmap.shape[1]
    first = qkv.shape[1] - 2 * kv_heads * head
    keeping = keep.astype(BF)
    for k in range(kv_heads):
        at = first + k * head
        key = jnp.concatenate([qkv[0, at : at + head], tails[0, k * head : (k + 1) * head, :WINDOW]], axis=1)
        at += kv_heads * head
        val = jnp.concatenate([qkv[0, at : at + head], tails[0, k * head : (k + 1) * head, WINDOW:]], axis=1)
        feat = soft_pair(dot(kmap[k], key, TN))
        phi[0, k] = feat
        con[0, k * AUG : (k + 1) * AUG] = dot(aug_value(val), feat * keeping, NT).astype(BF)


def masks(segq, segk, span):
    extent = segk.shape[0]
    row = lax.broadcasted_iota(jnp.int32, (extent, span), 0)
    pos = jnp.where(row < span, row, row - extent)
    query = lax.broadcasted_iota(jnp.int32, (extent, span), 1)
    same = segk == segq
    far = pos + WINDOW <= query
    return same & far, same & (pos <= query) & jnp.logical_not(far)


def local_kernel(
    kv_heads, group, qkv, tails, phik, frames, qmap, phiq, numer, den, lin_bias, win_bias, between,
):
    head = qmap.shape[1]
    span = qkv.shape[2]
    width = kv_heads * group * head
    segq, segk, _ = frames
    far, near = masks(segq, segk, span)
    lin_bias[...] = jnp.where(far, 1.0, 0.0)
    win_bias[...] = jnp.where(near, 0.0, -1e30)
    for k in range(kv_heads):
        at = width + k * head
        key = jnp.concatenate([qkv[0, at : at + head], tails[0, k * head : (k + 1) * head, :WINDOW]], axis=1)
        at += kv_heads * head
        val = jnp.concatenate([qkv[0, at : at + head], tails[0, k * head : (k + 1) * head, WINDOW:]], axis=1)
        queries, feats = [], []
        for h in range(k * group, (k + 1) * group):
            q = qkv[0, h * head : (h + 1) * head]
            f = soft_pair(dot(qmap[h], q, TN))
            phiq[0, h] = f
            queries.append(q)
            feats.append(f)
        query = jnp.concatenate(queries, axis=1) * (head**-0.5)
        feat = jnp.concatenate(feats, axis=1)
        lin = dot(phik[0, k], feat, TN)
        score = dot(key, query, TN)
        lb = jnp.concatenate([lin_bias[...]] * group, axis=1)
        wb = jnp.concatenate([win_bias[...]] * group, axis=1)
        weights = lin * lb + jnp.exp(score + wb)
        total = jnp.sum(weights, axis=0, keepdims=True)
        out = dot(val, weights.astype(BF))
        for g in range(group):
            h = k * group + g
            numer[0, h * head : (h + 1) * head] = out[:, g * span : (g + 1) * span]
            den[0, h : h + 1] = total[:, g * span : (g + 1) * span]
        between(k)


def join_kernel(
    kv_heads, group, phiq, numer, den_local, state, frames, tok, wo, down, gain,
    mixed, den, middle, normed, inner, ext,
):
    width = tok.shape[1]
    span = tok.shape[2]
    head = width // (kv_heads * group)
    shown = jnp.where(frames[0] == 0, 1.0, 0.0)
    den[0] = jnp.zeros_like(den[0])
    for h in range(kv_heads * group):
        k = h // group
        carried = dot(state[0, k * AUG : (k + 1) * AUG], phiq[0, h]) * shown
        total = den_local[0, h : h + 1] + carried[head : head + 1]
        at = pl.ds(h * head, head)
        ext[at] = ((numer[0, at] + carried[:head]) * (1.0 / total)).astype(BF)
        den[0, h : h + 1] = total
    got = ext[0:width]
    mixed[0] = got
    low = dot(down[...], got).astype(BF)
    inner[0] = low
    ext[width:] = jnp.zeros((ext.shape[0] - width, span), BF)
    ext[width : width + low.shape[0]] = low
    mid = tok[0].astype(F32) + dot(wo[...], ext[...], TN)
    middle[0] = mid
    normed[0] = (mid * rms(mid) * gain[...]).astype(BF)


def forward_kernel(
    rows, kv_heads, group,
    tok, tok_again, doc, gains, qb, kb, vb, ob, qu, ku, vu, ou, qd, kd, vd, od, qmap, kmap,
    qkv_out, normed, inner, tails_out, phik_out, phiq_out, state_out, mixed, den, middle, normed2, inner_o,
    wq, wkv, wo, down, columns,
    seg, kept, ext, qkv, sent, tails, phik, phiq, numer, den_local, lin_bias, win_bias, tail_sem, *refs,
):
    step = pl.program_id(0)
    place = Place()
    chain = Chain(place, False, 2, kept, *refs)
    width, span = tok.shape[1], tok.shape[2]

    def row(ref, r):
        return ref.at[pl.ds(r, 1)]

    def tail_copy(r):
        return remote(sent.at[r], tails.at[r], tail_sem.at[0, r], tail_sem.at[1, r], place.along(1))

    @pl.when(step == 0)
    def _():
        place.greet()

        @pl.when(jnp.logical_not(place.inside(-1)))
        def _():
            tails[...] = jnp.zeros_like(tails)

        frame(place, span, doc, seg, kept)
        assemble(width, (qb, kb, vb, ob, qu, ku, vu, ou, qd, kd, vd), gains, wq, wkv, wo, down, columns)

    @pl.when(step < rows)
    def _():
        qkv_kernel(tok, columns.at[0], wq, wkv, down, row(qkv, step), normed, inner, row(sent, step), ext)
        qkv_out[...] = qkv[pl.ds(step, 1)]

        @pl.when(place.inside(1))
        def _():
            tail_copy(step).start()

    @pl.when((step >= rows) & (step < 2 * rows))
    def _():
        r = step - rows

        @pl.when(place.inside(-1))
        def _():
            tail_copy(r).wait_recv()

        tails_out[...] = tails[pl.ds(r, 1)]
        keep = frame_row(seg, r, span)[2]
        key_kernel(kv_heads, row(qkv, r), row(tails, r), kmap, keep, row(phik, r), row(chain.own, r))
        phik_out[...] = phik[pl.ds(r, 1)]
        chain.turn(r, rows)

    @pl.when((step >= 2 * rows) & (step < 3 * rows))
    def _():
        r = step - 2 * rows

        def between(k):
            if k == kv_heads // 2 - 1:
                chain.turn(rows + 2 * r, rows, False)

        local_kernel(
            kv_heads, group, row(qkv, r), row(tails, r), row(phik, r), frame_row(seg, r, span), qmap,
            row(phiq, r), row(numer, r), row(den_local, r), lin_bias, win_bias, between,
        )
        phiq_out[...] = phiq[pl.ds(r, 1)]
        chain.turn(rows + 2 * r + 1, rows, False)

    @pl.when(step >= 3 * rows)
    def _():
        r = step - 3 * rows
        state_out[...] = chain.result[pl.ds(r, 1)]
        join_kernel(
            kv_heads, group, row(phiq, r), row(numer, r), row(den_local, r), row(chain.result, r),
            frame_row(seg, r, span), tok_again, wo, od, columns.at[1],
            mixed, den, middle, normed2, inner_o, ext,
        )

    @pl.when(step == 4 * rows - 1)
    def _():
        chain.close(rows)

        @pl.when(place.inside(1))
        def _():
            for r in range(rows):
                tail_copy(r).wait_send()


def ff_kernel(
    width, normed_h, cot_h, middle, gain, gate_h, up_h, down_h,
    hid_out, grad_mid, grad_gain, shards,
    normed, cot, gate_v, up_v, down_v, hid, dgate, dup, sem, act_sem, hid_sem, *refs,
):
    step = pl.program_id(0)
    rows = normed_h.shape[0]
    span = normed_h.shape[2]
    high = normed.shape[0]
    hidden = gate_h.shape[1]
    tiles = hidden // TILE
    place = Place()
    scatter = Scatter(place, 3 * width, refs)

    def act_copies():
        made = []
        for r in range(rows):
            at = pl.ds(r * span, span)
            made.append(pltpu.make_async_copy(normed_h.at[r], normed.at[0:width, at], act_sem.at[r, 0]))
            made.append(pltpu.make_async_copy(cot_h.at[r], cot.at[0:width, at], act_sem.at[r, 1]))
        return made

    def tile_copies(j):
        at = pl.ds(pl.multiple_of(j * TILE, TILE), TILE)
        return [
            pltpu.make_async_copy(gate_h.at[:, at], gate_v.at[0:width, at], sem.at[j, 0]),
            pltpu.make_async_copy(up_h.at[:, at], up_v.at[0:width, at], sem.at[j, 1]),
            pltpu.make_async_copy(down_h.at[:, at], down_v.at[0:width, at], sem.at[j, 2]),
        ]

    @pl.when(step == 0)
    def _():
        place.greet()
        for copy in act_copies():
            copy.start()
        for j in range(tiles):
            for copy in tile_copies(j):
                copy.start()
        for ref in (gate_v, up_v, down_v):
            ref[width:] = jnp.zeros((high - width, hidden), BF)
        for ref in (normed, cot):
            ref[width:] = jnp.zeros((high - width, rows * span), BF)
        for copy in act_copies():
            copy.wait()

    @pl.when(step < tiles)
    def _():
        for copy in tile_copies(step):
            copy.wait()
        at = pl.ds(pl.multiple_of(step * TILE, TILE), TILE)
        gate, up, down = gate_v[:, at], up_v[:, at], down_v[:, at]
        for r in range(rows):
            lane = pl.ds(r * span, span)
            n2 = normed[:, lane]
            g = dot(gate, n2, TN)
            u = dot(up, n2, TN)
            dh = dot(down, cot[:, lane], TN).astype(BF).astype(F32)
            sig = 1.0 / (1.0 + jnp.exp(-g))
            act = g * sig
            hid[at, lane] = (act * u).astype(BF)
            dup[at, lane] = (dh * act).astype(BF)
            dgate[at, lane] = (dh * u * (sig + act * (1.0 - sig))).astype(BF)
        slot = step % 2
        for i, (left, right) in enumerate(((normed, dgate), (normed, dup), (cot, hid))):
            grad = dot(left[...], right[at, :], NT)[:width].astype(BF)
            for half in range(2):
                scatter.mine[slot, half, i * width : (i + 1) * width] = grad[:, half * 128 : (half + 1) * 128]

    @pl.when(step >= tiles)
    def _():
        r = step - tiles
        lane = pl.ds(pl.multiple_of(r * span, span), span)
        back = dot(gate_v[0:width], dgate[:, lane]) + dot(up_v[0:width], dup[:, lane])
        mid = middle[0]
        scale = rms(mid)
        unit = back * mid
        column = gain[0]
        pull = jnp.mean(unit * column, axis=0, keepdims=True) * (scale * scale * scale)
        grad_mid[0] = cot[0:width, lane].astype(F32) + (back * column) * scale - mid * pull

        @pl.when(r == 0)
        def _():
            grad_gain[...] = jnp.zeros_like(grad_gain)

        grad_gain[...] += row_sum(unit * scale)

        @pl.when(r == 0)
        def _():
            pltpu.make_async_copy(hid, hid_out, hid_sem).start()

        @pl.when(r == rows - 1)
        def _():
            pltpu.make_async_copy(hid, hid_out, hid_sem).wait()

    def into(tile, stream, total):
        shards[tile, stream, 0 : total.shape[0]] = total.astype(BF)

    scatter.turn(step, tiles, into)


def pull_kernel(
    kv_heads, group, grad_mid, mixed, den, phiq, frames, inner, wo, down,
    dnum, dden, dstate, gup, gdown,
):
    width = mixed.shape[1]
    span = mixed.shape[2]
    head = width // (kv_heads * group)
    low = inner.shape[1]

    branch = grad_mid[0].astype(BF)
    wide = dot(wo[...], branch)
    grad_inner = wide[width : width + low].astype(BF)
    grad = (wide[:width] + dot(down[...], grad_inner, TN)).astype(BF).astype(F32)
    gup[...] += 2.0 * dot(inner[0], branch, NT)
    gdown[...] += dot(grad_inner, mixed[0], NT)
    shown = jnp.where(frames[0] == 0, 1.0, 0.0)
    dden[0] = jnp.zeros_like(dden[0])
    pad = jnp.zeros((AUG - head - 1, span), F32)
    for k in range(kv_heads):
        total = None
        for g in range(group):
            h = k * group + g
            at = pl.ds(h * head, head)
            dm = grad[h * head : (h + 1) * head]
            inv = 1.0 / den[0, h : h + 1]
            dd = -jnp.sum(dm * mixed[0, at].astype(F32), axis=0, keepdims=True) * inv
            dn = (dm * inv).astype(BF)
            dnum[0, at] = dn
            dden[0, h : h + 1] = dd
            aug = (jnp.concatenate([dn.astype(F32), dd, pad], axis=0) * shown).astype(BF)
            part = dot(aug, phiq[0, h], NT)
            total = part if total is None else total + part
        dstate[0, k * AUG : (k + 1) * AUG] = total.astype(BF)


def back_kernel(
    kv_heads, group, qkv, tails, phik, phiq, state, dcon, dnum, dden, frames, qmap, kmap,
    dq_out, dkv_out, dtails, gqmap, gkmap, lin_bias, win_bias, between,
):
    head = qmap.shape[1]
    width = dq_out.shape[1]
    span = dq_out.shape[2]
    scale = head**-0.5

    far, near = masks(frames[0], frames[1], span)
    lin_bias[...] = jnp.where(far, 1.0, 0.0)
    win_bias[...] = jnp.where(near, 0.0, -1e30)
    shown = jnp.where(frames[0] == 0, 1.0, 0.0)
    shown3 = jnp.concatenate([shown] * group, axis=1)
    keeping = frames[2]
    pad = jnp.zeros((AUG - head - 1, group * span), F32)
    for k in range(kv_heads):
        at = width + k * head
        key = jnp.concatenate([qkv[0, at : at + head], tails[0, k * head : (k + 1) * head, :WINDOW]], axis=1)
        at += kv_heads * head
        val = jnp.concatenate([qkv[0, at : at + head], tails[0, k * head : (k + 1) * head, WINDOW:]], axis=1)
        hs = range(k * group, (k + 1) * group)
        queries = [qkv[0, h * head : (h + 1) * head] for h in hs]
        query = jnp.concatenate(queries, axis=1) * scale
        feat = jnp.concatenate([phiq[0, h] for h in hs], axis=1)
        dn = jnp.concatenate([dnum[0, h * head : (h + 1) * head] for h in hs], axis=1)
        dd = jnp.concatenate([dden[0, h : h + 1] for h in hs], axis=1)
        kfeat = phik[0, k]
        lb = jnp.concatenate([lin_bias[...]] * group, axis=1)
        wb = jnp.concatenate([win_bias[...]] * group, axis=1)
        growth = jnp.exp(dot(key, query, TN) + wb)
        weights = (dot(kfeat, feat, TN) * lb + growth).astype(BF)
        dw = dot(val, dn, TN) + dd
        dlin = (dw * lb).astype(BF)
        dscore = (dw * growth).astype(BF)
        dv = dot(dn, weights, NT)
        aug = (jnp.concatenate([dn.astype(F32), dd, pad], axis=0) * shown3).astype(BF)
        held = state[0, k * AUG : (k + 1) * AUG]
        dfeat = dot(kfeat, dlin) + dot(held, aug, TN)
        con = dcon[0, k * AUG : (k + 1) * AUG]
        dkfeat = dot(feat, dlin, NT) + dot(con, aug_value(val), TN) * keeping
        dv = dv + dot(con[:head], kfeat * keeping.astype(BF))
        dq = dot(key, dscore) * scale
        dk = dot(query, dscore, NT)
        dt = soft_pair_back(feat, dfeat.astype(BF).astype(F32))
        for g in range(group):
            h = k * group + g
            part = dt[:, g * span : (g + 1) * span]
            gqmap[h] += dot(queries[g], part, NT)
            full = dq[:, g * span : (g + 1) * span] + dot(qmap[h], part)
            dq_out[0, h * head : (h + 1) * head] = full.astype(BF)
        dtk = soft_pair_back(kfeat, dkfeat.astype(BF).astype(F32))
        gkmap[k] += dot(key, dtk, NT)
        dk = dk + dot(kmap[k], dtk)
        ks, vs = k * head, (kv_heads + k) * head
        dkv_out[0, ks : ks + head] = dk[:, :span]
        dkv_out[0, vs : vs + head] = dv[:, :span]
        dtails[0, ks : ks + head] = jnp.concatenate([dk[:, span:], dv[:, span:]], axis=1).astype(BF)
        between(k)


def final_kernel(
    tok, grad_mid, gain, dq, dkv, returned, normed, inner, wq, wkv, down,
    grad_tok, ggain, gdown, gup,
):
    width = tok.shape[1]
    span = tok.shape[2]
    low = down.shape[0]

    got = returned[0].astype(F32)
    got = jnp.concatenate([got[:, :WINDOW], got[:, WINDOW:]], axis=0)
    own = dkv[0]
    both = jnp.concatenate([own[:, : span - WINDOW], own[:, span - WINDOW :] + got], axis=1).astype(BF)
    grad_q = dq[0]
    wide = dot(wq[...], grad_q) + dot(wkv[...], both, TN)
    grad_inner = wide[width : width + low].astype(BF)
    back = wide[:width] + dot(down[...], grad_inner, TN)
    gdown[...] += dot(grad_inner, normed[0], NT)
    gup[:, :width] += 2.0 * dot(inner[0], grad_q, NT)
    gup[:, width:] += 2.0 * dot(inner[0], both, NT)
    value = tok[0].astype(F32)
    scale = rms(value)
    unit = value * scale
    grad_unit = back * gain[...]
    ggain[...] += row_sum(back * unit)
    grad_tok[0] = grad_mid[0] + scale * (
        grad_unit - unit * jnp.mean(grad_unit * unit, axis=0, keepdims=True)
    )


def backward_kernel(
    rows, kv_heads, group, tiles, shard_rows, layout,
    doc, grad_mid_p, mixed, den, phiq_p, inner_o, wo, odown,
    qkv, tails, phik, phiq, state, qmap, kmap,
    tok, grad_mid, normed, inner, gain, wq, wkv, down, gpost, shards, hid_h, down_h, middle_h,
    grad_tok, whole, small_out, layer_out,
    dnum, dden, dq, dkv, dtails, returned, gup_o, gdown_o, gqmap, gkmap, ggain, gdown, gup, lin_bias, win_bias,
    seg, kept, tail_sem, small, hid, down_v, middle, out, in_sem, out_sem, *refs,
):
    step = pl.program_id(0)
    early = rows
    place = Place()
    chain = Chain(place, True, 1, kept, *refs[:9])
    refs = refs[9:]
    n_gather = len(gather_scratch(shard_rows, tiles))
    gather = Gather(place, shard_rows, shards, whole, refs[:n_gather])
    direct = Direct(place, small, *refs[n_gather:])

    def row(ref, r):
        return ref.at[pl.ds(r, 1)]

    def tail_copy(r):
        return remote(dtails.at[r], returned.at[r], tail_sem.at[0, r], tail_sem.at[1, r], place.along(-1))

    def fetches():
        pairs = ((hid_h, hid), (down_h, down_v), (middle_h, middle))
        return [pltpu.make_async_copy(src, dst, in_sem.at[i]) for i, (src, dst) in enumerate(pairs)]

    def out_copy(r):
        return pltpu.make_async_copy(out.at[r], layer_out.at[r], out_sem.at[r])

    def make_out(r):
        lane = slice(r * tok.shape[2], (r + 1) * tok.shape[2])
        out[r] = (middle[r] + dot(down_v[...], hid[:, lane])).astype(BF)
        out_copy(r).start()

    @pl.when(step == 0)
    def _():
        for copy in fetches():
            copy.start()
        place.greet(True)
        frame(place, tok.shape[2], doc, seg, kept)
        for ref in (gup_o, gdown_o, gqmap, gkmap, ggain, gdown, gup):
            ref[...] = jnp.zeros_like(ref)

        @pl.when(jnp.logical_not(place.inside(1)))
        def _():
            returned[...] = jnp.zeros_like(returned)

    @pl.when(step < rows)
    def _():
        pull_kernel(
            kv_heads, group, grad_mid_p, mixed, den, phiq_p, frame_row(seg, step, tok.shape[2]), inner_o, wo, odown,
            row(dnum, step), row(dden, step), row(chain.own, step), gup_o, gdown_o,
        )

    @pl.when((step >= rows) & (step < 2 * rows))
    def _():
        r = step - rows

        def between(k):
            if k == kv_heads // 2:

                @pl.when(r % 2 == 1)
                def _():
                    gather.turn(early + r + r // 2, tiles)

        back_kernel(
            kv_heads, group, qkv, tails, phik, phiq, state, row(chain.result, r), row(dnum, r), row(dden, r),
            frame_row(seg, r, tok.shape[2]), qmap, kmap,
            row(dq, r), row(dkv, r), row(dtails, r), gqmap, gkmap, lin_bias, win_bias, between,
        )

        @pl.when(place.inside(-1))
        def _():
            tail_copy(r).start()

    @pl.when(step >= 2 * rows)
    def _():
        r = step - 2 * rows

        @pl.when(place.inside(1))
        def _():
            tail_copy(r).wait_recv()

        final_kernel(
            tok, grad_mid, gain.at[0], row(dq, r), row(dkv, r), row(returned, r), normed, inner, wq, wkv, down,
            grad_tok, ggain, gdown, gup,
        )

    chain.turn(step, rows)

    r = step - rows
    late = early + rows + rows // 2
    turn = jnp.where(step < rows, step - (rows - early), jnp.where(r < rows, early + r + (r + 1) // 2, late + (r - rows) // 2))

    @pl.when((step >= rows - early) & ((r < rows) | ((r - rows) % 2 == 0)))
    def _():
        gather.turn(turn, tiles)

    @pl.when(step == 3 * rows - 1)
    def _():
        chain.close(rows)

        @pl.when(place.inside(-1))
        def _():
            for r in range(rows):
                tail_copy(r).wait_send()

        rank = gdown_o.shape[0]
        width = gdown_o.shape[1]
        kv_width = kv_heads * qmap.shape[1]
        mine = direct.mine
        mine[...] = jnp.zeros_like(mine)
        pad = [jnp.zeros((6, width), F32)]
        layout.put(mine, "down", jnp.concatenate([gdown[...], ggain[0:1], gpost[0:1]] + pad, axis=0))
        layout.put(mine, "out", jnp.concatenate([gdown_o[...], gup_o[...]], axis=0))
        layout.put(mine, "q_up", jnp.concatenate([gup[0:rank, :width], jnp.zeros((rank, width), F32)], axis=0))
        layout.put(
            mine, "kv_up",
            jnp.concatenate(
                [gup[rank : 2 * rank, width : width + kv_width], gup[2 * rank :, width + kv_width :]], axis=0
            ),
        )
        layout.put_heads(mine, "qmap", gqmap)
        layout.put_heads(mine, "kmap", gkmap)

        turns = list(range(late + rows // 2 + 1, tiles + WAYS[0]))
        for copy in fetches():
            copy.wait()
        shares = [list(range(rows))[n::4] for n in range(4)]
        for k in range(4):
            direct.start(k)
            for r in shares[k]:
                make_out(r)
            for turn in turns[k : k + 1] if k < 3 else turns[3:]:
                gather.turn(jnp.int32(turn), tiles)
            direct.finish(k)
        small_out[...] = small[...]
        for r in range(rows):
            out_copy(r).wait()


def row_spec(*shape):
    zeros = (0,) * len(shape)
    return pl.BlockSpec((1,) + shape, lambda r: (r,) + zeros)


def whole_spec(*shape):
    zeros = (0,) * len(shape)
    return pl.BlockSpec(shape, lambda r: zeros, pipeline_mode=pl.Buffered(1))


def shape_of(shape, kind):
    return jax.ShapeDtypeStruct(shape, kind)


def body(
    tokens, doc_starts, pregain, query_base, key_base, value_base, output_base, query_down, query_up,
    key_down, key_up, value_down, value_up, out_down, out_up, query_map, key_map, postgain, gate_proj,
    up_proj, down_proj, cotangent,
):
    rows, span, width = tokens.shape
    heads, head, _ = query_map.shape
    kv_heads = key_map.shape[0]
    group = heads // kv_heads
    kv_width = kv_heads * head
    rank = query_up.shape[0]
    extent = span + WINDOW
    hidden = gate_proj.shape[1]
    tiles = hidden // TILE
    high = -(-width // 256) * 256
    feats = 2 * head
    slots = -(-heads // 8) * 8

    tok = jnp.swapaxes(tokens, 1, 2)
    cot = jnp.swapaxes(cotangent, 1, 2)
    gains = jnp.stack([pregain, postgain]).astype(F32)
    odown = out_down.T

    def phase_spec(shape, phase):
        tail = (0,) * (len(shape) - 1)
        return pl.BlockSpec((1,) + tuple(shape[1:]), lambda s: (jnp.clip(s - phase * rows, 0, rows - 1),) + tail)

    args = [
        (tok, 0), (tok, 3), (doc_starts, None), (gains, None), (query_base, None), (key_base.T, None),
        (value_base.T, None), (output_base, None), (query_up, None), (key_up, None), (value_up, None),
        (out_up, None), (query_down.T, None), (key_down.T, None), (value_down.T, None), (odown, None),
        (query_map, None), (key_map, None),
    ]
    made = [
        ((rows, width + 2 * kv_width, span), BF, 0),
        ((rows, width, span), BF, 0),
        ((rows, 3 * rank, span), BF, 0),
        ((rows, kv_width, 2 * WINDOW), BF, 1),
        ((rows, kv_heads, feats, extent), BF, 1),
        ((rows, heads, feats, span), BF, 2),
        ((rows, kv_heads * AUG, feats), BF, 3),
        ((rows, width, span), BF, 3),
        ((rows, slots, span), F32, 3),
        ((rows, width, span), F32, 3),
        ((rows, width, span), BF, 3),
        ((rows, rank, span), BF, 3),
        ((high, width), BF, None),
        ((2 * kv_width, high), BF, None),
        ((high, width), BF, None),
        ((3 * rank, width), BF, None),
        ((2, width, 1), F32, None),
    ]
    biases = [pltpu.VMEM((extent, span), F32)] * 2
    frame_scratch = [pltpu.VMEM((8, extent), F32), pltpu.VMEM((8, 128), F32)]
    (
        qkv, normed, inner, tails, phik, phiq, state, mixed, den, middle, normed2, inner_o, wq, wkv, wo, down, columns,
    ) = pl.pallas_call(
        functools.partial(forward_kernel, rows, kv_heads, group),
        grid=(4 * rows,),
        in_specs=[whole_spec(*a.shape) if phase is None else phase_spec(a.shape, phase) for a, phase in args],
        out_specs=tuple(
            pl.BlockSpec(shape, functools.partial(lambda n, s: (0,) * n, len(shape)))
            if phase is None
            else phase_spec(shape, phase)
            for shape, _, phase in made
        ),
        out_shape=tuple(shape_of(shape, kind) for shape, kind, _ in made),
        scratch_shapes=frame_scratch
        + [
            pltpu.VMEM((high, span), BF),
            pltpu.VMEM((rows, width + 2 * kv_width, span), BF),
            pltpu.VMEM((rows, kv_width, 2 * WINDOW), BF),
            pltpu.VMEM((rows, kv_width, 2 * WINDOW), BF),
            pltpu.VMEM((rows, kv_heads, feats, extent), BF),
            pltpu.VMEM((rows, heads, feats, span), BF),
            pltpu.VMEM((rows, width, span), F32),
            pltpu.VMEM((rows, slots, span), F32),
        ]
        + biases
        + [pltpu.SemaphoreType.DMA((2, rows))]
        + chain_scratch(rows, kv_heads * AUG, feats),
        compiler_params=pltpu.CompilerParams(vmem_limit_bytes=VMEM, collective_id=2, has_side_effects=True),
    )(*[a for a, _ in args])

    last = lambda s: (jnp.maximum(s - tiles, 0), 0, 0)
    fixed = lambda s: (0, 0)
    anywhere = pl.BlockSpec(memory_space=pl.ANY)
    shard_shape = (tiles, len(stream_plan(3 * width)), shard_rows(3 * width), 128)
    hid, grad_mid, gpost, shards = pl.pallas_call(
        functools.partial(ff_kernel, width),
        grid=(tiles + rows,),
        in_specs=[anywhere, anywhere, pl.BlockSpec((1, width, span), last), pl.BlockSpec((1, width, 1), lambda s: (1, 0, 0))]
        + [anywhere] * 3,
        out_specs=(
            anywhere,
            pl.BlockSpec((1, width, span), last),
            pl.BlockSpec((8, width), fixed),
            pl.BlockSpec(shard_shape, lambda s: (0, 0, 0, 0)),
        ),
        out_shape=(
            shape_of((hidden, rows * span), BF),
            shape_of((rows, width, span), F32),
            shape_of((8, width), F32),
            shape_of(shard_shape, BF),
        ),
        scratch_shapes=[pltpu.VMEM((high, rows * span), BF)] * 2
        + [pltpu.VMEM((high, hidden), BF)] * 3
        + [pltpu.VMEM((hidden, rows * span), BF)] * 3
        + [pltpu.SemaphoreType.DMA((tiles, 3)), pltpu.SemaphoreType.DMA((rows, 2)), pltpu.SemaphoreType.DMA(())]
        + scatter_scratch(3 * width, BF),
        compiler_params=pltpu.CompilerParams(vmem_limit_bytes=VMEM, collective_id=0, has_side_effects=True),
    )(normed2, cot, middle, columns, gate_proj, up_proj, down_proj.T)

    layout = Small(rank, width, kv_width, heads, kv_heads, head)
    args = [(doc_starts, None)]
    args += [(a, 0) for a in (grad_mid, mixed, den, phiq, inner_o)] + [(wo, None), (odown, None)]
    args += [(a, 1) for a in (qkv, tails, phik, phiq, state)] + [(query_map, None), (key_map, None)]
    args += [(a, 2) for a in (tok, grad_mid, normed, inner)] + [(a, None) for a in (columns, wq, wkv, down, gpost)]
    specs = [whole_spec(*a.shape) if phase is None else phase_spec(a.shape, phase) for a, phase in args]
    args = [a for a, _ in args]
    args += [shards, hid, down_proj.T, middle]
    specs += [anywhere] * 4
    last = lambda s: (jnp.maximum(s - 2 * rows, 0), 0, 0)
    grad_tok, whole, small, layer_out = pl.pallas_call(
        functools.partial(backward_kernel, rows, kv_heads, group, tiles, 3 * width, layout),
        grid=(3 * rows,),
        in_specs=specs,
        out_specs=(
            pl.BlockSpec((1, width, span), last),
            anywhere,
            pl.BlockSpec((1, 2, layout.rows, 128), lambda s: (0, 0, 0, 0)),
            anywhere,
        ),
        out_shape=(
            shape_of((rows, width, span), F32),
            shape_of((tiles, 2, 3 * width, 128), BF),
            shape_of((1, 2, layout.rows, 128), BF),
            shape_of((rows, width, span), BF),
        ),
        scratch_shapes=[
            pltpu.VMEM((rows, width, span), BF),
            pltpu.VMEM((rows, slots, span), F32),
            pltpu.VMEM((rows, width, span), BF),
            pltpu.VMEM((rows, 2 * kv_width, span), F32),
            pltpu.VMEM((rows, kv_width, 2 * WINDOW), BF),
            pltpu.VMEM((rows, kv_width, 2 * WINDOW), BF),
            pltpu.VMEM((rank, width), F32),
            pltpu.VMEM((rank, width), F32),
            pltpu.VMEM((heads, head, head), F32),
            pltpu.VMEM((kv_heads, head, head), F32),
            pltpu.VMEM((8, width), F32),
            pltpu.VMEM((3 * rank, width), F32),
            pltpu.VMEM((3 * rank, width + 2 * kv_width), F32),
        ]
        + biases
        + frame_scratch
        + [
            pltpu.SemaphoreType.DMA((2, rows)),
            pltpu.VMEM((1, 2, layout.rows, 128), BF),
            pltpu.VMEM((hidden, rows * span), BF),
            pltpu.VMEM((width, hidden), BF),
            pltpu.VMEM((rows, width, span), F32),
            pltpu.VMEM((rows, width, span), BF),
            pltpu.SemaphoreType.DMA((3,)),
            pltpu.SemaphoreType.DMA((rows,)),
        ]
        + chain_scratch(rows, kv_heads * AUG, feats)
        + gather_scratch(3 * width, tiles)
        + direct_scratch(layout.rows),
        compiler_params=pltpu.CompilerParams(vmem_limit_bytes=VMEM, collective_id=1, has_side_effects=True),
    )(*args)

    column = pl.BlockSpec((width, TILE), lambda j: (0, j))
    flat = [(1, width)] * 2 + [(rank, width)] * 4 + [(rank, kv_width)] * 2 + [(rank, width)] * 2
    flat += [query_map.shape, key_map.shape]
    pieces = next(n for n in range(tiles // rows, 0, -1) if width % (16 * n) == 0 and tiles >= n * rows)
    part = pl.BlockSpec(
        (1, width // pieces, span),
        lambda j: (jnp.minimum(j // pieces, rows - 1), jnp.where(j < rows * pieces, j % pieces, pieces - 1), 0),
    )
    outs = pl.pallas_call(
        functools.partial(widen_kernel, width, high, rank, layout),
        grid=(tiles,),
        in_specs=[
            pl.BlockSpec((1, 2, 3 * width, 128), lambda j: (j, 0, 0, 0)),
            pl.BlockSpec((1, 2, layout.rows, 128), lambda j: (0, 0, 0, 0)),
            part,
            part,
        ],
        out_specs=(part, part)
        + (column,) * 3
        + tuple(pl.BlockSpec(f, functools.partial(lambda n, j: (0,) * n, len(f))) for f in flat),
        out_shape=(shape_of(layer_out.shape, BF), shape_of(grad_tok.shape, F32))
        + (shape_of((width, hidden), F32),) * 3
        + tuple(shape_of(f, F32) for f in flat),
        compiler_params=pltpu.CompilerParams(vmem_limit_bytes=VMEM),
    )(whole, small, layer_out, grad_tok)
    layer_out, grad_tok, gate, up, down_t, pre, post, qd, kd, vd, qu, ku, vu, od, ou, gq, gk = outs
    return (
        jnp.swapaxes(layer_out, 1, 2),
        jnp.swapaxes(grad_tok, 1, 2),
        pre[0],
        qd.T,
        qu,
        kd.T,
        ku,
        vd.T,
        vu,
        od.T,
        ou,
        gq,
        gk,
        post[0],
        gate,
        up,
        down_t.T,
    )


def solution(mesh):
    wide = P("batch", "seq", None)
    return jax.shard_map(
        body,
        mesh=mesh,
        in_specs=(wide, P("batch", None)) + (P(),) * 19 + (wide,),
        out_specs=(wide, wide) + (P(),) * 15,
        check_vma=False,
    )
```
